32 devices in a mesh: tp: 2 (over y), dp: 16 (over z, x, core).
Axes of the slice: x: 2, y: 2, z: 4, core: 2. Of those that a mesh axis runs over, the one named last changes fastest.
Arguments:
- activations: bfloat16 [4, 2048, 8192], P(None, 'dp', 'tp'), may hold values from -6 to 6
- value_weight: bfloat16 [8192, 1024], P('tp'), may hold values from -0.0625 to 0.0625
- shrink_store: bfloat16 [8192, 8192], P('tp', 'dp'), may hold values from -0.0625 to 0.0625
- expand_store: bfloat16 [8192, 1024], P('dp', 'tp'), may hold values from -0.75 to 0.75
- adapter_row: int32 [128], replicated, may hold values from 0 to 127, as said below
- token_adapter: int32 [4, 2048], P(None, 'dp'), may hold values from 0 to 132, as said below
- hot_ids: int32 [4, 4], replicated, may hold values from 0 to 127, as said below
Outputs:
- adapted: bfloat16 [4, 2048, 1024], P(None, 'dp', 'tp')
The draws below stay inside these ranges and needn't reach their ends.
Inputs may be any that keep to these rules, and one draw needn't show every extreme that they name: `token_adapter`: code 128 + 4 means no adapter. In each step, of the tokens of one device's aligned block of 128, at most 16 name adapters stored by one owner (rows owner * 8 to owner * 8 + 7), and at most 2 do so by a code of 4 or more. `hot_ids`: the 4 adapters of a step are different. `adapter_row`: A permutation of the stored rows.
All inputs are finite; a program needn't handle non-finite values.
Results may differ from the reference program's by a relative error of at most 0.0047.
Values may be sent and summed in bfloat16 or wider, within the bound.
No kernel may reach another device: no remote copies, remote signals or barrier semaphores. Data moves between devices by JAX's collectives and lax.ppermute only.
A program may use at most 128 MiB of HBM per device.

```python
import jax
import jax.numpy as jnp
from jax import lax

D = 8192
KV = 1024
R = 64
STEPS = 4
HOT = 4
CAP = 2
TOK_DEV = 128
ADP_DEV = 8
HCAP = 16
NCOLD = 8
NADP = 128
TOKENS = 2048


def routing_tables(key):
    dp_count = NADP // ADP_DEV
    block_count = TOKENS // TOK_DEV
    row_of = jax.random.permutation(jax.random.fold_in(key, 11), NADP).astype(jnp.int32)
    adapter_at = jnp.argsort(row_of).astype(jnp.int32)

    def one_step(step_key):
        keys = jax.random.split(step_key, 3)
        common = jax.random.randint(keys[0], (), 0, dp_count)
        hot_owner = (common + jnp.arange(HOT)) % dp_count
        hot_rows = hot_owner * ADP_DEV + jax.random.randint(keys[1], (HOT,), 0, ADP_DEV)
        hot_now = adapter_at[hot_rows]

        def one_block(block_key):
            parts = jax.random.split(block_key, 5)
            hot_size = jax.random.randint(parts[0], (HOT,), 1, HCAP + 1).at[0].set(HCAP)
            cold_size = jax.random.randint(parts[1], (NCOLD,), 1, CAP + 1).at[0].set(CAP)
            others = jax.random.permutation(parts[2], dp_count - HOT - 1)[:NCOLD - 1] + HOT + 1
            offsets = jnp.concatenate([jnp.full((1,), HOT, jnp.int32), others.astype(jnp.int32)])
            cold_owner = (common + offsets) % dp_count
            cold_rows = cold_owner[:, None] * ADP_DEV + jax.random.randint(parts[3], (NCOLD, CAP), 0, ADP_DEV)
            cold_ids = adapter_at[cold_rows] + HOT
            none_code = NADP + HOT
            hot_grid = jnp.where(jnp.arange(HCAP)[None, :] < hot_size[:, None], jnp.arange(HOT)[:, None], none_code)
            cold_grid = jnp.where(jnp.arange(CAP)[None, :] < cold_size[:, None], cold_ids, none_code)
            filler = jnp.full((TOK_DEV - HOT * HCAP - NCOLD * CAP,), none_code, jnp.int32)
            codes = jnp.concatenate([hot_grid.reshape(-1).astype(jnp.int32), cold_grid.reshape(-1).astype(jnp.int32), filler])
            return codes[jax.random.permutation(parts[4], TOK_DEV)]
        blocks = jax.vmap(one_block)(jax.random.split(keys[2], block_count))
        return (blocks.reshape(-1), hot_now.astype(jnp.int32))
    routes, hot_table = jax.vmap(one_step)(jax.random.split(jax.random.fold_in(key, 23), STEPS))
    return (row_of, routes.astype(jnp.int32), hot_table)


def draw_adapter_row(key, part):
    return routing_tables(key)[0]


def draw_token_adapter(key, part):
    return routing_tables(key)[1]


def draw_hot_ids(key, part):
    return routing_tables(key)[2]


def block_scale(key, shape, pieces, least, top_value):
    level, own = 1.0, jax.random.fold_in(key, 6)
    for axis_at, blocks in pieces:
        draws = jnp.exp(jax.random.uniform(jax.random.fold_in(own, axis_at), (blocks,), jnp.float32, least / len(pieces), top_value / len(pieces)))
        level = level * jnp.repeat(draws, shape[axis_at] // blocks).reshape([-1 if axis == axis_at else 1 for axis in range(len(shape))])
    return level


def noise(key, dims, width, limit, shards=(), dtype=jnp.bfloat16):
    drawn = jax.random.normal(key, dims, jnp.float32) * width
    if len(shards) > 0:
        drawn = block_scale(key, dims, shards, -0.22, 0.18) * drawn
    return jnp.clip(drawn, min=-limit, max=limit).astype(dtype)


def setup_inputs(seed: int = 0) -> dict:
    streams_of = jax.random.split(jax.random.key(seed), 8)
    return {
        "activations": noise(streams_of[0], (STEPS, TOKENS, D), 1.0, 6.0, ((1, 16), (2, 2))),
        "value_weight": noise(streams_of[1], (D, KV), D ** -0.5, 0.0625, ((0, 2),)),
        "shrink_store": noise(streams_of[2], (D, NADP * R), D ** -0.5, 0.0625, ((0, 2), (1, 16))),
        "expand_store": noise(streams_of[3], (NADP * R, KV), R ** -0.5, 0.75, ((0, 16), (1, 2))),
        "adapter_row": draw_adapter_row(jax.random.fold_in(streams_of[7], 71), 0),
        "token_adapter": draw_token_adapter(jax.random.fold_in(streams_of[7], 71), 0),
        "hot_ids": draw_hot_ids(jax.random.fold_in(streams_of[7], 71), 0),
    }


def reference(activations, value_weight, shrink_store, expand_store, adapter_row, token_adapter, hot_ids):
    shrink_rows = jnp.transpose(shrink_store.reshape(D, NADP, R), (1, 2, 0)).astype(jnp.float32)
    expand_rows = expand_store.reshape(NADP, R, KV).astype(jnp.float32)
    none_code = NADP + HOT
    results = []
    for step in range(STEPS):
        route_now = token_adapter[step]
        picked = hot_ids[step][jnp.clip(route_now, 0, HOT - 1)]
        adapter = jnp.where(route_now < HOT, picked, route_now - HOT)
        adapter = jnp.clip(adapter, 0, NADP - 1).astype(jnp.int32)
        store_row = adapter_row[adapter]
        is_live = route_now < none_code
        tokens_now = activations[step]
        base_part = jnp.dot(tokens_now, value_weight, preferred_element_type=jnp.float32)

        def one_block(packed):
            token_block, row_block = packed
            shrink_cols = shrink_rows[row_block]
            z_rows = jnp.einsum("td,trd->tr", token_block.astype(jnp.float32), shrink_cols).astype(jnp.bfloat16)
            expand_cols = expand_rows[row_block]
            return jnp.einsum("tr,trk->tk", z_rows.astype(jnp.float32), expand_cols).astype(jnp.bfloat16)

        delta_rows = lax.map(one_block, (tokens_now.reshape(-1, 64, D), store_row.reshape(-1, 64)))
        delta_rows = delta_rows.reshape(TOKENS, KV)
        delta_rows = jnp.where(is_live[:, None], delta_rows, jnp.zeros_like(delta_rows))
        delta_rows = lax.optimization_barrier(delta_rows)
        results.append((base_part + delta_rows.astype(jnp.float32)).astype(jnp.bfloat16))
    return jnp.stack(results)
```

```python
import jax
import jax.numpy as jnp
from jax import lax
from jax.sharding import Mesh, PartitionSpec as P

R = 64
CAP = 2
HCAP = 16
DP = ("z", "x", "core")
LAYER = ("x", "core")


def pick(flags):
    return flags.astype(jnp.bfloat16)


def matmul(a, b):
    return jnp.dot(a, b, preferred_element_type=jnp.float32)


def sum_over_tp(part):
    if lax.axis_size("tp") == 2:
        return part + lax.ppermute(part, "tp", [(0, 1), (1, 0)])
    return lax.psum(part, "tp")


def line_stages(n):
    half = n // 2
    stages = [([(k, k + 1), (n - 1 - k, n - 2 - k)], None) for k in range(half - 1)]
    stages.append(([(half - 1, half), (half, half - 1)], None))
    stages += [([(k + 1, k), (n - 2 - k, n - 1 - k)], k) for k in reversed(range(half - 1))]
    return stages


def hot_factors(store, selector, step_count):
    x_at, core_at, z_at = lax.axis_index("x"), lax.axis_index("core"), lax.axis_index("z")
    depth, width = store.shape
    quarter = depth // 4
    cols = selector.shape[1] // step_count
    halves = store.reshape(2, 2, quarter, width)
    other = lax.dynamic_index_in_dim(halves, 1 - core_at, 1, keepdims=False).reshape(2 * quarter, width)
    mine = lax.dynamic_index_in_dim(halves, core_at, 1, keepdims=False).reshape(2 * quarter, width)
    swap = [(0, 1), (1, 0)]
    z_count = lax.axis_size("z")
    stages = line_stages(z_count)
    stage_count = 2 + len(stages)
    picked = [selector[:, s * cols:(s + 1) * cols] for s in range(step_count)]
    sends = [matmul(other, p).astype(jnp.bfloat16) for p in picked]
    keeps = [matmul(mine, p).astype(jnp.bfloat16) for p in picked]
    held = [None] * step_count
    for wave in range(step_count + stage_count - 1):
        active = [s for s in range(step_count) if 0 <= wave - s < stage_count]
        got = []
        for s in active:
            stage = wave - s
            if stage == 0:
                got.append(lax.ppermute(sends[s], "core", swap))
            elif stage == 1:
                got.append(lax.ppermute(sends[s], "x", swap))
            else:
                got.append(lax.ppermute(held[s], "z", stages[stage - 2][0]))
        nxt = wave + 1
        if nxt < step_count:
            *got, sends[nxt] = lax.optimization_barrier((*got, sends[nxt]))
        else:
            got = lax.optimization_barrier(tuple(got))
        for s, piece in zip(active, got):
            stage = wave - s
            if stage == 0:
                total = (keeps[s] + piece).reshape(2, quarter, cols)
                sends[s] = lax.dynamic_index_in_dim(total, 1 - x_at, 0, keepdims=False)
                held[s] = lax.dynamic_index_in_dim(total, x_at, 0, keepdims=False)
            elif stage == 1 or stages[stage - 2][1] is None:
                held[s] = held[s] + piece
            else:
                k = stages[stage - 2][1]
                held[s] = jnp.where((z_at == k) | (z_at == z_count - 1 - k), piece, held[s])
    return held


def on_device(
    activations, value_weight, shrink_store, expand_store, adapter_row, token_adapter, hot_ids
):
    step_count, token_count, depth = activations.shape
    adapter_count = adapter_row.shape[0]
    hot_count = hot_ids.shape[1]
    per_dev = expand_store.shape[0] // R
    head_part = expand_store.shape[1]
    dp_count = lax.axis_size("z") * lax.axis_size("x") * lax.axis_size("core")
    layer_count = 4
    tp_count = lax.axis_size("tp")
    me = lax.axis_index(DP)
    none_code = adapter_count + hot_count
    tokens_all = step_count * token_count
    rows = activations.reshape(tokens_all, depth)

    names = jnp.arange(adapter_count, dtype=jnp.int32)
    hot_row = jnp.sum(jnp.where(hot_ids[:, :, None] == names, adapter_row, 0), axis=-1)
    hot_first = jnp.where(hot_row // per_dev == me, (hot_row % per_dev) * R, -R * per_dev)
    cold_row = jnp.sum(jnp.where((token_adapter - hot_count)[:, :, None] == names, adapter_row, 0), axis=-1)
    is_hot = token_adapter < hot_count
    is_cold = (token_adapter < none_code) & jnp.logical_not(is_hot)
    owner = cold_row // per_dev
    group = jnp.where(is_hot, token_adapter, jnp.where(is_cold, hot_count + owner, -1))
    at = jnp.arange(token_count, dtype=jnp.int32)
    before = (group[:, :, None] == group[:, None, :]) & (at[None, :] < at[:, None])
    rank = jnp.sum(before.astype(jnp.int32), axis=-1)
    step_at = jnp.arange(step_count, dtype=jnp.int32)[:, None]
    hot_rows = step_count * hot_count * HCAP
    cold_rows = dp_count * step_count * CAP
    hot_target = (step_at * hot_count + token_adapter) * HCAP + rank
    cold_target = (owner * step_count + step_at) * CAP + rank
    hot_target = jnp.where(is_hot, hot_target, -1).reshape(-1)
    cold_target = jnp.where(is_cold, cold_target, -1).reshape(-1)
    place_hot = pick(jnp.arange(hot_rows, dtype=jnp.int32)[:, None] == hot_target)
    cold_hit = jnp.arange(cold_rows, dtype=jnp.int32)[:, None] == cold_target
    place_cold = pick(cold_hit)
    tag = jnp.sum(jnp.where(cold_hit, (cold_row % per_dev + 1).reshape(-1), 0), axis=-1)

    column = jnp.arange(per_dev * R, dtype=jnp.int32)
    lane = jnp.arange(R, dtype=jnp.int32)
    wanted = (hot_first.reshape(-1)[:, None] + lane).reshape(-1)
    shrink_hot = hot_factors(shrink_store, pick(column[:, None] == wanted), step_count)
    expand_hot = lax.psum(
        matmul(pick(wanted[:, None] == column), expand_store).astype(jnp.bfloat16), DP
    )

    rows_out = matmul(place_cold, rows).astype(jnp.bfloat16)
    tag_out = jnp.broadcast_to(tag.astype(jnp.bfloat16)[:, None], (cold_rows, 128))
    packet = jnp.concatenate([rows_out, tag_out], axis=1).reshape(dp_count, step_count * CAP, depth + 128)
    packet = lax.all_to_all(packet, DP, split_axis=0, concat_axis=0, tiled=True)
    packet = packet.reshape(cold_rows, depth + 128)
    tag_in = packet[:, depth:depth + 1].astype(jnp.int32)
    chosen = (column // R + 1)[None, :] == tag_in
    z_cold = sum_over_tp(jnp.where(chosen, matmul(packet[:, :depth], shrink_store), 0.0))
    delta_cold = matmul(z_cold.astype(jnp.bfloat16), expand_store).astype(jnp.bfloat16)
    delta_cold = lax.all_to_all(
        delta_cold.reshape(dp_count, step_count * CAP, head_part), DP, split_axis=0, concat_axis=0, tiled=True
    ).reshape(cold_rows, head_part)

    quarter = depth // layer_count
    hot_out = jnp.stack(
        [matmul(place_hot, rows[:, q * quarter:(q + 1) * quarter]).astype(jnp.bfloat16) for q in range(layer_count)]
    )
    hot_in = lax.all_to_all(hot_out, LAYER, split_axis=0, concat_axis=0, tiled=True)
    hot_in = hot_in.reshape(layer_count, step_count, hot_count * HCAP, quarter)
    pairs = hot_count // 2
    low = (jnp.arange(2 * R) < R)[None, None, :]
    z_parts = []
    for s in range(step_count):
        dense = matmul(hot_in[:, s].reshape(-1, quarter), shrink_hot[s])
        dense = dense.reshape(layer_count, pairs, 2, HCAP, pairs, 2 * R)
        z_parts.append(
            jnp.stack(
                [jnp.where(low, dense[:, p, 0, :, p], dense[:, p, 1, :, p]) for p in range(pairs)], axis=1
            )
        )
    z_part = jnp.stack(z_parts, axis=1).reshape(layer_count, step_count * pairs * HCAP, 2 * R)
    z_part = jnp.broadcast_to(z_part[None], (tp_count, *z_part.shape)).reshape(-1, *z_part.shape[1:])
    z_hot = lax.all_to_all(z_part, ("tp", *LAYER), split_axis=0, concat_axis=0, tiled=True)
    z_hot = jnp.sum(z_hot, axis=0).astype(jnp.bfloat16)
    groups = step_count * pairs
    spread = jnp.where(
        (jnp.arange(groups)[:, None, None, None, None] == jnp.arange(groups)[:, None])
        & (jnp.arange(2)[:, None, None, None] == (jnp.arange(2 * R) // R)),
        z_hot.reshape(groups, 1, HCAP, 1, 2 * R),
        jnp.zeros((), jnp.bfloat16),
    ).reshape(hot_rows, groups * 2 * R)
    delta_hot = matmul(spread, expand_hot).astype(jnp.bfloat16)

    base = lax.psum_scatter(matmul(rows, value_weight), "tp", scatter_dimension=1, tiled=True)
    place = jnp.concatenate([place_hot, place_cold], axis=0)
    delta = lax.dot_general(
        place,
        jnp.concatenate([delta_hot, delta_cold], axis=0),
        (((0,), (0,)), ((), ())),
        preferred_element_type=jnp.float32,
    )
    return (base + delta).astype(jnp.bfloat16).reshape(step_count, token_count, head_part)


def solution(mesh):
    tp_count, dp_count = mesh.shape["tp"], mesh.shape["dp"]
    fine = Mesh(mesh.devices.reshape(tp_count, dp_count // 4, 2, 2), ("tp", *DP))
    placed = (
        P(None, DP, "tp"),
        P("tp", None),
        P("tp", DP),
        P(DP, "tp"),
        P(),
        P(None, DP),
        P(),
    )
    return jax.shard_map(
        on_device, mesh=fine, in_specs=placed, out_specs=P(None, DP, "tp"), check_vma=False
    )
```

```python
import jax
import jax.numpy as jnp
from jax import lax
from jax.sharding import Mesh, PartitionSpec as P

R = 64
CAP = 2
HCAP = 16
DP = ("z", "x", "core")
LAYER = ("x", "core")
SWAP = [(0, 1), (1, 0)]


def pick(flags):
    return flags.astype(jnp.bfloat16)


def matmul(a, b):
    return jnp.dot(a, b, preferred_element_type=jnp.float32)


def narrow(a, b):
    return matmul(a, b).astype(jnp.bfloat16)


def sum_over_tp(part):
    if lax.axis_size("tp") == 2:
        return part + lax.ppermute(part, "tp", SWAP)
    return lax.psum(part, "tp")


def after(value, *others):
    return lax.optimization_barrier((value, *others))[0]


def line_sum(held):
    n, z_at = lax.axis_size("z"), lax.axis_index("z")
    half = n // 2
    for k in range(half - 1):
        held = held + lax.ppermute(held, "z", [(k, k + 1), (n - 1 - k, n - 2 - k)])
    held = held + lax.ppermute(held, "z", [(half - 1, half), (half, half - 1)])
    pieces = [held]
    for k in reversed(range(half - 1)):
        got = lax.ppermute(held, "z", [(k + 1, k), (n - 2 - k, n - 1 - k)])
        here = (z_at == k) | (z_at == n - 1 - k)
        if k > 0:
            held = jnp.where(here, got, held)
        else:
            pieces = [jnp.where(here, jnp.zeros_like(held), held), got]
    return pieces


def on_device(
    activations, value_weight, shrink_store, expand_store, adapter_row, token_adapter, hot_ids
):
    step_count, token_count, depth = activations.shape
    adapter_count = adapter_row.shape[0]
    hot_count = hot_ids.shape[1]
    per_dev = expand_store.shape[0] // R
    head_part = expand_store.shape[1]
    dp_count = lax.axis_size("z") * lax.axis_size("x") * lax.axis_size("core")
    me = lax.axis_index(DP)
    x_at, core_at = lax.axis_index("x"), lax.axis_index("core")
    none_code = adapter_count + hot_count
    rows = activations.reshape(step_count * token_count, depth)

    names = jnp.arange(adapter_count, dtype=jnp.int32)
    hot_row = jnp.sum(jnp.where(hot_ids[:, :, None] == names, adapter_row, 0), axis=-1)
    hot_first = jnp.where(hot_row // per_dev == me, (hot_row % per_dev) * R, -R * per_dev)
    column = jnp.arange(per_dev * R, dtype=jnp.int32)
    lane = jnp.arange(R, dtype=jnp.int32)
    entry = jnp.arange(hot_count, dtype=jnp.int32)

    def wanted(core):
        order = [2 * x_at + core, 2 * (1 - x_at) + core]
        first = [jnp.sum(jnp.where(entry == e, hot_first, 0), axis=1) for e in order]
        return jnp.concatenate([(f[:, None] + lane).reshape(-1) for f in first])

    want_mine, want_other = wanted(core_at), wanted(1 - core_at)
    kept = step_count * R
    chunk_count = 4
    part = depth // chunk_count

    def gathered(other, mine, cut, previous):
        got = lax.ppermute(other, "core", SWAP)
        send = cut(mine, True) + cut(got, True)
        if previous is not None:
            send = after(send, previous)
        crossed = lax.ppermute(send, "x", SWAP)
        return line_sum(cut(mine) + cut(got) + crossed), send, crossed

    def cut_columns(block, last=False):
        return block[:, kept:] if last else block[:, :kept]

    def cut_rows(block, last=False):
        return block[kept:] if last else block[:kept]

    pick_mine, pick_other = lax.optimization_barrier(
        (pick(column[:, None] == want_mine), pick(column[:, None] == want_other))
    )
    shrink_hot, sent, over_x = [], [], []
    for c in range(chunk_count):
        store = shrink_store[c * part:(c + 1) * part]
        if c > 0:
            step_before = sent[0] if c == 1 else over_x[c - 2]
            pick_mine, pick_other = after(pick_mine, step_before), after(pick_other, step_before)
        pieces, send, crossed = gathered(
            narrow(store, pick_other), narrow(store, pick_mine), cut_columns, over_x[-1] if over_x else None
        )
        shrink_hot.append(pieces)
        sent.append(send)
        over_x.append(crossed)
    want_mine, want_other = after(want_mine, over_x[-2]), after(want_other, over_x[-2])
    expand_hot, _, _ = gathered(
        narrow(pick(want_other[:, None] == column), expand_store),
        narrow(pick(want_mine[:, None] == column), expand_store),
        cut_rows,
        over_x[-1],
    )
    expand_hot = sum(expand_hot[1:], expand_hot[0])

    token_adapter = after(token_adapter, sent[0])
    cold_row = jnp.sum(jnp.where((token_adapter - hot_count)[:, :, None] == names, adapter_row, 0), axis=-1)
    is_hot = token_adapter < hot_count
    is_cold = (token_adapter < none_code) & jnp.logical_not(is_hot)
    owner = cold_row // per_dev
    group = jnp.where(is_hot, token_adapter, jnp.where(is_cold, hot_count + owner, -1))
    at = jnp.arange(token_count, dtype=jnp.int32)
    before = (group[:, :, None] == group[:, None, :]) & (at[None, :] < at[:, None])
    rank = jnp.sum(before.astype(jnp.int32), axis=-1)
    step_at = jnp.arange(step_count, dtype=jnp.int32)[:, None]
    hot_rows = hot_count * step_count * HCAP
    cold_rows = dp_count * step_count * CAP
    hot_target = (token_adapter * step_count + step_at) * HCAP + rank
    cold_target = (owner * step_count + step_at) * CAP + rank
    hot_target = jnp.where(is_hot, hot_target, -1).reshape(-1)
    cold_target = jnp.where(is_cold, cold_target, -1).reshape(-1)
    place_hot = pick(jnp.arange(hot_rows, dtype=jnp.int32)[:, None] == hot_target)
    cold_hit = jnp.arange(cold_rows, dtype=jnp.int32)[:, None] == cold_target
    place_cold = pick(cold_hit)
    tag = jnp.sum(jnp.where(cold_hit, (cold_row % per_dev + 1).reshape(-1), 0), axis=-1)

    tag_out = jnp.broadcast_to(tag.astype(jnp.bfloat16)[:, None], (cold_rows, 128))
    packet = jnp.concatenate([narrow(place_cold, rows), tag_out], axis=1)
    packet = packet.reshape(dp_count, step_count * CAP, depth + 128)
    packet = lax.all_to_all(packet, DP, split_axis=0, concat_axis=0, tiled=True)
    packet = packet.reshape(cold_rows, depth + 128)
    tag_in = packet[:, depth:depth + 1].astype(jnp.int32)
    chosen = (column // R + 1)[None, :] == tag_in
    z_cold = sum_over_tp(jnp.where(chosen, matmul(packet[:, :depth], shrink_store), 0.0))
    delta_cold = narrow(z_cold.astype(jnp.bfloat16), expand_store)
    delta_cold = lax.all_to_all(
        delta_cold.reshape(dp_count, step_count * CAP, head_part), DP, split_axis=0, concat_axis=0, tiled=True
    ).reshape(cold_rows, head_part)

    base = lax.psum_scatter(
        matmul(rows, after(value_weight, over_x[0])), "tp", scatter_dimension=1, tiled=True
    )

    hot_out = after(narrow(after(place_hot, over_x[1]), rows), over_x[-1])
    hot_out = hot_out.reshape(hot_count, step_count * HCAP, depth)
    hot_in = lax.all_to_all(hot_out, LAYER, split_axis=0, concat_axis=0, tiled=True).reshape(hot_rows, depth)
    dense = None
    for c, pieces in enumerate(shrink_hot):
        for piece in pieces:
            product = matmul(hot_in[:, c * part:(c + 1) * part], piece)
            dense = product if dense is None else dense + product
    pairs = step_count // 2
    dense = dense.reshape(hot_count, pairs, 2, HCAP, pairs, 2 * R)
    low = (jnp.arange(2 * R) < R)[None, None, :]
    z_part = jnp.stack([jnp.where(low, dense[:, p, 0, :, p], dense[:, p, 1, :, p]) for p in range(pairs)], axis=1)
    z_part = after(z_part.reshape(hot_rows // 2, 2 * R), delta_cold)
    z_hot = sum_over_tp(z_part).astype(jnp.bfloat16)
    same_pair = jnp.arange(pairs)[:, None, None, None, None] == jnp.arange(pairs)[:, None]
    same_half = jnp.arange(2)[:, None, None, None] == jnp.arange(2 * R) // R
    spread = jnp.where(
        same_pair & same_half,
        z_hot.reshape(hot_count, pairs, 1, HCAP, 1, 2 * R),
        jnp.zeros((), jnp.bfloat16),
    ).reshape(hot_rows, kept)
    delta_hot = narrow(spread, expand_hot).reshape(hot_count, step_count * HCAP, head_part)
    delta_hot = lax.all_to_all(delta_hot, LAYER, split_axis=0, concat_axis=0, tiled=True)

    delta = lax.dot_general(
        jnp.concatenate([place_hot, place_cold], axis=0),
        jnp.concatenate([delta_hot.reshape(hot_rows, head_part), delta_cold], axis=0),
        (((0,), (0,)), ((), ())),
        preferred_element_type=jnp.float32,
    )
    return (base + delta).astype(jnp.bfloat16).reshape(step_count, token_count, head_part)


def solution(mesh):
    tp_count, dp_count = mesh.shape["tp"], mesh.shape["dp"]
    fine = Mesh(mesh.devices.reshape(tp_count, dp_count // 4, 2, 2), ("tp", *DP))
    placed = (
        P(None, DP, "tp"),
        P("tp", None),
        P("tp", DP),
        P(DP, "tp"),
        P(),
        P(None, DP),
        P(),
    )
    return jax.shard_map(
        on_device, mesh=fine, in_specs=placed, out_specs=P(None, DP, "tp"), check_vma=False
    )
```

```python
import jax
import jax.numpy as jnp
from jax import lax
from jax.sharding import Mesh, PartitionSpec as P

R = 64
CAP = 2
HCAP = 16
DP = ("z", "x", "core")
LAYER = ("x", "core")
SWAP = [(0, 1), (1, 0)]


def pick(flags):
    return flags.astype(jnp.bfloat16)


def matmul(a, b):
    return jnp.dot(a, b, preferred_element_type=jnp.float32)


def narrow(a, b):
    return matmul(a, b).astype(jnp.bfloat16)


def sum_over_tp(part):
    if lax.axis_size("tp") == 2:
        return part + lax.ppermute(part, "tp", SWAP)
    return lax.psum(part, "tp")


def after(value, *others):
    return lax.optimization_barrier((value, *others))[0]


class Chain:
    def __init__(self):
        self.last = None

    def hold(self, value):
        self.last = value if self.last is None else after(value, self.last)
        return self.last

    def permute(self, value, axis, pairs):
        return lax.ppermute(self.hold(value), axis, pairs)


def line_hops(n):
    half = n // 2
    hops = [([(k, k + 1), (n - 1 - k, n - 2 - k)], None) for k in range(half - 1)]
    hops.append(([(half - 1, half), (half, half - 1)], None))
    hops += [([(k + 1, k), (n - 2 - k, n - 1 - k)], k) for k in reversed(range(half - 1))]
    return hops


def on_device(
    activations, value_weight, shrink_store, expand_store, adapter_row, token_adapter, hot_ids
):
    step_count, token_count, depth = activations.shape
    adapter_count = adapter_row.shape[0]
    hot_count = hot_ids.shape[1]
    per_dev = expand_store.shape[0] // R
    head_part = expand_store.shape[1]
    dp_count = lax.axis_size("z") * lax.axis_size("x") * lax.axis_size("core")
    me = lax.axis_index(DP)
    x_at, core_at = lax.axis_index("x"), lax.axis_index("core")
    none_code = adapter_count + hot_count
    rows = activations.reshape(step_count * token_count, depth)

    names = jnp.arange(adapter_count, dtype=jnp.int32)
    hot_row = jnp.sum(jnp.where(hot_ids[:, :, None] == names, adapter_row, 0), axis=-1)
    hot_first = jnp.where(hot_row // per_dev == me, (hot_row % per_dev) * R, -R * per_dev)
    column = jnp.arange(per_dev * R, dtype=jnp.int32)
    lane = jnp.arange(R, dtype=jnp.int32)
    entry = jnp.arange(hot_count, dtype=jnp.int32)

    def wanted(core):
        order = [2 * x_at + core, 2 * (1 - x_at) + core]
        first = [jnp.sum(jnp.where(entry == e, hot_first, 0), axis=1) for e in order]
        return jnp.concatenate([(f[:, None] + lane).reshape(-1) for f in first])

    want_mine, want_other = wanted(core_at), wanted(1 - core_at)
    kept = step_count * R
    chunk_count = 4
    part = depth // chunk_count

    chain = Chain()
    pick_mine, pick_other = lax.optimization_barrier(
        (pick(column[:, None] == want_mine), pick(column[:, None] == want_other))
    )
    z_at, z_count = lax.axis_index("z"), lax.axis_size("z")
    hops = line_hops(z_count)

    swapped = [lax.ppermute(chain.hold(narrow(shrink_store[:part], pick_other)), "core", SWAP)]
    mine_all = narrow(after(shrink_store, chain.last), pick_mine)
    mine = [mine_all[:part]]
    crossed = [chain.permute(mine[0][:, kept:] + swapped[0][:, kept:], "x", SWAP)]
    rest = lax.ppermute(chain.hold(narrow(shrink_store[part:], after(pick_other, chain.last))), "core", SWAP)

    token_adapter = after(token_adapter, chain.last)
    cold_row = jnp.sum(jnp.where((token_adapter - hot_count)[:, :, None] == names, adapter_row, 0), axis=-1)
    is_hot = token_adapter < hot_count
    is_cold = (token_adapter < none_code) & jnp.logical_not(is_hot)
    owner = cold_row // per_dev
    group = jnp.where(is_hot, token_adapter, jnp.where(is_cold, hot_count + owner, -1))
    at = jnp.arange(token_count, dtype=jnp.int32)
    before = (group[:, :, None] == group[:, None, :]) & (at[None, :] < at[:, None])
    rank = jnp.sum(before.astype(jnp.int32), axis=-1)
    step_at = jnp.arange(step_count, dtype=jnp.int32)[:, None]
    hot_rows = hot_count * step_count * HCAP
    cold_rows = dp_count * step_count * CAP
    hot_target = (token_adapter * step_count + step_at) * HCAP + rank
    cold_target = (owner * step_count + step_at) * CAP + rank
    hot_target = jnp.where(is_hot, hot_target, -1).reshape(-1)
    cold_target = jnp.where(is_cold, cold_target, -1).reshape(-1)
    place_hot = pick(jnp.arange(hot_rows, dtype=jnp.int32)[:, None] == hot_target)
    cold_hit = jnp.arange(cold_rows, dtype=jnp.int32)[:, None] == cold_target
    place_cold = pick(cold_hit)
    tag = jnp.sum(jnp.where(cold_hit, (cold_row % per_dev + 1).reshape(-1), 0), axis=-1)

    tag_out = jnp.broadcast_to(tag.astype(jnp.bfloat16)[:, None], (cold_rows, 128))
    packet = jnp.concatenate([narrow(place_cold, rows), tag_out], axis=1)
    packet = chain.hold(packet.reshape(dp_count, step_count * CAP, depth + 128))
    packet = lax.all_to_all(packet, DP, split_axis=0, concat_axis=0, tiled=True).reshape(cold_rows, depth + 128)

    done = {}

    def expand_pick():
        late_mine, late_other = after(want_mine, chain.last), after(want_other, chain.last)
        done["expand_other"] = narrow(pick(late_other[:, None] == column), expand_store)
        done["expand_mine"] = narrow(pick(late_mine[:, None] == column), expand_store)

    def expand_over_core():
        done["expand_swapped"] = chain.permute(done["expand_other"], "core", SWAP)

    def hot_tokens_rows():
        done["hot_out"] = narrow(after(place_hot, chain.last), rows)

    def hot_tokens_out():
        hot_out = chain.hold(done["hot_out"].reshape(hot_count, step_count * HCAP, depth))
        hot_in = lax.all_to_all(hot_out, LAYER, split_axis=0, concat_axis=0, tiled=True)
        done["hot_in"] = hot_in.reshape(hot_rows, depth)

    def base_product():
        done["whole"] = matmul(rows, after(value_weight, chain.last))

    def base_over_tp():
        whole = done["whole"]
        if lax.axis_size("tp") == 2:
            first = lax.axis_index("tp") == 0
            halves = whole[:, :head_part], whole[:, head_part:]
            other = jnp.where(first, halves[1], halves[0])
            done["base"] = jnp.where(first, *halves), chain.permute(other, "tp", SWAP)
        else:
            base = lax.psum_scatter(chain.hold(whole), "tp", scatter_dimension=1, tiled=True)
            done["base"] = base, jnp.zeros_like(base)

    def cold_shrink():
        tag_in = packet[:, depth:depth + 1].astype(jnp.int32)
        chosen = (column // R + 1)[None, :] == tag_in
        product = matmul(packet[:, :depth], after(shrink_store, chain.last))
        done["z_part"] = jnp.where(chosen, product, 0.0)

    def cold_over_tp():
        done["z_cold"] = sum_over_tp(chain.hold(done["z_part"]))

    def cold_expand():
        done["delta"] = narrow(done["z_cold"].astype(jnp.bfloat16), after(expand_store, chain.last))

    def cold_back():
        delta = chain.hold(done["delta"].reshape(dp_count, step_count * CAP, head_part))
        delta = lax.all_to_all(delta, DP, split_axis=0, concat_axis=0, tiled=True)
        done["delta_cold"] = delta.reshape(cold_rows, head_part)

    between = {
        (1, "end"): [hot_tokens_rows, expand_pick],
        (2, "end"): [expand_over_core, base_product],
        (3, "end"): [cold_shrink],
        (4, "x"): [hot_tokens_out],
        (4, "end"): [base_over_tp, cold_over_tp],
        (5, "end"): [cold_expand],
        (6, "end"): [cold_back],
    }
    held = [None] * (chunk_count + 1)
    factors = [None] * (chunk_count + 1)
    for slot in range(1, chunk_count + 1 + len(hops)):
        if slot <= chunk_count:
            c = slot
            if c < chunk_count:
                at = slice(c * part, (c + 1) * part)
                mine.append(after(mine_all, crossed[c - 1])[at])
                swapped.append(after(rest, crossed[c - 1])[(c - 1) * part:c * part])
                send = mine[c][:, kept:] + swapped[c][:, kept:]
            else:
                mine.append(done["expand_mine"])
                swapped.append(done["expand_swapped"])
                send = mine[c][kept:] + swapped[c][kept:]
            crossed.append(chain.permute(after(send, crossed[c - 1]), "x", SWAP))
        for work in between.get((slot, "x"), []):
            work()
        for stage, (hop, outward) in enumerate(hops):
            c = slot - 1 - stage
            if not 0 <= c <= chunk_count:
                continue
            if stage == 0:
                own, got = mine[c], swapped[c]
                own, got = (own[:, :kept], got[:, :kept]) if c < chunk_count else (own[:kept], got[:kept])
                held[c] = own + got + crossed[c]
            got = chain.permute(held[c], "z", hop)
            if outward is None:
                held[c] = held[c] + got
                factors[c] = [held[c]]
            else:
                here = (z_at == outward) | (z_at == z_count - 1 - outward)
                if outward > 0:
                    held[c] = jnp.where(here, got, held[c])
                else:
                    factors[c] = [jnp.where(here, jnp.zeros_like(held[c]), held[c]), got]
        for work in between.get((slot, "end"), []):
            work()
    *shrink_hot, expand_hot = factors
    expand_hot = sum(expand_hot[1:], expand_hot[0])
    hot_in, delta_cold = done["hot_in"], done["delta_cold"]
    base_kept, base_got = done["base"]

    dense = None
    for c, pieces in enumerate(shrink_hot):
        for piece in pieces:
            product = matmul(hot_in[:, c * part:(c + 1) * part], piece)
            dense = product if dense is None else dense + product
    pairs = step_count // 2
    dense = dense.reshape(hot_count, pairs, 2, HCAP, pairs, 2 * R)
    low = (jnp.arange(2 * R) < R)[None, None, :]
    z_part = jnp.stack([jnp.where(low, dense[:, p, 0, :, p], dense[:, p, 1, :, p]) for p in range(pairs)], axis=1)
    z_part = after(z_part.reshape(hot_rows // 2, 2 * R), delta_cold, base_got)
    z_hot = sum_over_tp(z_part).astype(jnp.bfloat16)
    same_pair = jnp.arange(pairs)[:, None, None, None, None] == jnp.arange(pairs)[:, None]
    same_half = jnp.arange(2)[:, None, None, None] == jnp.arange(2 * R) // R
    spread = jnp.where(
        same_pair & same_half,
        z_hot.reshape(hot_count, pairs, 1, HCAP, 1, 2 * R),
        jnp.zeros((), jnp.bfloat16),
    ).reshape(hot_rows, kept)
    delta_hot = narrow(spread, expand_hot).reshape(hot_count, step_count * HCAP, head_part)
    delta_hot = lax.all_to_all(delta_hot, LAYER, split_axis=0, concat_axis=0, tiled=True)

    delta = lax.dot_general(
        jnp.concatenate([place_hot, place_cold], axis=0),
        jnp.concatenate([delta_hot.reshape(hot_rows, head_part), delta_cold], axis=0),
        (((0,), (0,)), ((), ())),
        preferred_element_type=jnp.float32,
    )
    return (base_kept + base_got + delta).astype(jnp.bfloat16).reshape(step_count, token_count, head_part)


def solution(mesh):
    tp_count, dp_count = mesh.shape["tp"], mesh.shape["dp"]
    fine = Mesh(mesh.devices.reshape(tp_count, dp_count // 4, 2, 2), ("tp", *DP))
    placed = (
        P(None, DP, "tp"),
        P("tp", None),
        P("tp", DP),
        P(DP, "tp"),
        P(),
        P(None, DP),
        P(),
    )
    return jax.shard_map(
        on_device, mesh=fine, in_specs=placed, out_specs=P(None, DP, "tp"), check_vma=False
    )
```

```python
import jax
import jax.numpy as jnp
from jax import lax
from jax.sharding import Mesh, PartitionSpec as P

R = 64
CAP = 2
HCAP = 16
DP = ("z_high", "z_low", "x", "core")
GROUP = ("z_low", "x", "core")
SWAP = [(0, 1), (1, 0)]


def pick(flags):
    return flags.astype(jnp.bfloat16)


def matmul(a, b):
    return jnp.dot(a, b, preferred_element_type=jnp.float32)


def narrow(a, b):
    return matmul(a, b).astype(jnp.bfloat16)


def sum_over_tp(part):
    if lax.axis_size("tp") == 2:
        return part + lax.ppermute(part, "tp", SWAP)
    return lax.psum(part, "tp")


def after(value, *others):
    return lax.optimization_barrier((value, *others))[0]


class Chain:
    def __init__(self):
        self.last = None

    def hold(self, value):
        self.last = value if self.last is None else after(value, self.last)
        return self.last

    def permute(self, value, axis, pairs):
        return lax.ppermute(self.hold(value), axis, pairs)


def on_device(
    activations, value_weight, shrink_store, expand_store, adapter_row, token_adapter, hot_ids
):
    step_count, token_count, depth = activations.shape
    adapter_count = adapter_row.shape[0]
    hot_count = hot_ids.shape[1]
    per_dev = expand_store.shape[0] // R
    head_part = expand_store.shape[1]
    far_count = lax.axis_size("z_high")
    group_count = 8
    dp_count = far_count * group_count
    me = lax.axis_index(DP)
    z_at, x_at, core_at = lax.axis_index("z_low"), lax.axis_index("x"), lax.axis_index("core")
    none_code = adapter_count + hot_count
    rows = activations.reshape(step_count * token_count, depth)

    names = jnp.arange(adapter_count, dtype=jnp.int32)
    hot_row = jnp.sum(jnp.where(hot_ids[:, :, None] == names, adapter_row, 0), axis=-1)
    hot_first = jnp.where(hot_row // per_dev == me, (hot_row % per_dev) * R, -R * per_dev)
    column = jnp.arange(per_dev * R, dtype=jnp.int32)
    lane = jnp.arange(R, dtype=jnp.int32)
    entry = jnp.arange(hot_count, dtype=jnp.int32)
    near = step_count // 2

    def wanted(core):
        firsts = []
        for x in (x_at, 1 - x_at):
            of_steps = jnp.sum(jnp.where(entry == 2 * x + core, hot_first, 0), axis=1)
            firsts += [jnp.where(z_at == 0, of_steps[:near], of_steps[near:])]
            firsts += [jnp.where(z_at == 0, of_steps[near:], of_steps[:near])]
        return jnp.concatenate([(f[:, None] + lane).reshape(-1) for f in firsts])

    want_mine, want_other = wanted(core_at), wanted(1 - core_at)
    kept = near * R
    chunk_count = 4
    part = depth // chunk_count

    chain = Chain()
    pick_mine, pick_other = lax.optimization_barrier(
        (pick(column[:, None] == want_mine), pick(column[:, None] == want_other))
    )
    hops = [("x", SWAP), ("z_low", SWAP)]
    bit = 1
    while bit < far_count:
        hops.append(("z_high", [(i, i ^ bit) for i in range(far_count)]))
        bit *= 2

    def cut(block, c, first, last):
        return block[:, first * kept:last * kept] if c < chunk_count else block[first * kept:last * kept]

    swapped = [lax.ppermute(chain.hold(narrow(shrink_store[:part], pick_other)), "core", SWAP)]
    mine_all = narrow(after(shrink_store, chain.last), pick_mine)
    mine = [mine_all[:part]]
    rest = None
    got = {}
    held = {}

    def send(c, stage):
        if stage == 0:
            value = cut(mine[c], c, 2, 4) + cut(swapped[c], c, 2, 4)
        elif stage == 1:
            value = cut(mine[c], c, 1, 2) + cut(swapped[c], c, 1, 2) + cut(got[c, 0], c, 1, 2)
        elif stage == 2:
            value = cut(mine[c], c, 0, 1) + cut(swapped[c], c, 0, 1) + cut(got[c, 0], c, 0, 1) + got[c, 1]
            held[c] = value
        else:
            value = held[c] = held[c] + got[c, stage - 1]
        if c > 0:
            value = after(value, got[c - 1, stage])
        got[c, stage] = chain.permute(value, *hops[stage])

    send(0, 0)
    rest = lax.ppermute(chain.hold(narrow(shrink_store[part:], after(pick_other, chain.last))), "core", SWAP)

    token_adapter = after(token_adapter, chain.last)
    cold_row = jnp.sum(jnp.where((token_adapter - hot_count)[:, :, None] == names, adapter_row, 0), axis=-1)
    is_hot = token_adapter < hot_count
    is_cold = (token_adapter < none_code) & jnp.logical_not(is_hot)
    owner = cold_row // per_dev
    group = jnp.where(is_hot, token_adapter, jnp.where(is_cold, hot_count + owner, -1))
    at = jnp.arange(token_count, dtype=jnp.int32)
    before = (group[:, :, None] == group[:, None, :]) & (at[None, :] < at[:, None])
    rank = jnp.sum(before.astype(jnp.int32), axis=-1)
    step_at = jnp.arange(step_count, dtype=jnp.int32)[:, None]
    hot_rows = hot_count * step_count * HCAP
    cold_rows = dp_count * step_count * CAP
    hot_target = (((step_at // near) * hot_count + token_adapter) * near + step_at % near) * HCAP + rank
    cold_target = (owner * step_count + step_at) * CAP + rank
    hot_target = jnp.where(is_hot, hot_target, -1).reshape(-1)
    cold_target = jnp.where(is_cold, cold_target, -1).reshape(-1)
    place_hot = pick(jnp.arange(hot_rows, dtype=jnp.int32)[:, None] == hot_target)
    cold_hit = jnp.arange(cold_rows, dtype=jnp.int32)[:, None] == cold_target
    place_cold = pick(cold_hit)
    tag = jnp.sum(jnp.where(cold_hit, (cold_row % per_dev + 1).reshape(-1), 0), axis=-1)

    tag_out = jnp.broadcast_to(tag.astype(jnp.bfloat16)[:, None], (cold_rows, 128))
    packet = jnp.concatenate([narrow(place_cold, rows), tag_out], axis=1)
    packet = chain.hold(packet.reshape(dp_count, step_count * CAP, depth + 128))
    packet = lax.all_to_all(packet, DP, split_axis=0, concat_axis=0, tiled=True).reshape(cold_rows, depth + 128)

    done = {"hot_out": narrow(after(place_hot, chain.last), rows)}

    def expand_pick():
        late_mine, late_other = after(want_mine, chain.last), after(want_other, chain.last)
        done["expand_other"] = narrow(pick(late_other[:, None] == column), expand_store)
        done["expand_mine"] = narrow(pick(late_mine[:, None] == column), expand_store)

    def expand_over_core():
        done["expand_swapped"] = chain.permute(done["expand_other"], "core", SWAP)

    def hot_tokens_out():
        hot_out = chain.hold(done["hot_out"].reshape(group_count, near * HCAP, depth))
        hot_in = lax.all_to_all(hot_out, GROUP, split_axis=0, concat_axis=0, tiled=True)
        done["hot_in"] = hot_in.reshape(hot_rows, depth)

    def base_product():
        done["whole"] = matmul(rows, after(value_weight, chain.last))

    def base_over_tp():
        whole = done["whole"]
        if lax.axis_size("tp") == 2:
            first = lax.axis_index("tp") == 0
            halves = whole[:, :head_part], whole[:, head_part:]
            other = jnp.where(first, halves[1], halves[0])
            done["base"] = jnp.where(first, *halves), chain.permute(other, "tp", SWAP)
        else:
            base = lax.psum_scatter(chain.hold(whole), "tp", scatter_dimension=1, tiled=True)
            done["base"] = base, jnp.zeros_like(base)

    def cold_shrink():
        tag_in = packet[:, depth:depth + 1].astype(jnp.int32)
        chosen = (column // R + 1)[None, :] == tag_in
        product = matmul(packet[:, :depth], after(shrink_store, chain.last))
        done["z_part"] = jnp.where(chosen, product, 0.0)

    def cold_over_tp():
        done["z_cold"] = sum_over_tp(chain.hold(done["z_part"]))

    def cold_expand():
        done["delta"] = narrow(done["z_cold"].astype(jnp.bfloat16), after(expand_store, chain.last))

    def cold_back():
        delta = chain.hold(done["delta"].reshape(dp_count, step_count * CAP, head_part))
        delta = lax.all_to_all(delta, DP, split_axis=0, concat_axis=0, tiled=True)
        done["delta_cold"] = delta.reshape(cold_rows, head_part)

    between = {
        (1, "end"): [expand_pick, base_product],
        (2, "end"): [expand_over_core, cold_shrink],
        (3, "end"): [base_over_tp, cold_over_tp],
        (4, "x"): [hot_tokens_out],
        (4, "end"): [cold_expand],
        (5, "end"): [cold_back],
    }
    for slot in range(1, chunk_count + 1 + len(hops) - 1):
        c = slot
        if c < chunk_count:
            mine.append(after(mine_all, got[c - 1, 0])[c * part:(c + 1) * part])
            swapped.append(after(rest, got[c - 1, 0])[(c - 1) * part:c * part])
        elif c == chunk_count:
            mine.append(done["expand_mine"])
            swapped.append(done["expand_swapped"])
        for stage in range(len(hops)):
            if 0 <= slot - stage <= chunk_count:
                send(slot - stage, stage)
            if stage == 0:
                for work in between.get((slot, "x"), []):
                    work()
        for work in between.get((slot, "end"), []):
            work()
    *shrink_hot, expand_hot = [(held[c], got[c, len(hops) - 1]) for c in range(chunk_count + 1)]
    expand_hot = expand_hot[0] + expand_hot[1]
    hot_in, delta_cold = done["hot_in"], done["delta_cold"]
    base_kept, base_got = done["base"]

    dense = None
    for c, pieces in enumerate(shrink_hot):
        for piece in pieces:
            product = matmul(hot_in[:, c * part:(c + 1) * part], piece)
            dense = product if dense is None else dense + product
    dense = dense.reshape(group_count, near, HCAP, kept)
    at_step = jnp.arange(kept) // R
    z_part = sum(jnp.where(at_step == i, dense[:, i], 0.0) for i in range(near))
    z_part = after(z_part.reshape(group_count * HCAP, kept), delta_cold, base_got)
    z_hot = sum_over_tp(z_part).astype(jnp.bfloat16).reshape(group_count, 1, HCAP, kept)
    same_step = jnp.arange(near)[:, None, None] == at_step
    spread = jnp.where(same_step, z_hot, jnp.zeros((), jnp.bfloat16)).reshape(hot_rows, kept)
    delta_hot = narrow(spread, expand_hot).reshape(group_count, near * HCAP, head_part)
    delta_hot = lax.all_to_all(delta_hot, GROUP, split_axis=0, concat_axis=0, tiled=True)

    delta = lax.dot_general(
        jnp.concatenate([place_hot, place_cold], axis=0),
        jnp.concatenate([delta_hot.reshape(hot_rows, head_part), delta_cold], axis=0),
        (((0,), (0,)), ((), ())),
        preferred_element_type=jnp.float32,
    )
    return (base_kept + base_got + delta).astype(jnp.bfloat16).reshape(step_count, token_count, head_part)


def solution(mesh):
    tp_count, dp_count = mesh.shape["tp"], mesh.shape["dp"]
    fine = Mesh(mesh.devices.reshape(tp_count, dp_count // 8, 2, 2, 2), ("tp", *DP))
    placed = (
        P(None, DP, "tp"),
        P("tp", None),
        P("tp", DP),
        P(DP, "tp"),
        P(),
        P(None, DP),
        P(),
    )
    return jax.shard_map(
        on_device, mesh=fine, in_specs=placed, out_specs=P(None, DP, "tp"), check_vma=False
    )
```

```python
import jax
import jax.numpy as jnp
from jax import lax
from jax.experimental import pallas as pl
from jax.experimental.pallas import tpu as pltpu
from jax.sharding import Mesh, PartitionSpec as P

R = 64
CAP = 2
HCAP = 16
TAG = 128
DP = ("z_high", "z_low", "x", "core")
GROUP = ("z_low", "x", "core")
SWAP = [(0, 1), (1, 0)]


def pick(flags):
    return flags.astype(jnp.bfloat16)


def matmul(a, b):
    return jnp.dot(a, b, preferred_element_type=jnp.float32)


def narrow(a, b):
    return matmul(a, b).astype(jnp.bfloat16)


def sum_over_tp(part):
    if lax.axis_size("tp") == 2:
        return part + lax.ppermute(part, "tp", SWAP)
    return lax.psum(part, "tp")


def after(value, *others):
    return lax.optimization_barrier((value, *others))[0]


class Chain:
    def __init__(self):
        self.last = None

    def hold(self, value):
        self.last = value if self.last is None else after(value, self.last)
        return self.last

    def permute(self, value, axis, pairs):
        return lax.ppermute(self.hold(value), axis, pairs)

    def wait(self, *arrived):
        self.last = after(self.last, *arrived)


def kernel_params():
    return dict(
        compiler_params=pltpu.CompilerParams(vmem_limit_bytes=40 * 2**20),
        cost_estimate=pl.CostEstimate(flops=1, bytes_accessed=1, transcendentals=0),
    )


def pick_columns(store, want_mine, want_other):
    depth, width = store.shape
    count = want_mine.shape[0]
    blocks = 8
    rows = depth // blocks

    def kernel(mine_at, other_at, store_ref, mine_ref, first_ref, rest_ref, pick_mine, pick_other):
        step = pl.program_id(0)

        @pl.when(step == 0)
        def _():
            column = lax.broadcasted_iota(jnp.int32, (width, count), 0)
            pick_mine[...] = (column == mine_at[...]).astype(jnp.float32).astype(jnp.bfloat16)
            pick_other[...] = (column == other_at[...]).astype(jnp.float32).astype(jnp.bfloat16)

        block = store_ref[...]
        other = narrow(block, pick_other[...])

        @pl.when(step < blocks // 4)
        def _():
            first_ref[...] = other

        @pl.when(step >= blocks // 4)
        def _():
            rest_ref[...] = other

        mine_ref[...] = narrow(block, pick_mine[...])

    out = lambda part: jax.ShapeDtypeStruct((depth * part // 4, count), jnp.bfloat16)
    index = pl.BlockSpec((1, count), lambda i: (0, 0))
    return pl.pallas_call(
        kernel,
        grid=(blocks,),
        in_specs=[index, index, pl.BlockSpec((rows, width), lambda i: (i, 0))],
        out_specs=[
            pl.BlockSpec((rows, count), lambda i: (i, 0)),
            pl.BlockSpec((rows, count), lambda i: (jnp.minimum(i, blocks // 4 - 1), 0)),
            pl.BlockSpec((rows, count), lambda i: (jnp.maximum(i - blocks // 4, 0), 0)),
        ],
        out_shape=[out(4), out(1), out(3)],
        scratch_shapes=[pltpu.VMEM((width, count), jnp.bfloat16)] * 2,
        **kernel_params(),
    )(want_mine[None], want_other[None], store)


def place_rows(rows, hot_target, cold_target, tag, hot_rows, cold_rows):
    count, depth = rows.shape
    blocks = 4
    width = depth // blocks

    def kernel(hot_at, cold_at, tag_at, rows_ref, hot_ref, cold_ref, place_hot, place_cold):
        step = pl.program_id(0)

        @pl.when(step == 0)
        def _():
            hot_hit = lax.broadcasted_iota(jnp.int32, (hot_rows, count), 0) == hot_at[...]
            cold_hit = lax.broadcasted_iota(jnp.int32, (cold_rows, count), 0) == cold_at[...]
            place_hot[...] = hot_hit.astype(jnp.float32).astype(jnp.bfloat16)
            place_cold[...] = cold_hit.astype(jnp.float32).astype(jnp.bfloat16)
            tags = jnp.sum(jnp.where(cold_hit, tag_at[...].astype(jnp.float32), 0.0), axis=1, keepdims=True)
            cold_ref[:, depth:] = jnp.broadcast_to(tags, (cold_rows, TAG)).astype(jnp.bfloat16)

        block = rows_ref[...]
        hot_ref[...] = narrow(place_hot[...], block)
        cold_ref[:, pl.ds(pl.multiple_of(step * width, 128), width)] = narrow(place_cold[...], block)

    index = pl.BlockSpec((1, count), lambda j: (0, 0))
    return pl.pallas_call(
        kernel,
        grid=(blocks,),
        in_specs=[index, index, index, pl.BlockSpec((count, width), lambda j: (0, j))],
        out_specs=[
            pl.BlockSpec((hot_rows, width), lambda j: (0, j)),
            pl.BlockSpec((cold_rows, depth + TAG), lambda j: (0, 0)),
        ],
        out_shape=[
            jax.ShapeDtypeStruct((hot_rows, depth), jnp.bfloat16),
            jax.ShapeDtypeStruct((cold_rows, depth + TAG), jnp.bfloat16),
        ],
        scratch_shapes=[pltpu.VMEM((hot_rows, count), jnp.bfloat16), pltpu.VMEM((cold_rows, count), jnp.bfloat16)],
        **kernel_params(),
    )(hot_target[None], cold_target[None], tag[None], rows)


def base_halves(rows, weight):
    count, depth = rows.shape
    width = weight.shape[1]
    half = width // 2
    blocks = 8
    part = depth // blocks

    def kernel(tp_at, rows_ref, weight_ref, own_ref, other_ref, total):
        step = pl.program_id(0)
        product = matmul(rows_ref[...], weight_ref[...])

        @pl.when(step == 0)
        def _():
            total[...] = product

        @pl.when(step > 0)
        def _():
            total[...] += product

        @pl.when(step == blocks - 1)
        def _():
            first = pl.multiple_of(tp_at[0] * half, 128)
            second = pl.multiple_of((1 - tp_at[0]) * half, 128)
            own_ref[...] = total[:, pl.ds(first, half)]
            other_ref[...] = total[:, pl.ds(second, half)]

    out = pl.BlockSpec((count, half), lambda k, at: (0, 0))
    return pl.pallas_call(
        kernel,
        grid_spec=pltpu.PrefetchScalarGridSpec(
            num_scalar_prefetch=1,
            grid=(blocks,),
            in_specs=[
                pl.BlockSpec((count, part), lambda k, at: (0, k)),
                pl.BlockSpec((part, width), lambda k, at: (k, 0)),
            ],
            out_specs=[out, out],
            scratch_shapes=[pltpu.VMEM((count, width), jnp.float32)],
        ),
        out_shape=[jax.ShapeDtypeStruct((count, half), jnp.float32)] * 2,
        **kernel_params(),
    )(lax.axis_index("tp").astype(jnp.int32)[None], rows, weight)


def hot_shrink(blocks, factors, before=None):
    near = factors[0][1][0].shape[1] // R
    served, kept = blocks[0].shape[0], near * R
    count = len(blocks)
    pieces = [piece for _, pair in factors for piece in pair]

    def kernel(*refs):
        *in_refs, out_ref = refs
        rows = in_refs[:count]
        piece_refs = in_refs[count:count + len(pieces)]
        total = in_refs[-1][...] if before is not None else None
        for n, (first, pair) in enumerate(factors):
            depth = pair[0].shape[0]
            factor = piece_refs[2 * n][...] + piece_refs[2 * n + 1][...]
            block = jnp.concatenate([row[:, first:first + depth] for row in rows], axis=0)
            product = matmul(block, factor)
            total = product if total is None else total + product
        if before is None:
            out_ref[...] = total
            return
        total = total.reshape(count, near, HCAP, kept)
        at_step = lax.broadcasted_iota(jnp.int32, (count, HCAP, kept), 2) // R
        z = sum(jnp.where(at_step == i, total[:, i], 0.0) for i in range(near))
        out_ref[...] = z.reshape(count * HCAP, kept)

    out_rows = count * (served if before is None else HCAP)
    return pl.pallas_call(
        kernel,
        out_shape=jax.ShapeDtypeStruct((out_rows, kept), jnp.float32),
        **kernel_params(),
    )(*blocks, *pieces, *(() if before is None else (before,)))


def hot_expand(z_own, z_got, expand):
    kept, head = expand[0].shape
    near = kept // R
    count = z_own.shape[0] // HCAP

    def kernel(own_ref, got_ref, first_ref, second_ref, *out_refs):
        z = (own_ref[...] + got_ref[...]).astype(jnp.bfloat16).astype(jnp.float32).reshape(count, 1, HCAP, kept)
        shape = (count, near, HCAP, kept)
        same = lax.broadcasted_iota(jnp.int32, shape, 3) // R == lax.broadcasted_iota(jnp.int32, shape, 1)
        spread = jnp.where(same, jnp.broadcast_to(z, shape), 0.0).astype(jnp.bfloat16)
        factor = first_ref[...] + second_ref[...]
        delta = narrow(spread.reshape(count * near * HCAP, kept), factor)
        for k, out_ref in enumerate(out_refs):
            out_ref[...] = delta[k * near * HCAP:(k + 1) * near * HCAP]

    return pl.pallas_call(
        kernel,
        out_shape=[jax.ShapeDtypeStruct((near * HCAP, head), jnp.bfloat16)] * count,
        **kernel_params(),
    )(z_own, z_got, *expand)


def add_hot(partial, target, blocks):
    count = partial.shape[0]
    hot_rows = len(blocks) * blocks[0].shape[0]

    def kernel(partial_ref, target_ref, *refs):
        *block_refs, out_ref = refs
        hit = lax.broadcasted_iota(jnp.int32, (count, hot_rows), 1) == target_ref[...]
        place = hit.astype(jnp.float32).astype(jnp.bfloat16)
        delta = matmul(place, jnp.concatenate([ref[...] for ref in block_refs], axis=0))
        out_ref[...] = (partial_ref[...] + delta).astype(jnp.bfloat16)

    return pl.pallas_call(
        kernel,
        out_shape=jax.ShapeDtypeStruct(partial.shape, jnp.bfloat16),
        **kernel_params(),
    )(partial, target[:, None], *blocks)


def on_device(
    activations, value_weight, shrink_store, expand_store, adapter_row, token_adapter, hot_ids
):
    step_count, token_count, depth = activations.shape
    adapter_count = adapter_row.shape[0]
    hot_count = hot_ids.shape[1]
    per_dev = expand_store.shape[0] // R
    head_part = expand_store.shape[1]
    far_count = lax.axis_size("z_high")
    group_count = 8
    dp_count = far_count * group_count
    me = lax.axis_index(DP)
    group_at = lax.axis_index(GROUP)
    z_at, x_at, core_at = lax.axis_index("z_low"), lax.axis_index("x"), lax.axis_index("core")
    none_code = adapter_count + hot_count
    rows = activations.reshape(step_count * token_count, depth)

    names = jnp.arange(adapter_count, dtype=jnp.int32)
    hot_row = jnp.sum(jnp.where(hot_ids[:, :, None] == names, adapter_row, 0), axis=-1)
    hot_first = jnp.where(hot_row // per_dev == me, (hot_row % per_dev) * R, -R * per_dev)
    column = jnp.arange(per_dev * R, dtype=jnp.int32)
    lane = jnp.arange(R, dtype=jnp.int32)
    entry = jnp.arange(hot_count, dtype=jnp.int32)
    near = step_count // 2

    def wanted(core):
        firsts = []
        for x in (x_at, 1 - x_at):
            of_steps = jnp.sum(jnp.where(entry == 2 * x + core, hot_first, 0), axis=1)
            firsts += [jnp.where(z_at == 0, of_steps[:near], of_steps[near:])]
            firsts += [jnp.where(z_at == 0, of_steps[near:], of_steps[:near])]
        return jnp.concatenate([(f[:, None] + lane).reshape(-1) for f in firsts])

    want_mine, want_other = wanted(core_at), wanted(1 - core_at)
    kept = near * R
    chunk_count = 4
    part = depth // chunk_count

    chain = Chain()
    hops = [("x", SWAP), ("z_low", SWAP)]
    bit = 1
    while bit < far_count:
        hops.append(("z_high", [(i, i ^ bit) for i in range(far_count)]))
        bit *= 2

    def cut(block, c, first, last):
        return block[:, first * kept:last * kept] if c > 0 else block[first * kept:last * kept]

    mine, swapped, got, held = {}, {}, {}, {}

    def operand(c, stage):
        if stage == 0:
            return cut(mine[c], c, 2, 4) + cut(swapped[c], c, 2, 4)
        if stage == 1:
            return cut(mine[c], c, 1, 2) + cut(swapped[c], c, 1, 2) + cut(got[c, 0], c, 1, 2)
        if stage == 2:
            held[c] = cut(mine[c], c, 0, 1) + cut(swapped[c], c, 0, 1) + cut(got[c, 0], c, 0, 1) + got[c, 1]
        else:
            held[c] = held[c] + got[c, stage - 1]
        return held[c]

    def send(c, stage, value=None):
        value = operand(c, stage) if value is None else value
        if c > 0:
            value = after(value, got[c - 1, stage])
        got[c, stage] = chain.permute(value, *hops[stage])

    swapped[0] = chain.permute(narrow(pick(want_other[:, None] == column), expand_store), "core", SWAP)
    mine[0] = narrow(pick(want_mine[:, None] == column), expand_store)
    mine_all, other_first, other_rest = pick_columns(after(shrink_store, chain.last), want_mine, want_other)
    send(0, 0)
    first_swapped = chain.permute(other_first, "core", SWAP)
    rest_swapped = chain.permute(other_rest, "core", SWAP)
    mine[1], swapped[1] = mine_all[:part], first_swapped

    token_adapter = after(token_adapter, chain.last)
    cold_row = jnp.sum(jnp.where((token_adapter - hot_count)[:, :, None] == names, adapter_row, 0), axis=-1)
    is_hot = token_adapter < hot_count
    is_cold = (token_adapter < none_code) & jnp.logical_not(is_hot)
    owner = cold_row // per_dev
    group = jnp.where(is_hot, token_adapter, jnp.where(is_cold, hot_count + owner, -1))
    at = jnp.arange(token_count, dtype=jnp.int32)
    before = (group[:, :, None] == group[:, None, :]) & (at[None, :] < at[:, None])
    rank = jnp.sum(before.astype(jnp.int32), axis=-1)
    step_at = jnp.arange(step_count, dtype=jnp.int32)[:, None]
    hot_rows = hot_count * step_count * HCAP
    cold_rows = dp_count * step_count * CAP
    server = ((step_at // near) * hot_count + token_adapter) ^ group_at
    hot_target = (server * near + step_at % near) * HCAP + rank
    cold_target = (owner * step_count + step_at) * CAP + rank
    hot_target = jnp.where(is_hot, hot_target, -1).reshape(-1)
    cold_target = jnp.where(is_cold, cold_target, -1).reshape(-1)
    hot_out, packet = place_rows(
        rows, hot_target, cold_target, (cold_row % per_dev + 1).reshape(-1), hot_rows, cold_rows
    )
    served = near * HCAP

    done = {}

    def cold_tokens_out():
        sent = chain.hold(packet.reshape(dp_count, step_count * CAP, depth + TAG))
        sent = lax.all_to_all(sent, DP, split_axis=0, concat_axis=0, tiled=True)
        done["packet"] = sent.reshape(cold_rows, depth + TAG)

    hot_in = [hot_out[:served]] + [None] * (group_count - 1)

    def hot_tokens_out(*blocks):
        def work():
            for k in blocks:
                pairs = [(i, i ^ k) for i in range(group_count)]
                hot_in[k] = chain.permute(hot_out[k * served:(k + 1) * served], GROUP, pairs)
        return work

    def base_product():
        if lax.axis_size("tp") == 2:
            done["base"] = base_halves(rows, after(value_weight, chain.last))
        else:
            done["base"] = matmul(rows, after(value_weight, chain.last)), None

    def hot_tokens_in(*blocks):
        return lambda: chain.wait(*[hot_in[k] for k in blocks])

    def base_over_tp():
        own, other = done["base"]
        if other is None:
            done["base"] = lax.psum_scatter(chain.hold(own), "tp", scatter_dimension=1, tiled=True)
            done["base_got"] = done["base"]
        else:
            done["base_got"] = chain.permute(other, "tp", SWAP)
            done["base"] = own + done["base_got"]

    def cold_shrink():
        tag_in = done["packet"][:, depth:depth + 1].astype(jnp.int32)
        chosen = (column // R + 1)[None, :] == tag_in
        product = matmul(done["packet"][:, :depth], after(shrink_store, chain.last))
        done["z_part"] = jnp.where(chosen, product, 0.0)

    def cold_over_tp():
        done["z_cold"] = sum_over_tp(chain.hold(done["z_part"]))

    def cold_expand():
        done["delta"] = narrow(done["z_cold"].astype(jnp.bfloat16), after(expand_store, chain.last))

    def cold_back():
        delta = chain.hold(done["delta"].reshape(dp_count, step_count * CAP, head_part))
        delta = lax.all_to_all(delta, DP, split_axis=0, concat_axis=0, tiled=True)
        done["delta_cold"] = delta.reshape(cold_rows, head_part)

    between = {
        (1, "x"): [cold_tokens_out],
        (2, "end"): [hot_tokens_out(1, 4), base_product],
        (3, "end"): [hot_tokens_out(5), cold_shrink],
        (4, "x"): [hot_tokens_out(2, 3), base_over_tp],
        (4, "end"): [hot_tokens_in(1, 4), cold_over_tp],
        (5, "x"): [hot_tokens_out(6, 7)],
        (5, "end"): [hot_tokens_in(5, 2, 3), cold_expand],
        (6, "x"): [cold_back],
    }
    ready = operand(1, 0)
    for slot in range(1, chunk_count + 1 + len(hops) - 1):
        for stage in range(len(hops)):
            c = slot - stage
            if 0 <= c <= chunk_count:
                send(c, stage, ready if stage == 0 else None)
                if stage == 0 and c < chunk_count:
                    mine[c + 1] = after(mine_all, chain.last)[c * part:(c + 1) * part]
                    swapped[c + 1] = after(rest_swapped, chain.last)[(c - 1) * part:c * part]
                    ready = chain.hold(operand(c + 1, 0))
            if stage == 0:
                for work in between.get((slot, "x"), []):
                    work()
        for work in between.get((slot, "end"), []):
            work()
    chain.wait(hot_in[6], hot_in[7], done["base_got"])
    expand_hot, *shrink_hot = [(held[c], got[c, len(hops) - 1]) for c in range(chunk_count + 1)]
    shrink_hot = [(c * part, pair) for c, pair in enumerate(shrink_hot)]

    place_cold = pick(jnp.arange(cold_rows, dtype=jnp.int32)[:, None] == cold_target)
    partial = done["base"] + lax.dot_general(
        place_cold, done["delta_cold"], (((0,), (0,)), ((), ())), preferred_element_type=jnp.float32
    )

    dense = hot_shrink(hot_in, shrink_hot[:-1])
    z_part = hot_shrink(hot_in, shrink_hot[-1:], dense)
    z_part, partial = lax.optimization_barrier((z_part, partial))
    if lax.axis_size("tp") == 2:
        z_got = lax.ppermute(z_part, "tp", SWAP)
    else:
        z_part = lax.psum(z_part, "tp")
        z_got = jnp.zeros_like(z_part)
    delta_hot = list(hot_expand(z_part, z_got, expand_hot))
    for k in range(1, group_count):
        delta_hot[k] = lax.ppermute(delta_hot[k], GROUP, [(i, i ^ k) for i in range(group_count)])
    added = add_hot(partial, hot_target, delta_hot)
    return added.reshape(step_count, token_count, head_part)


def solution(mesh):
    tp_count, dp_count = mesh.shape["tp"], mesh.shape["dp"]
    fine = Mesh(mesh.devices.reshape(tp_count, dp_count // 8, 2, 2, 2), ("tp", *DP))
    placed = (
        P(None, DP, "tp"),
        P("tp", None),
        P("tp", DP),
        P(DP, "tp"),
        P(),
        P(None, DP),
        P(),
    )
    return jax.shard_map(
        on_device, mesh=fine, in_specs=placed, out_specs=P(None, DP, "tp"), check_vma=False
    )
```

```python
import jax
import jax.numpy as jnp
from jax import lax
from jax.experimental import pallas as pl
from jax.experimental.pallas import tpu as pltpu
from jax.sharding import Mesh, PartitionSpec as P

R = 64
CAP = 2
HCAP = 16
TAG = 128
DP = ("z_high", "z_low", "x", "core")
GROUP = ("z_low", "x", "core")
SWAP = [(0, 1), (1, 0)]


def pick(flags):
    return flags.astype(jnp.bfloat16)


def matmul(a, b):
    return jnp.dot(a, b, preferred_element_type=jnp.float32)


def narrow(a, b):
    return matmul(a, b).astype(jnp.bfloat16)


def sum_over_tp(part):
    if lax.axis_size("tp") == 2:
        return part + lax.ppermute(part, "tp", SWAP)
    return lax.psum(part, "tp")


def after(value, *others):
    return lax.optimization_barrier((value, *others))[0]


class Chain:
    def __init__(self):
        self.last = None

    def hold(self, value):
        self.last = value if self.last is None else after(value, self.last)
        return self.last

    def permute(self, value, axis, pairs):
        return lax.ppermute(self.hold(value), axis, pairs)

    def wait(self, *arrived):
        self.last = after(self.last, *arrived)


def kernel_params():
    return dict(
        compiler_params=pltpu.CompilerParams(vmem_limit_bytes=40 * 2**20),
        cost_estimate=pl.CostEstimate(flops=1, bytes_accessed=1, transcendentals=0),
    )


def pick_columns(store, want_mine, want_other, first_blocks):
    depth, width = store.shape
    groups, lanes = want_mine.shape
    count = groups * lanes
    rows = depth // 8

    def kernel(mine_held, other_held, mine_at, other_at, store_ref, mine_ref, first_ref, rest_ref, pick_mine, pick_other):
        step = pl.program_id(0)

        @pl.when(step == 0)
        def _():
            column = lax.broadcasted_iota(jnp.int32, (width, count), 0)
            pick_mine[...] = (column == mine_at[...]).astype(jnp.float32).astype(jnp.bfloat16)
            pick_other[...] = (column == other_at[...]).astype(jnp.float32).astype(jnp.bfloat16)

        def fill(out_ref, held, picker):
            for g in range(groups):
                at = slice(g * lanes, (g + 1) * lanes)

                @pl.when(held[g] > 0)
                def _():
                    out_ref[:, at] = narrow(store_ref[...], picker[:, at])

                @pl.when(held[g] == 0)
                def _():
                    out_ref[:, at] = jnp.zeros((rows, lanes), jnp.bfloat16)

        fill(mine_ref, mine_held, pick_mine)

        @pl.when(step < first_blocks)
        def _():
            fill(first_ref, other_held, pick_other)

        @pl.when(step >= first_blocks)
        def _():
            fill(rest_ref, other_held, pick_other)

    out = lambda blocks: jax.ShapeDtypeStruct((rows * blocks, count), jnp.bfloat16)
    index = pl.BlockSpec((1, count), lambda i, *held: (0, 0))
    return pl.pallas_call(
        kernel,
        grid_spec=pltpu.PrefetchScalarGridSpec(
            num_scalar_prefetch=2,
            grid=(8,),
            in_specs=[index, index, pl.BlockSpec((rows, width), lambda i, *held: (i, 0))],
            out_specs=[
                pl.BlockSpec((rows, count), lambda i, *held: (i, 0)),
                pl.BlockSpec((rows, count), lambda i, *held: (jnp.minimum(i, first_blocks - 1), 0)),
                pl.BlockSpec((rows, count), lambda i, *held: (jnp.maximum(i - first_blocks, 0), 0)),
            ],
            scratch_shapes=[pltpu.VMEM((width, count), jnp.bfloat16)] * 2,
        ),
        out_shape=[out(8), out(first_blocks), out(8 - first_blocks)],
        **kernel_params(),
    )(
        jnp.any(want_mine >= 0, axis=1).astype(jnp.int32),
        jnp.any(want_other >= 0, axis=1).astype(jnp.int32),
        want_mine.reshape(1, -1),
        want_other.reshape(1, -1),
        store,
    )


def place_rows(rows, hot_target, cold_target, tag, hot_rows, cold_rows):
    count, depth = rows.shape
    blocks = 4
    width = depth // blocks

    def kernel(hot_at, cold_at, tag_at, rows_ref, hot_ref, cold_ref, place_hot, place_cold):
        step = pl.program_id(0)

        @pl.when(step == 0)
        def _():
            hot_hit = lax.broadcasted_iota(jnp.int32, (hot_rows, count), 0) == hot_at[...]
            cold_hit = lax.broadcasted_iota(jnp.int32, (cold_rows, count), 0) == cold_at[...]
            place_hot[...] = hot_hit.astype(jnp.float32).astype(jnp.bfloat16)
            place_cold[...] = cold_hit.astype(jnp.float32).astype(jnp.bfloat16)
            tags = jnp.sum(jnp.where(cold_hit, tag_at[...].astype(jnp.float32), 0.0), axis=1, keepdims=True)
            cold_ref[:, depth:] = jnp.broadcast_to(tags, (cold_rows, TAG)).astype(jnp.bfloat16)

        block = rows_ref[...]
        hot_ref[...] = narrow(place_hot[...], block)
        cold_ref[:, pl.ds(pl.multiple_of(step * width, 128), width)] = narrow(place_cold[...], block)

    index = pl.BlockSpec((1, count), lambda j: (0, 0))
    return pl.pallas_call(
        kernel,
        grid=(blocks,),
        in_specs=[index, index, index, pl.BlockSpec((count, width), lambda j: (0, j))],
        out_specs=[
            pl.BlockSpec((hot_rows, width), lambda j: (0, j)),
            pl.BlockSpec((cold_rows, depth + TAG), lambda j: (0, 0)),
        ],
        out_shape=[
            jax.ShapeDtypeStruct((hot_rows, depth), jnp.bfloat16),
            jax.ShapeDtypeStruct((cold_rows, depth + TAG), jnp.bfloat16),
        ],
        scratch_shapes=[pltpu.VMEM((hot_rows, count), jnp.bfloat16), pltpu.VMEM((cold_rows, count), jnp.bfloat16)],
        **kernel_params(),
    )(hot_target[None], cold_target[None], tag[None], rows)


def base_halves(rows, weight):
    count, depth = rows.shape
    width = weight.shape[1]
    half = width // 2
    blocks = 8
    part = depth // blocks

    def kernel(tp_at, rows_ref, weight_ref, own_ref, other_ref, total):
        step = pl.program_id(0)
        product = matmul(rows_ref[...], weight_ref[...])

        @pl.when(step == 0)
        def _():
            total[...] = product

        @pl.when(step > 0)
        def _():
            total[...] += product

        @pl.when(step == blocks - 1)
        def _():
            first = pl.multiple_of(tp_at[0] * half, 128)
            second = pl.multiple_of((1 - tp_at[0]) * half, 128)
            own_ref[...] = total[:, pl.ds(first, half)]
            other_ref[...] = total[:, pl.ds(second, half)]

    out = pl.BlockSpec((count, half), lambda k, at: (0, 0))
    return pl.pallas_call(
        kernel,
        grid_spec=pltpu.PrefetchScalarGridSpec(
            num_scalar_prefetch=1,
            grid=(blocks,),
            in_specs=[
                pl.BlockSpec((count, part), lambda k, at: (0, k)),
                pl.BlockSpec((part, width), lambda k, at: (k, 0)),
            ],
            out_specs=[out, out],
            scratch_shapes=[pltpu.VMEM((count, width), jnp.float32)],
        ),
        out_shape=[jax.ShapeDtypeStruct((count, half), jnp.float32)] * 2,
        **kernel_params(),
    )(lax.axis_index("tp").astype(jnp.int32)[None], rows, weight)


def hot_expand(z_own, z_got, expand):
    kept, head = expand.shape
    near = kept // R
    count = z_own.shape[0] // HCAP

    def kernel(own_ref, got_ref, expand_ref, *out_refs):
        z = (own_ref[...] + got_ref[...]).astype(jnp.bfloat16).astype(jnp.float32).reshape(count, 1, HCAP, kept)
        shape = (count, near, HCAP, kept)
        same = lax.broadcasted_iota(jnp.int32, shape, 3) // R == lax.broadcasted_iota(jnp.int32, shape, 1)
        spread = jnp.where(same, jnp.broadcast_to(z, shape), 0.0).astype(jnp.bfloat16)
        delta = narrow(spread.reshape(count * near * HCAP, kept), expand_ref[...])
        for k, out_ref in enumerate(out_refs):
            out_ref[...] = delta[k * near * HCAP:(k + 1) * near * HCAP]

    return pl.pallas_call(
        kernel,
        out_shape=[jax.ShapeDtypeStruct((near * HCAP, head), jnp.bfloat16)] * count,
        **kernel_params(),
    )(z_own, z_got, expand)


def add_hot(partial, target, blocks):
    count = partial.shape[0]
    hot_rows = len(blocks) * blocks[0].shape[0]

    def kernel(partial_ref, target_ref, *refs):
        *block_refs, out_ref = refs
        hit = lax.broadcasted_iota(jnp.int32, (count, hot_rows), 1) == target_ref[...]
        place = hit.astype(jnp.float32).astype(jnp.bfloat16)
        delta = matmul(place, jnp.concatenate([ref[...] for ref in block_refs], axis=0))
        out_ref[...] = (partial_ref[...] + delta).astype(jnp.bfloat16)

    return pl.pallas_call(
        kernel,
        out_shape=jax.ShapeDtypeStruct(partial.shape, jnp.bfloat16),
        **kernel_params(),
    )(partial, target[:, None], *blocks)


def on_device(
    activations, value_weight, shrink_store, expand_store, adapter_row, token_adapter, hot_ids
):
    step_count, token_count, depth = activations.shape
    adapter_count = adapter_row.shape[0]
    hot_count = hot_ids.shape[1]
    per_dev = expand_store.shape[0] // R
    head_part = expand_store.shape[1]
    far_count = lax.axis_size("z_high")
    group_count = 8
    dp_count = far_count * group_count
    me = lax.axis_index(DP)
    group_at = lax.axis_index(GROUP)
    z_at, x_at, core_at = lax.axis_index("z_low"), lax.axis_index("x"), lax.axis_index("core")
    none_code = adapter_count + hot_count
    rows = activations.reshape(step_count * token_count, depth)

    names = jnp.arange(adapter_count, dtype=jnp.int32)
    hot_row = jnp.sum(jnp.where(hot_ids[:, :, None] == names, adapter_row, 0), axis=-1)
    hot_first = jnp.where(hot_row // per_dev == me, (hot_row % per_dev) * R, -R * per_dev)
    column = jnp.arange(per_dev * R, dtype=jnp.int32)
    lane = jnp.arange(R, dtype=jnp.int32)
    entry = jnp.arange(hot_count, dtype=jnp.int32)
    near = step_count // 2

    def wanted(core):
        firsts = []
        for x in (x_at, 1 - x_at):
            of_steps = jnp.sum(jnp.where(entry == 2 * x + core, hot_first, 0), axis=1)
            firsts += [jnp.where(z_at == 0, of_steps[:near], of_steps[near:])]
            firsts += [jnp.where(z_at == 0, of_steps[near:], of_steps[:near])]
        return jnp.stack([(f[:, None] + lane).reshape(-1) for f in firsts])

    want_mine, want_other = wanted(core_at), wanted(1 - core_at)
    kept = near * R
    eighth = depth // 8
    edges = [0, 3 * eighth, 6 * eighth, depth]
    chunk_count = len(edges) - 1

    chain = Chain()
    hops = [("x", SWAP), ("z_low", SWAP)]
    bit = 1
    while bit < far_count:
        hops.append(("z_high", [(i, i ^ bit) for i in range(far_count)]))
        bit *= 2
    mine, swapped, got, held = {}, {}, {}, {}

    def operand(c, stage):
        if stage == 0:
            return mine[c][:, 2 * kept:] + swapped[c][:, 2 * kept:]
        if stage == 1:
            return mine[c][:, kept:2 * kept] + swapped[c][:, kept:2 * kept] + got[c, 0][:, kept:]
        if stage == 2:
            held[c] = mine[c][:, :kept] + swapped[c][:, :kept] + got[c, 0][:, :kept] + got[c, 1]
        else:
            held[c] = held[c] + got[c, stage - 1]
        return held[c]

    def send(c, stage, value=None):
        got[c, stage] = chain.permute(operand(c, stage) if value is None else value, *hops[stage])

    mine_all, other_first, other_rest = pick_columns(shrink_store, want_mine, want_other, 3)
    mine[0], swapped[0] = mine_all[:edges[1]], chain.permute(other_first, "core", SWAP)
    rest_swapped = chain.permute(other_rest, "core", SWAP)
    send(0, 0)

    by_server = hot_first.reshape(2, near, hot_count).transpose(0, 2, 1)
    by_server = (by_server[..., None] + lane).reshape(-1)
    expand_hot = narrow(pick(after(by_server, chain.last)[:, None] == column), expand_store)
    expand_part = lax.psum_scatter(expand_hot, GROUP, scatter_dimension=0, tiled=True)

    token_adapter = after(token_adapter, chain.last)
    cold_row = jnp.sum(jnp.where((token_adapter - hot_count)[:, :, None] == names, adapter_row, 0), axis=-1)
    is_hot = token_adapter < hot_count
    is_cold = (token_adapter < none_code) & jnp.logical_not(is_hot)
    owner = cold_row // per_dev
    group = jnp.where(is_hot, token_adapter, jnp.where(is_cold, hot_count + owner, -1))
    at = jnp.arange(token_count, dtype=jnp.int32)
    before = (group[:, :, None] == group[:, None, :]) & (at[None, :] < at[:, None])
    rank = jnp.sum(before.astype(jnp.int32), axis=-1)
    step_at = jnp.arange(step_count, dtype=jnp.int32)[:, None]
    hot_rows = hot_count * step_count * HCAP
    cold_rows = dp_count * step_count * CAP
    server = ((step_at // near) * hot_count + token_adapter) ^ group_at
    hot_target = (server * near + step_at % near) * HCAP + rank
    cold_target = (owner * step_count + step_at) * CAP + rank
    hot_target = jnp.where(is_hot, hot_target, -1).reshape(-1)
    cold_target = jnp.where(is_cold, cold_target, -1).reshape(-1)
    hot_out, packet = place_rows(
        rows, hot_target, cold_target, (cold_row % per_dev + 1).reshape(-1), hot_rows, cold_rows
    )
    served = near * HCAP

    done = {}

    def cold_tokens_out():
        sent = chain.hold(packet.reshape(dp_count, step_count * CAP, depth + TAG))
        sent = lax.all_to_all(sent, DP, split_axis=0, concat_axis=0, tiled=True)
        done["packet"] = sent.reshape(cold_rows, depth + TAG)

    done["hot_0"] = hot_out[:served]

    def hot_tokens_out(*blocks):
        def work():
            for k in blocks:
                pairs = [(i, i ^ k) for i in range(group_count)]
                done[f"hot_{k}"] = chain.permute(hot_out[k * served:(k + 1) * served], GROUP, pairs)
        return work

    def base_product():
        if lax.axis_size("tp") == 2:
            done["base"] = base_halves(rows, after(value_weight, chain.last))
        else:
            done["base"] = matmul(rows, after(value_weight, chain.last)), None

    def base_over_tp():
        own, other = done["base"]
        if other is None:
            done["base_own"] = None
            done["base_got"] = lax.psum_scatter(chain.hold(own), "tp", scatter_dimension=1, tiled=True)
        else:
            done["base_own"], done["base_got"] = own, chain.permute(other, "tp", SWAP)

    def expand_over_far():
        own = after(expand_part, chain.last)
        if far_count == 2:
            done["expand_own"], done["expand_got"] = own, chain.permute(own, "z_high", SWAP)
        else:
            done["expand_own"], done["expand_got"] = jnp.zeros_like(own), lax.psum(chain.hold(own), "z_high")

    def cold_shrink():
        tag_in = done["packet"][:, depth:depth + 1].astype(jnp.int32)
        chosen = (column // R + 1)[None, :] == tag_in
        product = matmul(done["packet"][:, :depth], after(shrink_store, chain.last))
        done["z_part"] = jnp.where(chosen, product, 0.0)

    def cold_over_tp():
        done["z_cold"] = sum_over_tp(chain.hold(done["z_part"]))

    def cold_expand():
        done["delta"] = narrow(done["z_cold"].astype(jnp.bfloat16), after(expand_store, chain.last))

    def cold_back():
        delta = chain.hold(done["delta"].reshape(dp_count, step_count * CAP, head_part))
        delta = lax.all_to_all(delta, DP, split_axis=0, concat_axis=0, tiled=True)
        done["delta_cold"] = delta.reshape(cold_rows, head_part)

    cold_tokens_out()
    base_product()
    between = {
        1: [hot_tokens_out(4, 5, 1)],
        2: [cold_shrink, cold_over_tp, base_over_tp],
        3: [hot_tokens_out(6, 7, 2, 3), expand_over_far, cold_expand, cold_back],
    }
    awaited = {
        1: ["packet", "hot_4", "hot_5", "hot_1"],
        2: ["z_cold"],
        3: ["hot_6", "hot_7", "hot_2", "hot_3", "expand_got", "base_got"],
        4: ["delta_cold"],
    }
    ready = None
    for slot in range(chunk_count + len(hops) - 1):
        if slot > 0:
            for stage in sorted(range(len(hops)), key=lambda stage: stage == 1):
                if 0 <= slot - stage < chunk_count:
                    send(slot - stage, stage, ready if stage == 0 else None)
        for work in between.get(slot, []):
            work()
        c = slot + 1
        if c < chunk_count:
            mine[c] = after(mine_all, chain.last)[edges[c]:edges[c + 1]]
            swapped[c] = after(rest_swapped, chain.last)[edges[c] - edges[1]:edges[c + 1] - edges[1]]
            ready = chain.hold(operand(c, 0))
        here = [(slot - stage, stage) for stage in range(len(hops)) if 0 <= slot - stage < chunk_count]
        names_here = awaited.get(slot, [])
        arrived = lax.optimization_barrier(
            (chain.last, *[got[at] for at in here], *[done[name] for name in names_here])
        )
        chain.last = arrived[0]
        got.update(zip(here, arrived[1:]))
        done.update(zip(names_here, arrived[1 + len(here):]))
    base = done["base_own"] + done["base_got"] if done["base_own"] is not None else done["base_got"]
    expand_hot = done["expand_own"] + done["expand_got"]

    place_cold = pick(jnp.arange(cold_rows, dtype=jnp.int32)[:, None] == cold_target)
    partial = base + lax.dot_general(
        place_cold, done["delta_cold"], (((0,), (0,)), ((), ())), preferred_element_type=jnp.float32
    )

    hot_in = jnp.concatenate([done[f"hot_{k}"] for k in range(group_count)], axis=0)
    dense = None
    for c in range(chunk_count):
        for piece in (held[c], got[c, len(hops) - 1]):
            product = matmul(hot_in[:, edges[c]:edges[c + 1]], piece)
            dense = product if dense is None else dense + product
    dense = dense.reshape(group_count, near, HCAP, kept)
    at_step = jnp.arange(kept) // R
    z_part = sum(jnp.where(at_step == i, dense[:, i], 0.0) for i in range(near)).reshape(group_count * HCAP, kept)
    z_part, partial = lax.optimization_barrier((z_part, partial))
    if lax.axis_size("tp") == 2:
        z_got = lax.ppermute(z_part, "tp", SWAP)
    else:
        z_part = lax.psum(z_part, "tp")
        z_got = jnp.zeros_like(z_part)
    delta_hot = list(hot_expand(z_part, z_got, expand_hot))
    for k in range(1, group_count):
        delta_hot[k] = lax.ppermute(delta_hot[k], GROUP, [(i, i ^ k) for i in range(group_count)])
    added = add_hot(partial, hot_target, delta_hot)
    return added.reshape(step_count, token_count, head_part)


def solution(mesh):
    tp_count, dp_count = mesh.shape["tp"], mesh.shape["dp"]
    fine = Mesh(mesh.devices.reshape(tp_count, dp_count // 8, 2, 2, 2), ("tp", *DP))
    placed = (
        P(None, DP, "tp"),
        P("tp", None),
        P("tp", DP),
        P(DP, "tp"),
        P(),
        P(None, DP),
        P(),
    )
    return jax.shard_map(
        on_device, mesh=fine, in_specs=placed, out_specs=P(None, DP, "tp"), check_vma=False
    )
```

```python
import jax
import jax.numpy as jnp
from jax import lax
from jax.experimental import pallas as pl
from jax.experimental.pallas import tpu as pltpu
from jax.sharding import Mesh, PartitionSpec as P

R = 64
CAP = 2
HCAP = 16
TAG = 128
DP = ("z_high", "z_low", "x", "core")
GROUP = ("z_low", "x", "core")
SWAP = [(0, 1), (1, 0)]


def pick(flags):
    return flags.astype(jnp.bfloat16)


def matmul(a, b):
    return jnp.dot(a, b, preferred_element_type=jnp.float32)


def narrow(a, b):
    return matmul(a, b).astype(jnp.bfloat16)


def sum_over_tp(part):
    if lax.axis_size("tp") == 2:
        return part + lax.ppermute(part, "tp", SWAP)
    return lax.psum(part, "tp")


def after(value, *others):
    return lax.optimization_barrier((value, *others))[0]


class Chain:
    def __init__(self):
        self.last = None

    def hold(self, value):
        self.last = value if self.last is None else after(value, self.last)
        return self.last

    def permute(self, value, axis, pairs):
        return lax.ppermute(self.hold(value), axis, pairs)

    def wait(self, *arrived):
        self.last = after(self.last, *arrived)


def kernel_params():
    return dict(
        compiler_params=pltpu.CompilerParams(vmem_limit_bytes=40 * 2**20),
        cost_estimate=pl.CostEstimate(flops=1, bytes_accessed=1, transcendentals=0),
    )


def pick_columns(store, want_mine, want_other, first_blocks):
    depth, width = store.shape
    groups, lanes = want_mine.shape
    count = groups * lanes
    rows = depth // 8

    def kernel(mine_held, other_held, mine_at, other_at, store_ref, mine_ref, first_ref, rest_ref, pick_mine, pick_other):
        step = pl.program_id(0)

        @pl.when(step == 0)
        def _():
            column = lax.broadcasted_iota(jnp.int32, (width, count), 0)
            pick_mine[...] = (column == mine_at[...]).astype(jnp.float32).astype(jnp.bfloat16)
            pick_other[...] = (column == other_at[...]).astype(jnp.float32).astype(jnp.bfloat16)

        def fill(out_ref, held, picker):
            for g in range(groups):
                at = slice(g * lanes, (g + 1) * lanes)

                @pl.when(held[g] > 0)
                def _():
                    out_ref[:, at] = narrow(store_ref[...], picker[:, at])

                @pl.when(held[g] == 0)
                def _():
                    out_ref[:, at] = jnp.zeros((rows, lanes), jnp.bfloat16)

        fill(mine_ref, mine_held, pick_mine)

        @pl.when(step < first_blocks)
        def _():
            fill(first_ref, other_held, pick_other)

        @pl.when(step >= first_blocks)
        def _():
            fill(rest_ref, other_held, pick_other)

    out = lambda blocks: jax.ShapeDtypeStruct((rows * blocks, count), jnp.bfloat16)
    index = pl.BlockSpec((1, count), lambda i, *held: (0, 0))
    return pl.pallas_call(
        kernel,
        grid_spec=pltpu.PrefetchScalarGridSpec(
            num_scalar_prefetch=2,
            grid=(8,),
            in_specs=[index, index, pl.BlockSpec((rows, width), lambda i, *held: (i, 0))],
            out_specs=[
                pl.BlockSpec((rows, count), lambda i, *held: (i, 0)),
                pl.BlockSpec((rows, count), lambda i, *held: (jnp.minimum(i, first_blocks - 1), 0)),
                pl.BlockSpec((rows, count), lambda i, *held: (jnp.maximum(i - first_blocks, 0), 0)),
            ],
            scratch_shapes=[pltpu.VMEM((width, count), jnp.bfloat16)] * 2,
        ),
        out_shape=[out(8), out(first_blocks), out(8 - first_blocks)],
        **kernel_params(),
    )(
        jnp.any(want_mine >= 0, axis=1).astype(jnp.int32),
        jnp.any(want_other >= 0, axis=1).astype(jnp.int32),
        want_mine.reshape(1, -1),
        want_other.reshape(1, -1),
        store,
    )


def place_rows(rows, hot_target, cold_target, tag, hot_rows, cold_rows):
    count, depth = rows.shape
    blocks = 4
    width = depth // blocks

    def kernel(hot_at, cold_at, tag_at, rows_ref, hot_ref, cold_ref, place_hot, place_cold):
        step = pl.program_id(0)

        @pl.when(step == 0)
        def _():
            hot_hit = lax.broadcasted_iota(jnp.int32, (hot_rows, count), 0) == hot_at[...]
            cold_hit = lax.broadcasted_iota(jnp.int32, (cold_rows, count), 0) == cold_at[...]
            place_hot[...] = hot_hit.astype(jnp.float32).astype(jnp.bfloat16)
            place_cold[...] = cold_hit.astype(jnp.float32).astype(jnp.bfloat16)
            tags = jnp.sum(jnp.where(cold_hit, tag_at[...].astype(jnp.float32), 0.0), axis=1, keepdims=True)
            cold_ref[:, depth:] = jnp.broadcast_to(tags, (cold_rows, TAG)).astype(jnp.bfloat16)

        block = rows_ref[...]
        hot_ref[...] = narrow(place_hot[...], block)
        cold_ref[:, pl.ds(pl.multiple_of(step * width, 128), width)] = narrow(place_cold[...], block)

    index = pl.BlockSpec((1, count), lambda j: (0, 0))
    return pl.pallas_call(
        kernel,
        grid=(blocks,),
        in_specs=[index, index, index, pl.BlockSpec((count, width), lambda j: (0, j))],
        out_specs=[
            pl.BlockSpec((hot_rows, width), lambda j: (0, j)),
            pl.BlockSpec((cold_rows, depth + TAG), lambda j: (0, 0)),
        ],
        out_shape=[
            jax.ShapeDtypeStruct((hot_rows, depth), jnp.bfloat16),
            jax.ShapeDtypeStruct((cold_rows, depth + TAG), jnp.bfloat16),
        ],
        scratch_shapes=[pltpu.VMEM((hot_rows, count), jnp.bfloat16), pltpu.VMEM((cold_rows, count), jnp.bfloat16)],
        **kernel_params(),
    )(hot_target[None], cold_target[None], tag[None], rows)


def base_halves(rows, weight):
    count, depth = rows.shape
    width = weight.shape[1]
    half = width // 2
    blocks = 8
    part = depth // blocks

    def kernel(tp_at, rows_ref, weight_ref, own_ref, other_ref, total):
        step = pl.program_id(0)
        product = matmul(rows_ref[...], weight_ref[...])

        @pl.when(step == 0)
        def _():
            total[...] = product

        @pl.when(step > 0)
        def _():
            total[...] += product

        @pl.when(step == blocks - 1)
        def _():
            first = pl.multiple_of(tp_at[0] * half, 128)
            second = pl.multiple_of((1 - tp_at[0]) * half, 128)
            own_ref[...] = total[:, pl.ds(first, half)]
            other_ref[...] = total[:, pl.ds(second, half)]

    out = pl.BlockSpec((count, half), lambda k, at: (0, 0))
    return pl.pallas_call(
        kernel,
        grid_spec=pltpu.PrefetchScalarGridSpec(
            num_scalar_prefetch=1,
            grid=(blocks,),
            in_specs=[
                pl.BlockSpec((count, part), lambda k, at: (0, k)),
                pl.BlockSpec((part, width), lambda k, at: (k, 0)),
            ],
            out_specs=[out, out],
            scratch_shapes=[pltpu.VMEM((count, width), jnp.float32)],
        ),
        out_shape=[jax.ShapeDtypeStruct((count, half), jnp.float32)] * 2,
        **kernel_params(),
    )(lax.axis_index("tp").astype(jnp.int32)[None], rows, weight)


def hot_expand(z_own, z_got, expand):
    kept, head = expand.shape
    near = kept // R
    count = z_own.shape[0] // HCAP

    def kernel(own_ref, got_ref, expand_ref, out_ref):
        z = (own_ref[...] + got_ref[...]).astype(jnp.bfloat16).astype(jnp.float32).reshape(count, 1, HCAP, kept)
        shape = (count, near, HCAP, kept)
        same = lax.broadcasted_iota(jnp.int32, shape, 3) // R == lax.broadcasted_iota(jnp.int32, shape, 1)
        spread = jnp.where(same, jnp.broadcast_to(z, shape), 0.0).astype(jnp.bfloat16)
        out_ref[...] = narrow(spread.reshape(count * near * HCAP, kept), expand_ref[...])

    return pl.pallas_call(
        kernel,
        out_shape=jax.ShapeDtypeStruct((count * near * HCAP, head), jnp.bfloat16),
        **kernel_params(),
    )(z_own, z_got, expand)


def add_hot(partial, target, delta):
    count = partial.shape[0]
    hot_rows = delta.shape[0]

    def kernel(partial_ref, target_ref, delta_ref, out_ref):
        hit = lax.broadcasted_iota(jnp.int32, (count, hot_rows), 1) == target_ref[...]
        place = hit.astype(jnp.float32).astype(jnp.bfloat16)
        out_ref[...] = (partial_ref[...] + matmul(place, delta_ref[...])).astype(jnp.bfloat16)

    return pl.pallas_call(
        kernel,
        out_shape=jax.ShapeDtypeStruct(partial.shape, jnp.bfloat16),
        **kernel_params(),
    )(partial, target[:, None], delta)


def on_device(
    activations, value_weight, shrink_store, expand_store, adapter_row, token_adapter, hot_ids
):
    step_count, token_count, depth = activations.shape
    adapter_count = adapter_row.shape[0]
    hot_count = hot_ids.shape[1]
    per_dev = expand_store.shape[0] // R
    head_part = expand_store.shape[1]
    far_count = lax.axis_size("z_high")
    group_count = 8
    dp_count = far_count * group_count
    me = lax.axis_index(DP)
    z_at, x_at, core_at = lax.axis_index("z_low"), lax.axis_index("x"), lax.axis_index("core")
    none_code = adapter_count + hot_count
    rows = activations.reshape(step_count * token_count, depth)

    near = step_count // 2
    names = jnp.arange(adapter_count, dtype=jnp.int32)
    cold_row = jnp.sum(jnp.where((token_adapter - hot_count)[:, :, None] == names, adapter_row, 0), axis=-1)
    is_hot = token_adapter < hot_count
    is_cold = (token_adapter < none_code) & jnp.logical_not(is_hot)
    owner = cold_row // per_dev
    group = jnp.where(is_hot, token_adapter, jnp.where(is_cold, hot_count + owner, -1))
    at = jnp.arange(token_count, dtype=jnp.int32)
    before = (group[:, :, None] == group[:, None, :]) & (at[None, :] < at[:, None])
    rank = jnp.sum(before.astype(jnp.int32), axis=-1)
    step_at = jnp.arange(step_count, dtype=jnp.int32)[:, None]
    hot_rows = hot_count * step_count * HCAP
    cold_rows = dp_count * step_count * CAP
    server = (step_at // near) * hot_count + token_adapter
    hot_target = (server * near + step_at % near) * HCAP + rank
    cold_target = (owner * step_count + step_at) * CAP + rank
    hot_target = jnp.where(is_hot, hot_target, -1).reshape(-1)
    cold_target = jnp.where(is_cold, cold_target, -1).reshape(-1)
    hot_out, packet = place_rows(
        rows, hot_target, cold_target, (cold_row % per_dev + 1).reshape(-1), hot_rows, cold_rows
    )
    chain = Chain()
    hot_in = lax.all_to_all(
        chain.hold(hot_out.reshape(group_count, near * HCAP, depth)), GROUP, split_axis=0, concat_axis=0, tiled=True
    )

    hot_row = jnp.sum(jnp.where(hot_ids[:, :, None] == names, adapter_row, 0), axis=-1)
    hot_first = jnp.where(hot_row // per_dev == me, (hot_row % per_dev) * R, -R * per_dev)
    column = jnp.arange(per_dev * R, dtype=jnp.int32)
    lane = jnp.arange(R, dtype=jnp.int32)
    entry = jnp.arange(hot_count, dtype=jnp.int32)

    def wanted(core):
        firsts = []
        for x in (x_at, 1 - x_at):
            of_steps = jnp.sum(jnp.where(entry == 2 * x + core, hot_first, 0), axis=1)
            firsts += [jnp.where(z_at == 0, of_steps[:near], of_steps[near:])]
            firsts += [jnp.where(z_at == 0, of_steps[near:], of_steps[:near])]
        return jnp.stack([(f[:, None] + lane).reshape(-1) for f in firsts])

    want_mine, want_other = wanted(core_at), wanted(1 - core_at)
    kept = near * R
    eighth = depth // 8
    edges = [0, 3 * eighth, 6 * eighth, depth]
    chunk_count = len(edges) - 1

    hops = [("x", SWAP), ("z_low", SWAP)]
    bit = 1
    while bit < far_count:
        hops.append(("z_high", [(i, i ^ bit) for i in range(far_count)]))
        bit *= 2
    mine, swapped, got, held = {}, {}, {}, {}

    def operand(c, stage):
        if stage == 0:
            return mine[c][:, 2 * kept:] + swapped[c][:, 2 * kept:]
        if stage == 1:
            return mine[c][:, kept:2 * kept] + swapped[c][:, kept:2 * kept] + got[c, 0][:, kept:]
        if stage == 2:
            held[c] = mine[c][:, :kept] + swapped[c][:, :kept] + got[c, 0][:, :kept] + got[c, 1]
        else:
            held[c] = held[c] + got[c, stage - 1]
        return held[c]

    def send(c, stage, value=None):
        got[c, stage] = chain.permute(operand(c, stage) if value is None else value, *hops[stage])

    mine_all, other_first, other_rest = pick_columns(after(shrink_store, chain.last), want_mine, want_other, 3)
    mine[0], swapped[0] = mine_all[:edges[1]], chain.permute(other_first, "core", SWAP)
    rest_swapped = chain.permute(other_rest, "core", SWAP)
    chain.last, hot_in, swapped[0] = lax.optimization_barrier((chain.last, hot_in, swapped[0]))
    send(0, 0)

    by_server = hot_first.reshape(2, near, hot_count).transpose(0, 2, 1)
    by_server = (by_server[..., None] + lane).reshape(-1)
    expand_hot = narrow(pick(after(by_server, chain.last)[:, None] == column), expand_store)
    expand_part = lax.psum_scatter(expand_hot, GROUP, scatter_dimension=0, tiled=True)

    done = {}

    def cold_tokens_out():
        sent = chain.hold(packet.reshape(dp_count, step_count * CAP, depth + TAG))
        sent = lax.all_to_all(sent, DP, split_axis=0, concat_axis=0, tiled=True)
        done["packet"] = sent.reshape(cold_rows, depth + TAG)

    def base_product():
        if lax.axis_size("tp") == 2:
            done["base"] = base_halves(rows, after(value_weight, chain.last))
        else:
            done["base"] = matmul(rows, after(value_weight, chain.last)), None

    def base_over_tp():
        own, other = done["base"]
        if other is None:
            done["base_own"] = None
            done["base_got"] = lax.psum_scatter(chain.hold(own), "tp", scatter_dimension=1, tiled=True)
        else:
            done["base_own"], done["base_got"] = own, chain.permute(other, "tp", SWAP)

    def expand_over_far():
        own = after(expand_part, chain.last)
        if far_count == 2:
            done["expand_own"], done["expand_got"] = own, chain.permute(own, "z_high", SWAP)
        else:
            done["expand_own"], done["expand_got"] = jnp.zeros_like(own), lax.psum(chain.hold(own), "z_high")

    def cold_shrink():
        tag_in = done["packet"][:, depth:depth + 1].astype(jnp.int32)
        chosen = (column // R + 1)[None, :] == tag_in
        product = matmul(done["packet"][:, :depth], after(shrink_store, chain.last))
        done["z_part"] = jnp.where(chosen, product, 0.0)

    def cold_over_tp():
        done["z_cold"] = sum_over_tp(chain.hold(done["z_part"]))

    def cold_expand():
        done["delta"] = narrow(done["z_cold"].astype(jnp.bfloat16), after(expand_store, chain.last))

    def cold_back():
        delta = chain.hold(done["delta"].reshape(dp_count, step_count * CAP, head_part))
        delta = lax.all_to_all(delta, DP, split_axis=0, concat_axis=0, tiled=True)
        done["delta_cold"] = delta.reshape(cold_rows, head_part)

    cold_tokens_out()
    def all_but_hot():
        place_cold = pick(jnp.arange(cold_rows, dtype=jnp.int32)[:, None] == cold_target)
        partial = lax.dot_general(
            place_cold, done["delta_cold"], (((0,), (0,)), ((), ())), preferred_element_type=jnp.float32
        )
        if done["base_own"] is not None:
            partial = partial + done["base_own"]
        done["partial"] = partial + done["base_got"]

    between = {
        2: [cold_shrink, cold_over_tp, base_product],
        3: [base_over_tp, expand_over_far, cold_expand, cold_back],
        4: [all_but_hot],
    }
    awaited = {1: ["packet"], 2: ["z_cold"], 3: ["expand_got"], 4: ["partial"]}
    ready = None
    for slot in range(chunk_count + len(hops) - 1):
        if slot > 0:
            for stage in sorted(range(len(hops)), key=lambda stage: stage == 1):
                if 0 <= slot - stage < chunk_count:
                    send(slot - stage, stage, ready if stage == 0 else None)
        for work in between.get(slot, []):
            work()
        c = slot + 1
        if c < chunk_count:
            mine[c] = after(mine_all, chain.last)[edges[c]:edges[c + 1]]
            swapped[c] = after(rest_swapped, chain.last)[edges[c] - edges[1]:edges[c + 1] - edges[1]]
            ready = chain.hold(operand(c, 0))
        here = [(slot - stage, stage) for stage in range(len(hops)) if 0 <= slot - stage < chunk_count]
        names_here = awaited.get(slot, [])
        arrived = lax.optimization_barrier(
            (chain.last, *[got[at] for at in here], *[done[name] for name in names_here])
        )
        chain.last = arrived[0]
        got.update(zip(here, arrived[1:]))
        done.update(zip(names_here, arrived[1 + len(here):]))
    expand_hot = done["expand_own"] + done["expand_got"]
    partial = done["partial"]

    hot_in = hot_in.reshape(hot_rows, depth)
    dense = None
    for c in range(chunk_count):
        for piece in (held[c], got[c, len(hops) - 1]):
            product = matmul(hot_in[:, edges[c]:edges[c + 1]], piece)
            dense = product if dense is None else dense + product
    dense = dense.reshape(group_count, near, HCAP, kept)
    at_step = jnp.arange(kept) // R
    z_part = sum(jnp.where(at_step == i, dense[:, i], 0.0) for i in range(near)).reshape(group_count * HCAP, kept)
    if lax.axis_size("tp") == 2:
        z_got = lax.ppermute(z_part, "tp", SWAP)
    else:
        z_part = lax.psum(z_part, "tp")
        z_got = jnp.zeros_like(z_part)
    delta_hot = hot_expand(z_part, z_got, expand_hot).reshape(group_count, near * HCAP, head_part)
    delta_hot = lax.all_to_all(delta_hot, GROUP, split_axis=0, concat_axis=0, tiled=True)
    added = add_hot(partial, hot_target, delta_hot.reshape(hot_rows, head_part))
    return added.reshape(step_count, token_count, head_part)


def solution(mesh):
    tp_count, dp_count = mesh.shape["tp"], mesh.shape["dp"]
    fine = Mesh(mesh.devices.reshape(tp_count, dp_count // 8, 2, 2, 2), ("tp", *DP))
    placed = (
        P(None, DP, "tp"),
        P("tp", None),
        P("tp", DP),
        P(DP, "tp"),
        P(),
        P(None, DP),
        P(),
    )
    return jax.shard_map(
        on_device, mesh=fine, in_specs=placed, out_specs=P(None, DP, "tp"), check_vma=False
    )
```

```python
import jax
import jax.numpy as jnp
from jax import lax
from jax.experimental import pallas as pl
from jax.experimental.pallas import tpu as pltpu
from jax.sharding import Mesh, PartitionSpec as P

R = 64
CAP = 2
HCAP = 16
TAG = 128
DP = ("z_high", "z_low", "x", "core")
GROUP = ("z_low", "x", "core")
SWAP = [(0, 1), (1, 0)]


def pick(flags):
    return flags.astype(jnp.bfloat16)


def matmul(a, b):
    return jnp.dot(a, b, preferred_element_type=jnp.float32)


def narrow(a, b):
    return matmul(a, b).astype(jnp.bfloat16)


def sum_over_tp(part):
    if lax.axis_size("tp") == 2:
        return part + lax.ppermute(part, "tp", SWAP)
    return lax.psum(part, "tp")


def after(value, *others):
    return lax.optimization_barrier((value, *others))[0]


class Chain:
    def __init__(self):
        self.last = None

    def hold(self, value):
        self.last = value if self.last is None else after(value, self.last)
        return self.last

    def permute(self, value, axis, pairs):
        return lax.ppermute(self.hold(value), axis, pairs)

    def wait(self, *arrived):
        self.last = after(self.last, *arrived)


def kernel_params():
    return dict(
        compiler_params=pltpu.CompilerParams(vmem_limit_bytes=40 * 2**20),
        cost_estimate=pl.CostEstimate(flops=1, bytes_accessed=1, transcendentals=0),
    )


def pick_columns(store, expand, want_mine, want_other):
    depth, width = store.shape
    groups, lanes = want_mine.shape
    count = groups * lanes
    blocks = 8
    rows = depth // blocks

    def kernel(mine_held, other_held, mine_at, other_at, store_ref, expand_ref, mine_ref, first_ref, rest_ref, pick_mine, pick_other):
        step = pl.program_id(0)

        @pl.when(step == 0)
        def _():
            column = lax.broadcasted_iota(jnp.int32, (width, count), 0)
            pick_mine[...] = (column == mine_at[...]).astype(jnp.float32).astype(jnp.bfloat16)
            pick_other[...] = (column == other_at[...]).astype(jnp.float32).astype(jnp.bfloat16)

        def fill(out_ref, held, picker):
            for g in range(groups):
                at = slice(g * lanes, (g + 1) * lanes)

                @pl.when((held[g] > 0) & (step < blocks))
                def _():
                    out_ref[:, at] = narrow(store_ref[...], picker[:, at])

                @pl.when((held[g] > 0) & (step == blocks))
                def _():
                    product = lax.dot_general(
                        expand_ref[...], picker[:, at], (((0,), (0,)), ((), ())), preferred_element_type=jnp.float32
                    )
                    out_ref[:, at] = product.astype(jnp.bfloat16)

                @pl.when(held[g] == 0)
                def _():
                    out_ref[:, at] = jnp.zeros((rows, lanes), jnp.bfloat16)

        fill(mine_ref, mine_held, pick_mine)

        @pl.when(step < 3)
        def _():
            fill(first_ref, other_held, pick_other)

        @pl.when(step >= 3)
        def _():
            fill(rest_ref, other_held, pick_other)

    out = lambda thirds: jax.ShapeDtypeStruct((3 * rows * thirds, count), jnp.bfloat16)
    index = pl.BlockSpec((1, count), lambda i, *held: (0, 0))
    return pl.pallas_call(
        kernel,
        grid_spec=pltpu.PrefetchScalarGridSpec(
            num_scalar_prefetch=2,
            grid=(blocks + 1,),
            in_specs=[
                index,
                index,
                pl.BlockSpec((rows, width), lambda i, *held: (jnp.minimum(i, blocks - 1), 0)),
                pl.BlockSpec(expand.shape, lambda i, *held: (0, 0)),
            ],
            out_specs=[
                pl.BlockSpec((rows, count), lambda i, *held: (i, 0)),
                pl.BlockSpec((rows, count), lambda i, *held: (jnp.minimum(i, 2), 0)),
                pl.BlockSpec((rows, count), lambda i, *held: (jnp.maximum(i - 3, 0), 0)),
            ],
            scratch_shapes=[pltpu.VMEM((width, count), jnp.bfloat16)] * 2,
        ),
        out_shape=[out(3), out(1), out(2)],
        **kernel_params(),
    )(
        jnp.any(want_mine >= 0, axis=1).astype(jnp.int32),
        jnp.any(want_other >= 0, axis=1).astype(jnp.int32),
        want_mine.reshape(1, -1),
        want_other.reshape(1, -1),
        store,
        expand,
    )


def place_rows(rows, target, placed_rows):
    count, depth = rows.shape
    blocks = 4
    width = depth // blocks

    def kernel(target_at, rows_ref, out_ref, place):
        @pl.when(pl.program_id(0) == 0)
        def _():
            hit = lax.broadcasted_iota(jnp.int32, (placed_rows, count), 0) == target_at[...]
            place[...] = hit.astype(jnp.float32).astype(jnp.bfloat16)

        out_ref[...] = narrow(place[...], rows_ref[...])

    return pl.pallas_call(
        kernel,
        grid=(blocks,),
        in_specs=[pl.BlockSpec((1, count), lambda j: (0, 0)), pl.BlockSpec((count, width), lambda j: (0, j))],
        out_specs=pl.BlockSpec((placed_rows, width), lambda j: (0, j)),
        out_shape=jax.ShapeDtypeStruct((placed_rows, depth), jnp.bfloat16),
        scratch_shapes=[pltpu.VMEM((placed_rows, count), jnp.bfloat16)],
        **kernel_params(),
    )(target[None], rows)


def base_halves(rows, weight):
    count, depth = rows.shape
    width = weight.shape[1]
    half = width // 2
    blocks = 8
    part = depth // blocks

    def kernel(tp_at, rows_ref, weight_ref, own_ref, other_ref, total):
        step = pl.program_id(0)
        product = matmul(rows_ref[...], weight_ref[...])

        @pl.when(step == 0)
        def _():
            total[...] = product

        @pl.when(step > 0)
        def _():
            total[...] += product

        @pl.when(step == blocks - 1)
        def _():
            first = pl.multiple_of(tp_at[0] * half, 128)
            second = pl.multiple_of((1 - tp_at[0]) * half, 128)
            own_ref[...] = total[:, pl.ds(first, half)]
            other_ref[...] = total[:, pl.ds(second, half)]

    out = pl.BlockSpec((count, half), lambda k, at: (0, 0))
    return pl.pallas_call(
        kernel,
        grid_spec=pltpu.PrefetchScalarGridSpec(
            num_scalar_prefetch=1,
            grid=(blocks,),
            in_specs=[
                pl.BlockSpec((count, part), lambda k, at: (0, k)),
                pl.BlockSpec((part, width), lambda k, at: (k, 0)),
            ],
            out_specs=[out, out],
            scratch_shapes=[pltpu.VMEM((count, width), jnp.float32)],
        ),
        out_shape=[jax.ShapeDtypeStruct((count, half), jnp.float32)] * 2,
        **kernel_params(),
    )(lax.axis_index("tp").astype(jnp.int32)[None], rows, weight)


def hot_expand(z_own, z_got, factors, head):
    kept = factors[0].shape[1]
    near = kept // R
    count = z_own.shape[0] // HCAP

    def kernel(own_ref, got_ref, first_ref, second_ref, out_ref):
        z = (own_ref[...] + got_ref[...]).astype(jnp.bfloat16).astype(jnp.float32).reshape(count, 1, HCAP, kept)
        shape = (count, near, HCAP, kept)
        same = lax.broadcasted_iota(jnp.int32, shape, 3) // R == lax.broadcasted_iota(jnp.int32, shape, 1)
        spread = jnp.where(same, jnp.broadcast_to(z, shape), 0.0).astype(jnp.bfloat16)
        product = lax.dot_general(
            spread.reshape(count * near * HCAP, kept),
            first_ref[-head:] + second_ref[-head:],
            (((1,), (1,)), ((), ())),
            preferred_element_type=jnp.float32,
        )
        out_ref[...] = product.astype(jnp.bfloat16)

    return pl.pallas_call(
        kernel,
        out_shape=jax.ShapeDtypeStruct((count * near * HCAP, head), jnp.bfloat16),
        **kernel_params(),
    )(z_own, z_got, *factors)


def add_hot(partial, target, delta):
    count = partial.shape[0]
    hot_rows = delta.shape[0]

    def kernel(partial_ref, target_ref, delta_ref, out_ref):
        hit = lax.broadcasted_iota(jnp.int32, (count, hot_rows), 1) == target_ref[...]
        place = hit.astype(jnp.float32).astype(jnp.bfloat16)
        out_ref[...] = (partial_ref[...] + matmul(place, delta_ref[...])).astype(jnp.bfloat16)

    return pl.pallas_call(
        kernel,
        out_shape=jax.ShapeDtypeStruct(partial.shape, jnp.bfloat16),
        **kernel_params(),
    )(partial, target[:, None], delta)


def on_device(
    activations, value_weight, shrink_store, expand_store, adapter_row, token_adapter, hot_ids
):
    step_count, token_count, depth = activations.shape
    adapter_count = adapter_row.shape[0]
    hot_count = hot_ids.shape[1]
    per_dev = expand_store.shape[0] // R
    head_part = expand_store.shape[1]
    far_count = lax.axis_size("z_high")
    group_count = 8
    dp_count = far_count * group_count
    me = lax.axis_index(DP)
    z_at, x_at, core_at = lax.axis_index("z_low"), lax.axis_index("x"), lax.axis_index("core")
    none_code = adapter_count + hot_count
    rows = activations.reshape(step_count * token_count, depth)

    near = step_count // 2
    names = jnp.arange(adapter_count, dtype=jnp.int32)
    cold_row = jnp.sum(jnp.where((token_adapter - hot_count)[:, :, None] == names, adapter_row, 0), axis=-1)
    is_hot = token_adapter < hot_count
    is_cold = (token_adapter < none_code) & jnp.logical_not(is_hot)
    owner = cold_row // per_dev
    group = jnp.where(is_hot, token_adapter, jnp.where(is_cold, hot_count + owner, -1))
    at = jnp.arange(token_count, dtype=jnp.int32)
    before = (group[:, :, None] == group[:, None, :]) & (at[None, :] < at[:, None])
    rank = jnp.sum(before.astype(jnp.int32), axis=-1)
    step_at = jnp.arange(step_count, dtype=jnp.int32)[:, None]
    hot_rows = hot_count * step_count * HCAP
    cold_rows = dp_count * step_count * CAP
    server = (step_at // near) * hot_count + token_adapter
    hot_target = (server * near + step_at % near) * HCAP + rank
    cold_target = (owner * step_count + step_at) * CAP + rank
    hot_target = jnp.where(is_hot, hot_target, -1).reshape(-1)
    cold_target = jnp.where(is_cold, cold_target, -1).reshape(-1)
    hot_out = place_rows(rows, hot_target, hot_rows)
    chain = Chain()
    hot_in = lax.all_to_all(
        chain.hold(hot_out.reshape(group_count, near * HCAP, depth)), GROUP, split_axis=0, concat_axis=0, tiled=True
    )

    hot_row = jnp.sum(jnp.where(hot_ids[:, :, None] == names, adapter_row, 0), axis=-1)
    hot_first = jnp.where(hot_row // per_dev == me, (hot_row % per_dev) * R, -R * per_dev)
    column = jnp.arange(per_dev * R, dtype=jnp.int32)
    lane = jnp.arange(R, dtype=jnp.int32)
    entry = jnp.arange(hot_count, dtype=jnp.int32)

    def wanted(core):
        firsts = []
        for x in (x_at, 1 - x_at):
            of_steps = jnp.sum(jnp.where(entry == 2 * x + core, hot_first, 0), axis=1)
            firsts += [jnp.where(z_at == 0, of_steps[:near], of_steps[near:])]
            firsts += [jnp.where(z_at == 0, of_steps[near:], of_steps[:near])]
        return jnp.stack([(f[:, None] + lane).reshape(-1) for f in firsts])

    want_mine, want_other = wanted(core_at), wanted(1 - core_at)
    kept = near * R
    chunk_count = 3
    part = (depth + head_part) // chunk_count

    hops = [("x", SWAP), ("z_low", SWAP)]
    bit = 1
    while bit < far_count:
        hops.append(("z_high", [(i, i ^ bit) for i in range(far_count)]))
        bit *= 2
    mine, swapped, got, held = {}, {}, {}, {}

    def operand(c, stage):
        if stage == 0:
            return mine[c][:, 2 * kept:] + swapped[c][:, 2 * kept:]
        if stage == 1:
            return mine[c][:, kept:2 * kept] + swapped[c][:, kept:2 * kept] + got[c, 0][:, kept:]
        if stage == 2:
            held[c] = mine[c][:, :kept] + swapped[c][:, :kept] + got[c, 0][:, :kept] + got[c, 1]
        else:
            held[c] = held[c] + got[c, stage - 1]
        return held[c]

    def send(c, stage, value=None):
        got[c, stage] = chain.permute(operand(c, stage) if value is None else value, *hops[stage])

    mine_all, other_first, other_rest = pick_columns(
        after(shrink_store, chain.last), expand_store, want_mine, want_other
    )
    mine[0], swapped[0] = mine_all[:part], chain.permute(other_first, "core", SWAP)
    rest_swapped = chain.permute(other_rest, "core", SWAP)
    ready, hot_in = lax.optimization_barrier((operand(0, 0), hot_in))
    send(0, 0, ready)

    cold_at = after(cold_target, chain.last)
    cold_hit = jnp.arange(cold_rows, dtype=jnp.int32)[:, None] == cold_at
    tag = jnp.sum(jnp.where(cold_hit, (cold_row % per_dev + 1).reshape(-1), 0), axis=-1)
    tag = jnp.broadcast_to(tag.astype(jnp.bfloat16)[:, None], (cold_rows, TAG))
    packet = jnp.concatenate([narrow(pick(cold_hit), rows), tag], axis=1)
    packet = chain.hold(packet.reshape(dp_count, step_count * CAP, depth + TAG))
    packet = lax.all_to_all(packet, DP, split_axis=0, concat_axis=0, tiled=True).reshape(cold_rows, depth + TAG)

    done = {"packet": packet}

    def base_product():
        weight = after(value_weight, chain.last)
        if lax.axis_size("tp") == 2:
            done["base_own"], done["base_other"] = base_halves(rows, weight)
        else:
            done["base_own"], done["base_other"] = jnp.zeros((1, 1), jnp.float32), matmul(rows, weight)

    def base_over_tp():
        if lax.axis_size("tp") == 2:
            done["base_got"] = chain.permute(done["base_other"], "tp", SWAP)
        else:
            whole = chain.hold(done["base_other"])
            done["base_got"] = lax.psum_scatter(whole, "tp", scatter_dimension=1, tiled=True)

    def cold_shrink():
        tag_in = done["packet"][:, depth:depth + 1].astype(jnp.int32)
        chosen = (column // R + 1)[None, :] == tag_in
        product = matmul(done["packet"][:, :depth], after(shrink_store, chain.last))
        done["z_part"] = jnp.where(chosen, product, 0.0)

    def cold_over_tp():
        done["z_cold"] = sum_over_tp(chain.hold(done["z_part"]))

    def cold_expand():
        done["delta"] = narrow(done["z_cold"].astype(jnp.bfloat16), after(expand_store, chain.last))

    def cold_back():
        delta = chain.hold(done["delta"].reshape(dp_count, step_count * CAP, head_part))
        delta = lax.all_to_all(delta, DP, split_axis=0, concat_axis=0, tiled=True)
        done["delta_cold"] = delta.reshape(cold_rows, head_part)

    def all_but_hot():
        place_cold = pick(jnp.arange(cold_rows, dtype=jnp.int32)[:, None] == cold_target)
        partial = lax.dot_general(
            place_cold, done["delta_cold"], (((0,), (0,)), ((), ())), preferred_element_type=jnp.float32
        )
        done["partial"] = partial + done["base_own"] + done["base_got"]

    between = {
        1: [base_product],
        2: [cold_shrink, cold_over_tp, base_over_tp],
        3: [cold_expand, cold_back],
        4: [all_but_hot],
    }
    awaited = {1: ["packet", "base_own", "base_other"], 2: ["z_cold"], 4: ["partial"]}
    ready = None
    for slot in range(chunk_count + len(hops) - 1):
        if slot > 0:
            for stage in sorted(range(len(hops)), key=lambda stage: stage == 1):
                if 0 <= slot - stage < chunk_count:
                    send(slot - stage, stage, ready if stage == 0 else None)
        for work in between.get(slot, []):
            work()
        c = slot + 1
        if c < chunk_count:
            mine[c] = after(mine_all, chain.last)[c * part:(c + 1) * part]
            swapped[c] = after(rest_swapped, chain.last)[(c - 1) * part:c * part]
            ready = chain.hold(operand(c, 0))
        here = [(slot - stage, stage) for stage in range(len(hops)) if 0 <= slot - stage < chunk_count]
        names_here = awaited.get(slot, [])
        arrived = lax.optimization_barrier(
            (chain.last, *[got[at] for at in here], *[done[name] for name in names_here])
        )
        chain.last = arrived[0]
        got.update(zip(here, arrived[1:]))
        done.update(zip(names_here, arrived[1 + len(here):]))
    partial = done["partial"]

    hot_in = hot_in.reshape(hot_rows, depth)
    dense = None
    for c in range(chunk_count):
        last = min((c + 1) * part, depth)
        for piece in (held[c], got[c, len(hops) - 1]):
            product = matmul(hot_in[:, c * part:last], piece[:last - c * part])
            dense = product if dense is None else dense + product
    dense = dense.reshape(group_count, near, HCAP, kept)
    at_step = jnp.arange(kept) // R
    z_part = sum(jnp.where(at_step == i, dense[:, i], 0.0) for i in range(near)).reshape(group_count * HCAP, kept)
    if lax.axis_size("tp") == 2:
        z_got = lax.ppermute(z_part, "tp", SWAP)
    else:
        z_part = lax.psum(z_part, "tp")
        z_got = jnp.zeros_like(z_part)
    delta_hot = hot_expand(z_part, z_got, (held[c], got[c, len(hops) - 1]), head_part).reshape(group_count, near * HCAP, head_part)
    delta_hot = lax.all_to_all(delta_hot, GROUP, split_axis=0, concat_axis=0, tiled=True)
    added = add_hot(partial, hot_target, delta_hot.reshape(hot_rows, head_part))
    return added.reshape(step_count, token_count, head_part)


def solution(mesh):
    tp_count, dp_count = mesh.shape["tp"], mesh.shape["dp"]
    fine = Mesh(mesh.devices.reshape(tp_count, dp_count // 8, 2, 2, 2), ("tp", *DP))
    placed = (
        P(None, DP, "tp"),
        P("tp", None),
        P("tp", DP),
        P(DP, "tp"),
        P(),
        P(None, DP),
        P(),
    )
    return jax.shard_map(
        on_device, mesh=fine, in_specs=placed, out_specs=P(None, DP, "tp"), check_vma=False
    )
```

```python
import jax
import jax.numpy as jnp
from jax import lax
from jax.experimental import pallas as pl
from jax.experimental.pallas import tpu as pltpu
from jax.sharding import Mesh, PartitionSpec as P

R = 64
CAP = 2
HCAP = 16
TAG = 128
DP = ("z_high", "z_low", "x", "core")
GROUP = ("z_low", "x", "core")
SWAP = [(0, 1), (1, 0)]


def pick(flags):
    return flags.astype(jnp.bfloat16)


def matmul(a, b):
    return jnp.dot(a, b, preferred_element_type=jnp.float32)


def narrow(a, b):
    return matmul(a, b).astype(jnp.bfloat16)


def sum_over_tp(part):
    if lax.axis_size("tp") == 2:
        return part + lax.ppermute(part, "tp", SWAP)
    return lax.psum(part, "tp")


def after(value, *others):
    return lax.optimization_barrier((value, *others))[0]


class Chain:
    def __init__(self):
        self.last = None

    def hold(self, value):
        self.last = value if self.last is None else after(value, self.last)
        return self.last

    def permute(self, value, axis, pairs):
        return lax.ppermute(self.hold(value), axis, pairs)

    def wait(self, *arrived):
        self.last = after(self.last, *arrived)


def kernel_params(flops=1, bytes_accessed=1):
    return dict(
        compiler_params=pltpu.CompilerParams(vmem_limit_bytes=40 * 2**20),
        cost_estimate=pl.CostEstimate(flops=flops, bytes_accessed=bytes_accessed, transcendentals=0),
    )


def pick_columns(store, expand, want_mine, want_other):
    depth, width = store.shape
    groups, lanes = want_mine.shape
    count = groups * lanes
    blocks = 8
    rows = depth // blocks

    def kernel(mine_held, other_held, mine_at, other_at, store_ref, expand_ref, mine_ref, first_ref, rest_ref, pick_mine, pick_other):
        step = pl.program_id(0)

        @pl.when(step == 0)
        def _():
            column = lax.broadcasted_iota(jnp.int32, (width, count), 0)
            pick_mine[...] = (column == mine_at[...]).astype(jnp.float32).astype(jnp.bfloat16)
            pick_other[...] = (column == other_at[...]).astype(jnp.float32).astype(jnp.bfloat16)

        def fill(out_ref, held, picker):
            for g in range(groups):
                at = slice(g * lanes, (g + 1) * lanes)

                @pl.when((held[g] > 0) & (step < blocks))
                def _():
                    out_ref[:, at] = narrow(store_ref[...], picker[:, at])

                @pl.when((held[g] > 0) & (step == blocks))
                def _():
                    product = lax.dot_general(
                        expand_ref[...], picker[:, at], (((0,), (0,)), ((), ())), preferred_element_type=jnp.float32
                    )
                    out_ref[:, at] = product.astype(jnp.bfloat16)

                @pl.when(held[g] == 0)
                def _():
                    out_ref[:, at] = jnp.zeros((rows, lanes), jnp.bfloat16)

        fill(mine_ref, mine_held, pick_mine)

        @pl.when(step < 3)
        def _():
            fill(first_ref, other_held, pick_other)

        @pl.when(step >= 3)
        def _():
            fill(rest_ref, other_held, pick_other)

    out = lambda thirds: jax.ShapeDtypeStruct((3 * rows * thirds, count), jnp.bfloat16)
    index = pl.BlockSpec((1, count), lambda i, *held: (0, 0))
    return pl.pallas_call(
        kernel,
        grid_spec=pltpu.PrefetchScalarGridSpec(
            num_scalar_prefetch=2,
            grid=(blocks + 1,),
            in_specs=[
                index,
                index,
                pl.BlockSpec((rows, width), lambda i, *held: (jnp.minimum(i, blocks - 1), 0)),
                pl.BlockSpec(expand.shape, lambda i, *held: (0, 0)),
            ],
            out_specs=[
                pl.BlockSpec((rows, count), lambda i, *held: (i, 0)),
                pl.BlockSpec((rows, count), lambda i, *held: (jnp.minimum(i, 2), 0)),
                pl.BlockSpec((rows, count), lambda i, *held: (jnp.maximum(i - 3, 0), 0)),
            ],
            scratch_shapes=[pltpu.VMEM((width, count), jnp.bfloat16)] * 2,
        ),
        out_shape=[out(3), out(1), out(2)],
        **kernel_params(),
    )(
        jnp.any(want_mine >= 0, axis=1).astype(jnp.int32),
        jnp.any(want_other >= 0, axis=1).astype(jnp.int32),
        want_mine.reshape(1, -1),
        want_other.reshape(1, -1),
        store,
        expand,
    )


def place_rows(rows, target, placed_rows):
    count, depth = rows.shape
    blocks = 4
    width = depth // blocks

    def kernel(target_at, rows_ref, out_ref, place):
        @pl.when(pl.program_id(0) == 0)
        def _():
            hit = lax.broadcasted_iota(jnp.int32, (placed_rows, count), 0) == target_at[...]
            place[...] = hit.astype(jnp.float32).astype(jnp.bfloat16)

        out_ref[...] = narrow(place[...], rows_ref[...])

    return pl.pallas_call(
        kernel,
        grid=(blocks,),
        in_specs=[pl.BlockSpec((1, count), lambda j: (0, 0)), pl.BlockSpec((count, width), lambda j: (0, j))],
        out_specs=pl.BlockSpec((placed_rows, width), lambda j: (0, j)),
        out_shape=jax.ShapeDtypeStruct((placed_rows, depth), jnp.bfloat16),
        scratch_shapes=[pltpu.VMEM((placed_rows, count), jnp.bfloat16)],
        **kernel_params(2 * placed_rows * count * depth, 2 * (placed_rows + count) * depth),
    )(target[None], rows)


def base_halves(rows, weight):
    count, depth = rows.shape
    width = weight.shape[1]
    half = width // 2
    blocks = 8
    part = depth // blocks

    def kernel(tp_at, rows_ref, weight_ref, own_ref, other_ref, total):
        step = pl.program_id(0)
        product = matmul(rows_ref[...], weight_ref[...])

        @pl.when(step == 0)
        def _():
            total[...] = product

        @pl.when(step > 0)
        def _():
            total[...] += product

        @pl.when(step == blocks - 1)
        def _():
            first = pl.multiple_of(tp_at[0] * half, 128)
            second = pl.multiple_of((1 - tp_at[0]) * half, 128)
            own_ref[...] = total[:, pl.ds(first, half)]
            other_ref[...] = total[:, pl.ds(second, half)]

    out = pl.BlockSpec((count, half), lambda k, at: (0, 0))
    return pl.pallas_call(
        kernel,
        grid_spec=pltpu.PrefetchScalarGridSpec(
            num_scalar_prefetch=1,
            grid=(blocks,),
            in_specs=[
                pl.BlockSpec((count, part), lambda k, at: (0, k)),
                pl.BlockSpec((part, width), lambda k, at: (k, 0)),
            ],
            out_specs=[out, out],
            scratch_shapes=[pltpu.VMEM((count, width), jnp.float32)],
        ),
        out_shape=[jax.ShapeDtypeStruct((count, half), jnp.float32)] * 2,
        **kernel_params(),
    )(lax.axis_index("tp").astype(jnp.int32)[None], rows, weight)


def hot_expand(z_own, z_got, factors, head):
    kept = factors[0].shape[1]
    near = kept // R
    count = z_own.shape[0] // HCAP

    def kernel(own_ref, got_ref, first_ref, second_ref, out_ref):
        z = (own_ref[...] + got_ref[...]).astype(jnp.bfloat16).astype(jnp.float32).reshape(count, 1, HCAP, kept)
        shape = (count, near, HCAP, kept)
        same = lax.broadcasted_iota(jnp.int32, shape, 3) // R == lax.broadcasted_iota(jnp.int32, shape, 1)
        spread = jnp.where(same, jnp.broadcast_to(z, shape), 0.0).astype(jnp.bfloat16)
        product = lax.dot_general(
            spread.reshape(count * near * HCAP, kept),
            first_ref[-head:] + second_ref[-head:],
            (((1,), (1,)), ((), ())),
            preferred_element_type=jnp.float32,
        )
        out_ref[...] = product.astype(jnp.bfloat16)

    return pl.pallas_call(
        kernel,
        out_shape=jax.ShapeDtypeStruct((count * near * HCAP, head), jnp.bfloat16),
        **kernel_params(),
    )(z_own, z_got, *factors)


def add_hot(partial, target, delta):
    count = partial.shape[0]
    hot_rows = delta.shape[0]

    def kernel(partial_ref, target_ref, delta_ref, out_ref):
        hit = lax.broadcasted_iota(jnp.int32, (count, hot_rows), 1) == target_ref[...]
        place = hit.astype(jnp.float32).astype(jnp.bfloat16)
        out_ref[...] = (partial_ref[...] + matmul(place, delta_ref[...])).astype(jnp.bfloat16)

    return pl.pallas_call(
        kernel,
        out_shape=jax.ShapeDtypeStruct(partial.shape, jnp.bfloat16),
        **kernel_params(),
    )(partial, target[:, None], delta)


def on_device(
    activations, value_weight, shrink_store, expand_store, adapter_row, token_adapter, hot_ids
):
    step_count, token_count, depth = activations.shape
    adapter_count = adapter_row.shape[0]
    hot_count = hot_ids.shape[1]
    per_dev = expand_store.shape[0] // R
    head_part = expand_store.shape[1]
    far_count = lax.axis_size("z_high")
    group_count = 8
    dp_count = far_count * group_count
    me = lax.axis_index(DP)
    z_at, x_at, core_at = lax.axis_index("z_low"), lax.axis_index("x"), lax.axis_index("core")
    none_code = adapter_count + hot_count
    rows = activations.reshape(step_count * token_count, depth)

    near = step_count // 2
    names = jnp.arange(adapter_count, dtype=jnp.int32)
    chain = Chain()

    hot_row = jnp.sum(jnp.where(hot_ids[:, :, None] == names, adapter_row, 0), axis=-1)
    hot_first = jnp.where(hot_row // per_dev == me, (hot_row % per_dev) * R, -R * per_dev)
    column = jnp.arange(per_dev * R, dtype=jnp.int32)
    lane = jnp.arange(R, dtype=jnp.int32)
    entry = jnp.arange(hot_count, dtype=jnp.int32)

    def wanted(core):
        firsts = []
        for x in (x_at, 1 - x_at):
            of_steps = jnp.sum(jnp.where(entry == 2 * x + core, hot_first, 0), axis=1)
            firsts += [jnp.where(z_at == 0, of_steps[:near], of_steps[near:])]
            firsts += [jnp.where(z_at == 0, of_steps[near:], of_steps[:near])]
        return jnp.stack([(f[:, None] + lane).reshape(-1) for f in firsts])

    want_mine, want_other = wanted(core_at), wanted(1 - core_at)
    kept = near * R
    chunk_count = 3
    part = (depth + head_part) // chunk_count

    hops = [("x", SWAP), ("z_low", SWAP)]
    bit = 1
    while bit < far_count:
        hops.append(("z_high", [(i, i ^ bit) for i in range(far_count)]))
        bit *= 2
    mine, swapped, got, held = {}, {}, {}, {}

    def operand(c, stage):
        if stage == 0:
            return mine[c][:, 2 * kept:] + swapped[c][:, 2 * kept:]
        if stage == 1:
            return mine[c][:, kept:2 * kept] + swapped[c][:, kept:2 * kept] + got[c, 0][:, kept:]
        if stage == 2:
            held[c] = mine[c][:, :kept] + swapped[c][:, :kept] + got[c, 0][:, :kept] + got[c, 1]
        else:
            held[c] = held[c] + got[c, stage - 1]
        return held[c]

    def send(c, stage, value=None):
        got[c, stage] = chain.permute(operand(c, stage) if value is None else value, *hops[stage])

    mine_all, other_first, other_rest = pick_columns(
        shrink_store, expand_store, want_mine, want_other
    )
    mine[0], swapped[0] = mine_all[:part], chain.permute(other_first, "core", SWAP)
    rest_swapped = chain.permute(other_rest, "core", SWAP)
    send(0, 0)

    token_adapter = after(token_adapter, chain.last)
    cold_row = jnp.sum(jnp.where((token_adapter - hot_count)[:, :, None] == names, adapter_row, 0), axis=-1)
    is_hot = token_adapter < hot_count
    is_cold = (token_adapter < none_code) & jnp.logical_not(is_hot)
    owner = cold_row // per_dev
    group = jnp.where(is_hot, token_adapter, jnp.where(is_cold, hot_count + owner, -1))
    at = jnp.arange(token_count, dtype=jnp.int32)
    before = (group[:, :, None] == group[:, None, :]) & (at[None, :] < at[:, None])
    rank = jnp.sum(before.astype(jnp.int32), axis=-1)
    step_at = jnp.arange(step_count, dtype=jnp.int32)[:, None]
    hot_rows = hot_count * step_count * HCAP
    cold_rows = dp_count * step_count * CAP
    server = (step_at // near) * hot_count + token_adapter
    hot_target = (server * near + step_at % near) * HCAP + rank
    cold_target = (owner * step_count + step_at) * CAP + rank
    hot_target = jnp.where(is_hot, hot_target, -1).reshape(-1)
    cold_target = jnp.where(is_cold, cold_target, -1).reshape(-1)

    hot_out = place_rows(rows, after(hot_target, chain.last), hot_rows)
    hot_out = chain.hold(hot_out.reshape(group_count, near * HCAP, depth))
    done = {"hot_in": lax.all_to_all(hot_out, GROUP, split_axis=0, concat_axis=0, tiled=True)}

    def cold_tokens_out():
        cold_at = after(cold_target, chain.last)
        cold_hit = jnp.arange(cold_rows, dtype=jnp.int32)[:, None] == cold_at
        tag = jnp.sum(jnp.where(cold_hit, (cold_row % per_dev + 1).reshape(-1), 0), axis=-1)
        tag = jnp.broadcast_to(tag.astype(jnp.bfloat16)[:, None], (cold_rows, TAG))
        packet = jnp.concatenate([narrow(pick(cold_hit), rows), tag], axis=1)
        packet = chain.hold(packet.reshape(dp_count, step_count * CAP, depth + TAG))
        packet = lax.all_to_all(packet, DP, split_axis=0, concat_axis=0, tiled=True)
        done["packet"] = packet.reshape(cold_rows, depth + TAG)

    def base_product():
        weight = after(value_weight, chain.last)
        if lax.axis_size("tp") == 2:
            done["base_own"], done["base_other"] = base_halves(rows, weight)
        else:
            done["base_own"], done["base_other"] = jnp.zeros((1, 1), jnp.float32), matmul(rows, weight)

    def base_over_tp():
        if lax.axis_size("tp") == 2:
            done["base_got"] = chain.permute(done["base_other"], "tp", SWAP)
        else:
            whole = chain.hold(done["base_other"])
            done["base_got"] = lax.psum_scatter(whole, "tp", scatter_dimension=1, tiled=True)

    def cold_shrink():
        tag_in = done["packet"][:, depth:depth + 1].astype(jnp.int32)
        chosen = (column // R + 1)[None, :] == tag_in
        product = matmul(done["packet"][:, :depth], after(shrink_store, chain.last))
        done["z_part"] = jnp.where(chosen, product, 0.0)

    def cold_over_tp():
        done["z_cold"] = sum_over_tp(chain.hold(done["z_part"]))

    def cold_expand():
        done["delta"] = narrow(done["z_cold"].astype(jnp.bfloat16), after(expand_store, chain.last))

    def cold_back():
        delta = chain.hold(done["delta"].reshape(dp_count, step_count * CAP, head_part))
        delta = lax.all_to_all(delta, DP, split_axis=0, concat_axis=0, tiled=True)
        done["delta_cold"] = delta.reshape(cold_rows, head_part)

    def all_but_hot():
        place_cold = pick(jnp.arange(cold_rows, dtype=jnp.int32)[:, None] == cold_target)
        partial = lax.dot_general(
            place_cold, done["delta_cold"], (((0,), (0,)), ((), ())), preferred_element_type=jnp.float32
        )
        done["partial"] = partial + done["base_own"] + done["base_got"]

    between = {
        1: [cold_tokens_out, base_product],
        2: [base_over_tp],
        3: [cold_shrink, cold_over_tp],
        4: [cold_expand, cold_back, all_but_hot],
    }
    awaited = {1: ["hot_in", "base_own", "base_other"], 2: ["packet"], 3: ["z_cold", "base_got"]}
    ready = None
    for slot in range(chunk_count + len(hops) - 1):
        if slot > 0:
            for stage in sorted(range(len(hops)), key=lambda stage: stage == 1):
                if 0 <= slot - stage < chunk_count:
                    send(slot - stage, stage, ready if stage == 0 else None)
        for work in between.get(slot, []):
            work()
        c = slot + 1
        if c < chunk_count:
            mine[c] = after(mine_all, chain.last)[c * part:(c + 1) * part]
            swapped[c] = after(rest_swapped, chain.last)[(c - 1) * part:c * part]
            ready = chain.hold(operand(c, 0))
        here = [(slot - stage, stage) for stage in range(len(hops)) if 0 <= slot - stage < chunk_count]
        names_here = awaited.get(slot, [])
        arrived = lax.optimization_barrier(
            (chain.last, *[got[at] for at in here], *[done[name] for name in names_here])
        )
        chain.last = arrived[0]
        got.update(zip(here, arrived[1:]))
        done.update(zip(names_here, arrived[1 + len(here):]))
    partial = done["partial"]

    hot_in = done["hot_in"].reshape(hot_rows, depth)
    dense = None
    for c in range(chunk_count):
        last = min((c + 1) * part, depth)
        for piece in (held[c], got[c, len(hops) - 1]):
            product = matmul(hot_in[:, c * part:last], piece[:last - c * part])
            dense = product if dense is None else dense + product
    dense = dense.reshape(group_count, near, HCAP, kept)
    at_step = jnp.arange(kept) // R
    z_part = sum(jnp.where(at_step == i, dense[:, i], 0.0) for i in range(near)).reshape(group_count * HCAP, kept)
    if lax.axis_size("tp") == 2:
        z_got = lax.ppermute(z_part, "tp", SWAP)
    else:
        z_part = lax.psum(z_part, "tp")
        z_got = jnp.zeros_like(z_part)
    delta_hot = hot_expand(z_part, z_got, (held[c], got[c, len(hops) - 1]), head_part).reshape(group_count, near * HCAP, head_part)
    delta_hot = lax.all_to_all(delta_hot, GROUP, split_axis=0, concat_axis=0, tiled=True)
    added = add_hot(partial, hot_target, delta_hot.reshape(hot_rows, head_part))
    return added.reshape(step_count, token_count, head_part)


def solution(mesh):
    tp_count, dp_count = mesh.shape["tp"], mesh.shape["dp"]
    fine = Mesh(mesh.devices.reshape(tp_count, dp_count // 8, 2, 2, 2), ("tp", *DP))
    placed = (
        P(None, DP, "tp"),
        P("tp", None),
        P("tp", DP),
        P(DP, "tp"),
        P(),
        P(None, DP),
        P(),
    )
    return jax.shard_map(
        on_device, mesh=fine, in_specs=placed, out_specs=P(None, DP, "tp"), check_vma=False
    )
```

```python
import jax
import jax.numpy as jnp
from jax import lax
from jax.experimental import pallas as pl
from jax.experimental.pallas import tpu as pltpu
from jax.sharding import Mesh, PartitionSpec as P

R = 64
CAP = 2
HCAP = 16
TAG = 128
DP = ("z_high", "z_low", "x", "core")
GROUP = ("z_low", "x", "core")
SWAP = [(0, 1), (1, 0)]


def pick(flags):
    return flags.astype(jnp.bfloat16)


def matmul(a, b):
    return jnp.dot(a, b, preferred_element_type=jnp.float32)


def narrow(a, b):
    return matmul(a, b).astype(jnp.bfloat16)


def sum_over_tp(part):
    if lax.axis_size("tp") == 2:
        return part + lax.ppermute(part, "tp", SWAP)
    return lax.psum(part, "tp")


def after(value, *others):
    return lax.optimization_barrier((value, *others))[0]


class Chain:
    def __init__(self):
        self.last = None

    def hold(self, value):
        self.last = value if self.last is None else after(value, self.last)
        return self.last

    def permute(self, value, axis, pairs):
        return lax.ppermute(self.hold(value), axis, pairs)

    def wait(self, *arrived):
        self.last = after(self.last, *arrived)


def kernel_params(flops=1, bytes_accessed=1):
    return dict(
        compiler_params=pltpu.CompilerParams(vmem_limit_bytes=40 * 2**20),
        cost_estimate=pl.CostEstimate(flops=flops, bytes_accessed=bytes_accessed, transcendentals=0),
    )


def pick_columns(store, expand, want_mine, want_other):
    depth, width = store.shape
    groups, lanes = want_mine.shape
    count = groups * lanes
    blocks = 8
    rows = depth // blocks

    def kernel(mine_held, other_held, mine_at, other_at, store_ref, expand_ref, mine_ref, first_ref, rest_ref, pick_mine, pick_other):
        step = pl.program_id(0)

        @pl.when(step == 0)
        def _():
            column = lax.broadcasted_iota(jnp.int32, (width, count), 0)
            pick_mine[...] = (column == mine_at[...]).astype(jnp.float32).astype(jnp.bfloat16)
            pick_other[...] = (column == other_at[...]).astype(jnp.float32).astype(jnp.bfloat16)

        def fill(out_ref, held, picker):
            for g in range(groups):
                at = slice(g * lanes, (g + 1) * lanes)

                @pl.when((held[g] > 0) & (step < blocks))
                def _():
                    out_ref[:, at] = narrow(store_ref[...], picker[:, at])

                @pl.when((held[g] > 0) & (step == blocks))
                def _():
                    product = lax.dot_general(
                        expand_ref[...], picker[:, at], (((0,), (0,)), ((), ())), preferred_element_type=jnp.float32
                    )
                    out_ref[:, at] = product.astype(jnp.bfloat16)

                @pl.when(held[g] == 0)
                def _():
                    out_ref[:, at] = jnp.zeros((rows, lanes), jnp.bfloat16)

        fill(mine_ref, mine_held, pick_mine)

        @pl.when(step < 3)
        def _():
            fill(first_ref, other_held, pick_other)

        @pl.when(step >= 3)
        def _():
            fill(rest_ref, other_held, pick_other)

    out = lambda thirds: jax.ShapeDtypeStruct((3 * rows * thirds, count), jnp.bfloat16)
    index = pl.BlockSpec((1, count), lambda i, *held: (0, 0))
    return pl.pallas_call(
        kernel,
        grid_spec=pltpu.PrefetchScalarGridSpec(
            num_scalar_prefetch=2,
            grid=(blocks + 1,),
            in_specs=[
                index,
                index,
                pl.BlockSpec((rows, width), lambda i, *held: (jnp.minimum(i, blocks - 1), 0)),
                pl.BlockSpec(expand.shape, lambda i, *held: (0, 0)),
            ],
            out_specs=[
                pl.BlockSpec((rows, count), lambda i, *held: (i, 0)),
                pl.BlockSpec((rows, count), lambda i, *held: (jnp.minimum(i, 2), 0)),
                pl.BlockSpec((rows, count), lambda i, *held: (jnp.maximum(i - 3, 0), 0)),
            ],
            scratch_shapes=[pltpu.VMEM((width, count), jnp.bfloat16)] * 2,
        ),
        out_shape=[out(3), out(1), out(2)],
        **kernel_params(),
    )(
        jnp.any(want_mine >= 0, axis=1).astype(jnp.int32),
        jnp.any(want_other >= 0, axis=1).astype(jnp.int32),
        want_mine.reshape(1, -1),
        want_other.reshape(1, -1),
        store,
        expand,
    )


def place_rows(rows, target, placed_rows):
    count, depth = rows.shape
    blocks = 4
    width = depth // blocks

    def kernel(target_at, rows_ref, out_ref, place):
        @pl.when(pl.program_id(0) == 0)
        def _():
            hit = lax.broadcasted_iota(jnp.int32, (placed_rows, count), 0) == target_at[...]
            place[...] = hit.astype(jnp.float32).astype(jnp.bfloat16)

        out_ref[...] = narrow(place[...], rows_ref[...])

    return pl.pallas_call(
        kernel,
        grid=(blocks,),
        in_specs=[pl.BlockSpec((1, count), lambda j: (0, 0)), pl.BlockSpec((count, width), lambda j: (0, j))],
        out_specs=pl.BlockSpec((placed_rows, width), lambda j: (0, j)),
        out_shape=jax.ShapeDtypeStruct((placed_rows, depth), jnp.bfloat16),
        scratch_shapes=[pltpu.VMEM((placed_rows, count), jnp.bfloat16)],
        **kernel_params(2 * placed_rows * count * depth, 2 * (placed_rows + count) * depth),
    )(target[None], rows)


def base_halves(rows, weight):
    count, depth = rows.shape
    width = weight.shape[1]
    half = width // 2
    blocks = 8
    part = depth // blocks

    def kernel(tp_at, rows_ref, weight_ref, own_ref, other_ref, total):
        step = pl.program_id(0)
        product = matmul(rows_ref[...], weight_ref[...])

        @pl.when(step == 0)
        def _():
            total[...] = product

        @pl.when(step > 0)
        def _():
            total[...] += product

        @pl.when(step == blocks - 1)
        def _():
            first = pl.multiple_of(tp_at[0] * half, 128)
            second = pl.multiple_of((1 - tp_at[0]) * half, 128)
            own_ref[...] = total[:, pl.ds(first, half)]
            other_ref[...] = total[:, pl.ds(second, half)]

    out = pl.BlockSpec((count, half), lambda k, at: (0, 0))
    return pl.pallas_call(
        kernel,
        grid_spec=pltpu.PrefetchScalarGridSpec(
            num_scalar_prefetch=1,
            grid=(blocks,),
            in_specs=[
                pl.BlockSpec((count, part), lambda k, at: (0, k)),
                pl.BlockSpec((part, width), lambda k, at: (k, 0)),
            ],
            out_specs=[out, out],
            scratch_shapes=[pltpu.VMEM((count, width), jnp.float32)],
        ),
        out_shape=[jax.ShapeDtypeStruct((count, half), jnp.float32)] * 2,
        **kernel_params(),
    )(lax.axis_index("tp").astype(jnp.int32)[None], rows, weight)


def hot_expand(z_own, z_got, factors, head):
    kept = factors[0].shape[1]
    near = kept // R
    count = z_own.shape[0] // HCAP

    def kernel(own_ref, got_ref, first_ref, second_ref, out_ref):
        z = (own_ref[...] + got_ref[...]).astype(jnp.bfloat16).astype(jnp.float32).reshape(count, 1, HCAP, kept)
        shape = (count, near, HCAP, kept)
        same = lax.broadcasted_iota(jnp.int32, shape, 3) // R == lax.broadcasted_iota(jnp.int32, shape, 1)
        spread = jnp.where(same, jnp.broadcast_to(z, shape), 0.0).astype(jnp.bfloat16)
        product = lax.dot_general(
            spread.reshape(count * near * HCAP, kept),
            first_ref[-head:] + second_ref[-head:],
            (((1,), (1,)), ((), ())),
            preferred_element_type=jnp.float32,
        )
        out_ref[...] = product.astype(jnp.bfloat16)

    return pl.pallas_call(
        kernel,
        out_shape=jax.ShapeDtypeStruct((count * near * HCAP, head), jnp.bfloat16),
        **kernel_params(),
    )(z_own, z_got, *factors)


def add_hot(partial, target, delta):
    count = partial.shape[0]
    hot_rows = delta.shape[0]

    def kernel(partial_ref, target_ref, delta_ref, out_ref):
        hit = lax.broadcasted_iota(jnp.int32, (count, hot_rows), 1) == target_ref[...]
        place = hit.astype(jnp.float32).astype(jnp.bfloat16)
        out_ref[...] = (partial_ref[...] + matmul(place, delta_ref[...])).astype(jnp.bfloat16)

    return pl.pallas_call(
        kernel,
        out_shape=jax.ShapeDtypeStruct(partial.shape, jnp.bfloat16),
        **kernel_params(),
    )(partial, target[:, None], delta)


def on_device(
    activations, value_weight, shrink_store, expand_store, adapter_row, token_adapter, hot_ids
):
    step_count, token_count, depth = activations.shape
    adapter_count = adapter_row.shape[0]
    hot_count = hot_ids.shape[1]
    per_dev = expand_store.shape[0] // R
    head_part = expand_store.shape[1]
    far_count = lax.axis_size("z_high")
    group_count = 8
    dp_count = far_count * group_count
    me = lax.axis_index(DP)
    z_at, x_at, core_at = lax.axis_index("z_low"), lax.axis_index("x"), lax.axis_index("core")
    none_code = adapter_count + hot_count
    rows = activations.reshape(step_count * token_count, depth)

    near = step_count // 2
    names = jnp.arange(adapter_count, dtype=jnp.int32)
    chain = Chain()

    hot_row = jnp.sum(jnp.where(hot_ids[:, :, None] == names, adapter_row, 0), axis=-1)
    hot_first = jnp.where(hot_row // per_dev == me, (hot_row % per_dev) * R, -R * per_dev)
    column = jnp.arange(per_dev * R, dtype=jnp.int32)
    lane = jnp.arange(R, dtype=jnp.int32)
    entry = jnp.arange(hot_count, dtype=jnp.int32)

    def wanted(core):
        firsts = []
        for x in (x_at, 1 - x_at):
            of_steps = jnp.sum(jnp.where(entry == 2 * x + core, hot_first, 0), axis=1)
            firsts += [jnp.where(z_at == 0, of_steps[:near], of_steps[near:])]
            firsts += [jnp.where(z_at == 0, of_steps[near:], of_steps[:near])]
        return jnp.stack([(f[:, None] + lane).reshape(-1) for f in firsts])

    want_mine, want_other = wanted(core_at), wanted(1 - core_at)
    kept = near * R
    chunk_count = 3
    part = (depth + head_part) // chunk_count

    hops = [("x", SWAP), ("z_low", SWAP)]
    bit = 1
    while bit < far_count:
        hops.append(("z_high", [(i, i ^ bit) for i in range(far_count)]))
        bit *= 2
    mine, swapped, got, held = {}, {}, {}, {}

    def operand(c, stage):
        if stage == 0:
            return mine[c][:, 2 * kept:] + swapped[c][:, 2 * kept:]
        if stage == 1:
            return mine[c][:, kept:2 * kept] + swapped[c][:, kept:2 * kept] + got[c, 0][:, kept:]
        if stage == 2:
            held[c] = mine[c][:, :kept] + swapped[c][:, :kept] + got[c, 0][:, :kept] + got[c, 1]
        else:
            held[c] = held[c] + got[c, stage - 1]
        return held[c]

    def send(c, stage):
        got[c, stage] = chain.permute(operand(c, stage), *hops[stage])

    mine_all, other_first, other_rest = pick_columns(
        shrink_store, expand_store, want_mine, want_other
    )
    mine[0], swapped[0] = mine_all[:part], chain.permute(other_first, "core", SWAP)
    rest_swapped = chain.permute(other_rest, "core", SWAP)
    send(0, 0)

    token_adapter = after(token_adapter, chain.last)
    cold_row = jnp.sum(jnp.where((token_adapter - hot_count)[:, :, None] == names, adapter_row, 0), axis=-1)
    is_hot = token_adapter < hot_count
    is_cold = (token_adapter < none_code) & jnp.logical_not(is_hot)
    owner = cold_row // per_dev
    group = jnp.where(is_hot, token_adapter, jnp.where(is_cold, hot_count + owner, -1))
    at = jnp.arange(token_count, dtype=jnp.int32)
    before = (group[:, :, None] == group[:, None, :]) & (at[None, :] < at[:, None])
    rank = jnp.sum(before.astype(jnp.int32), axis=-1)
    step_at = jnp.arange(step_count, dtype=jnp.int32)[:, None]
    hot_rows = hot_count * step_count * HCAP
    cold_rows = dp_count * step_count * CAP
    server = (step_at // near) * hot_count + token_adapter
    hot_target = (server * near + step_at % near) * HCAP + rank
    cold_target = (owner * step_count + step_at) * CAP + rank
    hot_target = jnp.where(is_hot, hot_target, -1).reshape(-1)
    cold_target = jnp.where(is_cold, cold_target, -1).reshape(-1)

    hot_out = place_rows(rows, after(hot_target, chain.last), hot_rows)
    hot_out = chain.hold(hot_out.reshape(group_count, near * HCAP, depth))
    done = {"hot_in": lax.all_to_all(hot_out, GROUP, split_axis=0, concat_axis=0, tiled=True)}

    def cold_tokens_out():
        cold_at = after(cold_target, chain.last)
        cold_hit = jnp.arange(cold_rows, dtype=jnp.int32)[:, None] == cold_at
        tag = jnp.sum(jnp.where(cold_hit, (cold_row % per_dev + 1).reshape(-1), 0), axis=-1)
        tag = jnp.broadcast_to(tag.astype(jnp.bfloat16)[:, None], (cold_rows, TAG))
        packet = jnp.concatenate([narrow(pick(cold_hit), rows), tag], axis=1)
        packet = chain.hold(packet.reshape(dp_count, step_count * CAP, depth + TAG))
        packet = lax.all_to_all(packet, DP, split_axis=0, concat_axis=0, tiled=True)
        done["packet"] = packet.reshape(cold_rows, depth + TAG)

    def base_product():
        weight = after(value_weight, chain.last)
        if lax.axis_size("tp") == 2:
            done["base_own"], done["base_other"] = base_halves(rows, weight)
        else:
            done["base_own"], done["base_other"] = jnp.zeros((1, 1), jnp.float32), matmul(rows, weight)

    def base_over_tp():
        if lax.axis_size("tp") == 2:
            done["base_got"] = chain.permute(done["base_other"], "tp", SWAP)
        else:
            whole = chain.hold(done["base_other"])
            done["base_got"] = lax.psum_scatter(whole, "tp", scatter_dimension=1, tiled=True)

    def cold_shrink():
        tag_in = done["packet"][:, depth:depth + 1].astype(jnp.int32)
        chosen = (column // R + 1)[None, :] == tag_in
        product = matmul(done["packet"][:, :depth], after(shrink_store, chain.last))
        done["z_part"] = jnp.where(chosen, product, 0.0)

    def cold_over_tp():
        done["z_cold"] = sum_over_tp(chain.hold(done["z_part"]))

    def cold_expand():
        done["delta"] = narrow(done["z_cold"].astype(jnp.bfloat16), after(expand_store, chain.last))

    def cold_back():
        delta = chain.hold(done["delta"].reshape(dp_count, step_count * CAP, head_part))
        delta = lax.all_to_all(delta, DP, split_axis=0, concat_axis=0, tiled=True)
        done["delta_cold"] = delta.reshape(cold_rows, head_part)

    def all_but_hot():
        place_cold = pick(jnp.arange(cold_rows, dtype=jnp.int32)[:, None] == cold_target)
        partial = lax.dot_general(
            place_cold, done["delta_cold"], (((0,), (0,)), ((), ())), preferred_element_type=jnp.float32
        )
        done["partial"] = partial + done["base_own"] + done["base_got"]

    between = {
        1: [cold_tokens_out, base_product],
        2: [base_over_tp],
        3: [cold_shrink, cold_over_tp],
        4: [cold_expand, cold_back, all_but_hot],
    }
    awaited = {1: ["hot_in", "base_own", "base_other"], 2: ["packet"], 3: ["z_cold", "base_got"]}
    for slot in range(chunk_count + len(hops) - 1):
        if slot > 0:
            if slot < chunk_count:
                mine[slot] = after(mine_all, chain.last)[slot * part:(slot + 1) * part]
                swapped[slot] = after(rest_swapped, chain.last)[(slot - 1) * part:slot * part]
            for stage in sorted(range(len(hops)), key=lambda stage: stage == 1):
                if 0 <= slot - stage < chunk_count:
                    send(slot - stage, stage)
        for work in between.get(slot, []):
            work()
        here = [(slot - stage, stage) for stage in range(len(hops)) if 0 <= slot - stage < chunk_count]
        names_here = awaited.get(slot, [])
        arrived = lax.optimization_barrier(
            (chain.last, *[got[at] for at in here], *[done[name] for name in names_here])
        )
        chain.last = arrived[0]
        got.update(zip(here, arrived[1:]))
        done.update(zip(names_here, arrived[1 + len(here):]))
    partial = done["partial"]

    hot_in = done["hot_in"].reshape(hot_rows, depth)
    dense = None
    for c in range(chunk_count):
        last = min((c + 1) * part, depth)
        for piece in (held[c], got[c, len(hops) - 1]):
            product = matmul(hot_in[:, c * part:last], piece[:last - c * part])
            dense = product if dense is None else dense + product
    dense = dense.reshape(group_count, near, HCAP, kept)
    at_step = jnp.arange(kept) // R
    z_part = sum(jnp.where(at_step == i, dense[:, i], 0.0) for i in range(near)).reshape(group_count * HCAP, kept)
    if lax.axis_size("tp") == 2:
        z_got = lax.ppermute(z_part, "tp", SWAP)
    else:
        z_part = lax.psum(z_part, "tp")
        z_got = jnp.zeros_like(z_part)
    delta_hot = hot_expand(z_part, z_got, (held[c], got[c, len(hops) - 1]), head_part).reshape(group_count, near * HCAP, head_part)
    delta_hot = lax.all_to_all(delta_hot, GROUP, split_axis=0, concat_axis=0, tiled=True)
    added = add_hot(partial, hot_target, delta_hot.reshape(hot_rows, head_part))
    return added.reshape(step_count, token_count, head_part)


def solution(mesh):
    tp_count, dp_count = mesh.shape["tp"], mesh.shape["dp"]
    fine = Mesh(mesh.devices.reshape(tp_count, dp_count // 8, 2, 2, 2), ("tp", *DP))
    placed = (
        P(None, DP, "tp"),
        P("tp", None),
        P("tp", DP),
        P(DP, "tp"),
        P(),
        P(None, DP),
        P(),
    )
    return jax.shard_map(
        on_device, mesh=fine, in_specs=placed, out_specs=P(None, DP, "tp"), check_vma=False
    )
```

```python
import jax
import jax.numpy as jnp
from jax import lax
from jax.experimental import pallas as pl
from jax.experimental.pallas import tpu as pltpu
from jax.sharding import Mesh, PartitionSpec as P

R = 64
CAP = 2
HCAP = 16
TAG = 128
DP = ("z_high", "z_low", "x", "core")
GROUP = ("z_low", "x", "core")
SWAP = [(0, 1), (1, 0)]


def pick(flags):
    return flags.astype(jnp.bfloat16)


def matmul(a, b):
    return jnp.dot(a, b, preferred_element_type=jnp.float32)


def narrow(a, b):
    return matmul(a, b).astype(jnp.bfloat16)


def sum_over_tp(part):
    if lax.axis_size("tp") == 2:
        return part + lax.ppermute(part, "tp", SWAP)
    return lax.psum(part, "tp")


def after(value, *others):
    return lax.optimization_barrier((value, *others))[0]


class Chain:
    def __init__(self):
        self.last = None

    def hold(self, value):
        self.last = value if self.last is None else after(value, self.last)
        return self.last

    def permute(self, value, axis, pairs):
        return lax.ppermute(self.hold(value), axis, pairs)

    def wait(self, *arrived):
        self.last = after(self.last, *arrived)


def kernel_params(flops=1, bytes_accessed=1):
    return dict(
        compiler_params=pltpu.CompilerParams(vmem_limit_bytes=40 * 2**20),
        cost_estimate=pl.CostEstimate(flops=flops, bytes_accessed=bytes_accessed, transcendentals=0),
    )


def pick_columns(store, expand, want_mine, want_other):
    depth, width = store.shape
    groups, lanes = want_mine.shape
    count = groups * lanes
    blocks = 8
    rows = depth // blocks

    def kernel(mine_held, other_held, mine_at, other_at, store_ref, expand_ref, mine_ref, first_ref, rest_ref, pick_mine, pick_other):
        step = pl.program_id(0)

        @pl.when(step == 0)
        def _():
            column = lax.broadcasted_iota(jnp.int32, (width, count), 0)
            pick_mine[...] = (column == mine_at[...]).astype(jnp.float32).astype(jnp.bfloat16)
            pick_other[...] = (column == other_at[...]).astype(jnp.float32).astype(jnp.bfloat16)

        def fill(out_ref, held, picker):
            for g in range(groups):
                at = slice(g * lanes, (g + 1) * lanes)

                @pl.when((held[g] > 0) & (step < blocks))
                def _():
                    out_ref[:, at] = narrow(store_ref[...], picker[:, at])

                @pl.when((held[g] > 0) & (step == blocks))
                def _():
                    product = lax.dot_general(
                        expand_ref[...], picker[:, at], (((0,), (0,)), ((), ())), preferred_element_type=jnp.float32
                    )
                    out_ref[:, at] = product.astype(jnp.bfloat16)

                @pl.when(held[g] == 0)
                def _():
                    out_ref[:, at] = jnp.zeros((rows, lanes), jnp.bfloat16)

        fill(mine_ref, mine_held, pick_mine)

        @pl.when(step < 3)
        def _():
            fill(first_ref, other_held, pick_other)

        @pl.when(step >= 3)
        def _():
            fill(rest_ref, other_held, pick_other)

    out = lambda thirds: jax.ShapeDtypeStruct((3 * rows * thirds, count), jnp.bfloat16)
    index = pl.BlockSpec((1, count), lambda i, *held: (0, 0))
    return pl.pallas_call(
        kernel,
        grid_spec=pltpu.PrefetchScalarGridSpec(
            num_scalar_prefetch=2,
            grid=(blocks + 1,),
            in_specs=[
                index,
                index,
                pl.BlockSpec((rows, width), lambda i, *held: (jnp.minimum(i, blocks - 1), 0)),
                pl.BlockSpec(expand.shape, lambda i, *held: (0, 0)),
            ],
            out_specs=[
                pl.BlockSpec((rows, count), lambda i, *held: (i, 0)),
                pl.BlockSpec((rows, count), lambda i, *held: (jnp.minimum(i, 2), 0)),
                pl.BlockSpec((rows, count), lambda i, *held: (jnp.maximum(i - 3, 0), 0)),
            ],
            scratch_shapes=[pltpu.VMEM((width, count), jnp.bfloat16)] * 2,
        ),
        out_shape=[out(3), out(1), out(2)],
        **kernel_params(),
    )(
        jnp.any(want_mine >= 0, axis=1).astype(jnp.int32),
        jnp.any(want_other >= 0, axis=1).astype(jnp.int32),
        want_mine.reshape(1, -1),
        want_other.reshape(1, -1),
        store,
        expand,
    )


def place_rows(rows, target, placed_rows):
    count, depth = rows.shape
    blocks = 4
    width = depth // blocks

    def kernel(target_at, rows_ref, out_ref, place):
        @pl.when(pl.program_id(0) == 0)
        def _():
            hit = lax.broadcasted_iota(jnp.int32, (placed_rows, count), 0) == target_at[...]
            place[...] = hit.astype(jnp.float32).astype(jnp.bfloat16)

        out_ref[...] = narrow(place[...], rows_ref[...])

    return pl.pallas_call(
        kernel,
        grid=(blocks,),
        in_specs=[pl.BlockSpec((1, count), lambda j: (0, 0)), pl.BlockSpec((count, width), lambda j: (0, j))],
        out_specs=pl.BlockSpec((placed_rows, width), lambda j: (0, j)),
        out_shape=jax.ShapeDtypeStruct((placed_rows, depth), jnp.bfloat16),
        scratch_shapes=[pltpu.VMEM((placed_rows, count), jnp.bfloat16)],
        **kernel_params(2 * placed_rows * count * depth, 2 * (placed_rows + count) * depth),
    )(target[None], rows)


def base_halves(rows, weight):
    count, depth = rows.shape
    width = weight.shape[1]
    half = width // 2
    blocks = 8
    part = depth // blocks

    def kernel(tp_at, rows_ref, weight_ref, own_ref, other_ref, total):
        step = pl.program_id(0)
        product = matmul(rows_ref[...], weight_ref[...])

        @pl.when(step == 0)
        def _():
            total[...] = product

        @pl.when(step > 0)
        def _():
            total[...] += product

        @pl.when(step == blocks - 1)
        def _():
            first = pl.multiple_of(tp_at[0] * half, 128)
            second = pl.multiple_of((1 - tp_at[0]) * half, 128)
            own_ref[...] = total[:, pl.ds(first, half)]
            other_ref[...] = total[:, pl.ds(second, half)]

    out = pl.BlockSpec((count, half), lambda k, at: (0, 0))
    return pl.pallas_call(
        kernel,
        grid_spec=pltpu.PrefetchScalarGridSpec(
            num_scalar_prefetch=1,
            grid=(blocks,),
            in_specs=[
                pl.BlockSpec((count, part), lambda k, at: (0, k)),
                pl.BlockSpec((part, width), lambda k, at: (k, 0)),
            ],
            out_specs=[out, out],
            scratch_shapes=[pltpu.VMEM((count, width), jnp.float32)],
        ),
        out_shape=[jax.ShapeDtypeStruct((count, half), jnp.float32)] * 2,
        **kernel_params(),
    )(lax.axis_index("tp").astype(jnp.int32)[None], rows, weight)


def hot_expand(z_own, z_got, factors, head):
    kept = factors[0].shape[1]
    near = kept // R
    count = z_own.shape[0] // HCAP

    def kernel(own_ref, got_ref, first_ref, second_ref, out_ref):
        z = (own_ref[...] + got_ref[...]).astype(jnp.bfloat16).astype(jnp.float32).reshape(count, 1, HCAP, kept)
        shape = (count, near, HCAP, kept)
        same = lax.broadcasted_iota(jnp.int32, shape, 3) // R == lax.broadcasted_iota(jnp.int32, shape, 1)
        spread = jnp.where(same, jnp.broadcast_to(z, shape), 0.0).astype(jnp.bfloat16)
        product = lax.dot_general(
            spread.reshape(count * near * HCAP, kept),
            first_ref[-head:] + second_ref[-head:],
            (((1,), (1,)), ((), ())),
            preferred_element_type=jnp.float32,
        )
        out_ref[...] = product.astype(jnp.bfloat16)

    return pl.pallas_call(
        kernel,
        out_shape=jax.ShapeDtypeStruct((count * near * HCAP, head), jnp.bfloat16),
        **kernel_params(),
    )(z_own, z_got, *factors)


def add_hot(partial, target, delta):
    count = partial.shape[0]
    hot_rows = delta.shape[0]

    def kernel(partial_ref, target_ref, delta_ref, out_ref):
        hit = lax.broadcasted_iota(jnp.int32, (count, hot_rows), 1) == target_ref[...]
        place = hit.astype(jnp.float32).astype(jnp.bfloat16)
        out_ref[...] = (partial_ref[...] + matmul(place, delta_ref[...])).astype(jnp.bfloat16)

    return pl.pallas_call(
        kernel,
        out_shape=jax.ShapeDtypeStruct(partial.shape, jnp.bfloat16),
        **kernel_params(),
    )(partial, target[:, None], delta)


def on_device(
    activations, value_weight, shrink_store, expand_store, adapter_row, token_adapter, hot_ids
):
    step_count, token_count, depth = activations.shape
    adapter_count = adapter_row.shape[0]
    hot_count = hot_ids.shape[1]
    per_dev = expand_store.shape[0] // R
    head_part = expand_store.shape[1]
    far_count = lax.axis_size("z_high")
    group_count = 8
    dp_count = far_count * group_count
    me = lax.axis_index(DP)
    z_at, x_at, core_at = lax.axis_index("z_low"), lax.axis_index("x"), lax.axis_index("core")
    none_code = adapter_count + hot_count
    rows = activations.reshape(step_count * token_count, depth)

    near = step_count // 2
    names = jnp.arange(adapter_count, dtype=jnp.int32)
    chain = Chain()

    cold_row = jnp.sum(jnp.where((token_adapter - hot_count)[:, :, None] == names, adapter_row, 0), axis=-1)
    is_hot = token_adapter < hot_count
    is_cold = (token_adapter < none_code) & jnp.logical_not(is_hot)
    owner = cold_row // per_dev
    group = jnp.where(is_hot, token_adapter, jnp.where(is_cold, hot_count + owner, -1))
    at = jnp.arange(token_count, dtype=jnp.int32)
    before = (group[:, :, None] == group[:, None, :]) & (at[None, :] < at[:, None])
    rank = jnp.sum(before.astype(jnp.int32), axis=-1)
    step_at = jnp.arange(step_count, dtype=jnp.int32)[:, None]
    hot_rows = hot_count * step_count * HCAP
    cold_rows = dp_count * step_count * CAP
    server = (step_at // near) * hot_count + token_adapter
    hot_target = (server * near + step_at % near) * HCAP + rank
    cold_target = (owner * step_count + step_at) * CAP + rank
    hot_target = jnp.where(is_hot, hot_target, -1).reshape(-1)
    cold_target = jnp.where(is_cold, cold_target, -1).reshape(-1)

    hot_out = place_rows(rows, hot_target, hot_rows)
    hot_out = chain.hold(hot_out.reshape(group_count, near * HCAP, depth))
    done = {"hot_in": lax.all_to_all(hot_out, GROUP, split_axis=0, concat_axis=0, tiled=True)}

    hot_row = jnp.sum(jnp.where(hot_ids[:, :, None] == names, adapter_row, 0), axis=-1)
    hot_first = jnp.where(hot_row // per_dev == me, (hot_row % per_dev) * R, -R * per_dev)
    column = jnp.arange(per_dev * R, dtype=jnp.int32)
    lane = jnp.arange(R, dtype=jnp.int32)
    entry = jnp.arange(hot_count, dtype=jnp.int32)

    def wanted(core):
        firsts = []
        for x in (x_at, 1 - x_at):
            of_steps = jnp.sum(jnp.where(entry == 2 * x + core, hot_first, 0), axis=1)
            firsts += [jnp.where(z_at == 0, of_steps[:near], of_steps[near:])]
            firsts += [jnp.where(z_at == 0, of_steps[near:], of_steps[:near])]
        return jnp.stack([(f[:, None] + lane).reshape(-1) for f in firsts])

    want_mine, want_other = wanted(core_at), wanted(1 - core_at)
    kept = near * R
    chunk_count = 3
    part = (depth + head_part) // chunk_count

    hops = [("x", SWAP), ("z_low", SWAP)]
    bit = 1
    while bit < far_count:
        hops.append(("z_high", [(i, i ^ bit) for i in range(far_count)]))
        bit *= 2
    mine, swapped, got, held = {}, {}, {}, {}

    def operand(c, stage):
        if stage == 0:
            return mine[c][:, 2 * kept:] + swapped[c][:, 2 * kept:]
        if stage == 1:
            return mine[c][:, kept:2 * kept] + swapped[c][:, kept:2 * kept] + got[c, 0][:, kept:]
        if stage == 2:
            held[c] = mine[c][:, :kept] + swapped[c][:, :kept] + got[c, 0][:, :kept] + got[c, 1]
        else:
            held[c] = held[c] + got[c, stage - 1]
        return held[c]

    def send(c, stage):
        got[c, stage] = chain.permute(operand(c, stage), *hops[stage])

    mine_all, other_first, other_rest = pick_columns(
        after(shrink_store, chain.last), expand_store, want_mine, want_other
    )
    mine[0], swapped[0] = mine_all[:part], chain.permute(other_first, "core", SWAP)
    rest_swapped = chain.permute(other_rest, "core", SWAP)
    send(0, 0)

    def cold_tokens_out():
        cold_at = after(cold_target, chain.last)
        cold_hit = jnp.arange(cold_rows, dtype=jnp.int32)[:, None] == cold_at
        tag = jnp.sum(jnp.where(cold_hit, (cold_row % per_dev + 1).reshape(-1), 0), axis=-1)
        tag = jnp.broadcast_to(tag.astype(jnp.bfloat16)[:, None], (cold_rows, TAG))
        packet = jnp.concatenate([narrow(pick(cold_hit), rows), tag], axis=1)
        packet = chain.hold(packet.reshape(dp_count, step_count * CAP, depth + TAG))
        packet = lax.all_to_all(packet, DP, split_axis=0, concat_axis=0, tiled=True)
        done["packet"] = packet.reshape(cold_rows, depth + TAG)

    def base_product():
        weight = after(value_weight, chain.last)
        if lax.axis_size("tp") == 2:
            done["base_own"], done["base_other"] = base_halves(rows, weight)
        else:
            done["base_own"], done["base_other"] = jnp.zeros((1, 1), jnp.float32), matmul(rows, weight)

    def base_over_tp():
        if lax.axis_size("tp") == 2:
            done["base_got"] = chain.permute(done["base_other"], "tp", SWAP)
        else:
            whole = chain.hold(done["base_other"])
            done["base_got"] = lax.psum_scatter(whole, "tp", scatter_dimension=1, tiled=True)

    def cold_shrink():
        tag_in = done["packet"][:, depth:depth + 1].astype(jnp.int32)
        chosen = (column // R + 1)[None, :] == tag_in
        product = matmul(done["packet"][:, :depth], after(shrink_store, chain.last))
        done["z_part"] = jnp.where(chosen, product, 0.0)

    def cold_over_tp():
        done["z_cold"] = sum_over_tp(chain.hold(done["z_part"]))

    def cold_expand():
        done["delta"] = narrow(done["z_cold"].astype(jnp.bfloat16), after(expand_store, chain.last))

    def cold_back():
        delta = chain.hold(done["delta"].reshape(dp_count, step_count * CAP, head_part))
        delta = lax.all_to_all(delta, DP, split_axis=0, concat_axis=0, tiled=True)
        done["delta_cold"] = delta.reshape(cold_rows, head_part)

    def all_but_hot():
        place_cold = pick(jnp.arange(cold_rows, dtype=jnp.int32)[:, None] == cold_target)
        partial = lax.dot_general(
            place_cold, done["delta_cold"], (((0,), (0,)), ((), ())), preferred_element_type=jnp.float32
        )
        done["partial"] = partial + done["base_own"] + done["base_got"]

    between = {
        0: [cold_tokens_out, base_product],
        2: [base_over_tp],
        3: [cold_shrink, cold_over_tp],
        4: [cold_expand, cold_back, all_but_hot],
    }
    awaited = {0: ["base_own", "base_other"], 2: ["packet"], 3: ["z_cold", "base_got"]}
    for slot in range(chunk_count + len(hops) - 1):
        if slot > 0:
            if slot < chunk_count:
                mine[slot] = after(mine_all, chain.last)[slot * part:(slot + 1) * part]
                swapped[slot] = after(rest_swapped, chain.last)[(slot - 1) * part:slot * part]
            for stage in sorted(range(len(hops)), key=lambda stage: stage == 1):
                if 0 <= slot - stage < chunk_count:
                    send(slot - stage, stage)
        for work in between.get(slot, []):
            work()
        here = [(slot - stage, stage) for stage in range(len(hops)) if 0 <= slot - stage < chunk_count]
        names_here = awaited.get(slot, [])
        arrived = lax.optimization_barrier(
            (chain.last, *[got[at] for at in here], *[done[name] for name in names_here])
        )
        chain.last = arrived[0]
        got.update(zip(here, arrived[1:]))
        done.update(zip(names_here, arrived[1 + len(here):]))
    partial = done["partial"]

    hot_in = done["hot_in"].reshape(hot_rows, depth)
    dense = None
    for c in range(chunk_count):
        last = min((c + 1) * part, depth)
        for piece in (held[c], got[c, len(hops) - 1]):
            product = matmul(hot_in[:, c * part:last], piece[:last - c * part])
            dense = product if dense is None else dense + product
    dense = dense.reshape(group_count, near, HCAP, kept)
    at_step = jnp.arange(kept) // R
    z_part = sum(jnp.where(at_step == i, dense[:, i], 0.0) for i in range(near)).reshape(group_count * HCAP, kept)
    if lax.axis_size("tp") == 2:
        z_got = lax.ppermute(z_part, "tp", SWAP)
    else:
        z_part = lax.psum(z_part, "tp")
        z_got = jnp.zeros_like(z_part)
    delta_hot = hot_expand(z_part, z_got, (held[c], got[c, len(hops) - 1]), head_part).reshape(group_count, near * HCAP, head_part)
    delta_hot = lax.all_to_all(delta_hot, GROUP, split_axis=0, concat_axis=0, tiled=True)
    added = add_hot(partial, hot_target, delta_hot.reshape(hot_rows, head_part))
    return added.reshape(step_count, token_count, head_part)


def solution(mesh):
    tp_count, dp_count = mesh.shape["tp"], mesh.shape["dp"]
    fine = Mesh(mesh.devices.reshape(tp_count, dp_count // 8, 2, 2, 2), ("tp", *DP))
    placed = (
        P(None, DP, "tp"),
        P("tp", None),
        P("tp", DP),
        P(DP, "tp"),
        P(),
        P(None, DP),
        P(),
    )
    return jax.shard_map(
        on_device, mesh=fine, in_specs=placed, out_specs=P(None, DP, "tp"), check_vma=False
    )
```

```python
import jax
import jax.numpy as jnp
from jax import lax
from jax.experimental import pallas as pl
from jax.experimental.pallas import tpu as pltpu
from jax.sharding import Mesh, PartitionSpec as P

R = 64
CAP = 2
HCAP = 16
TAG = 128
DP = ("z_high", "z_low", "x", "core")
GROUP = ("z_low", "x", "core")
SWAP = [(0, 1), (1, 0)]


def pick(flags):
    return flags.astype(jnp.bfloat16)


def matmul(a, b):
    return jnp.dot(a, b, preferred_element_type=jnp.float32)


def narrow(a, b):
    return matmul(a, b).astype(jnp.bfloat16)


def sum_over_tp(part):
    if lax.axis_size("tp") == 2:
        return part + lax.ppermute(part, "tp", SWAP)
    return lax.psum(part, "tp")


def after(value, *others):
    return lax.optimization_barrier((value, *others))[0]


class Chain:
    def __init__(self):
        self.last = None

    def hold(self, value):
        self.last = value if self.last is None else after(value, self.last)
        return self.last

    def permute(self, value, axis, pairs):
        return lax.ppermute(self.hold(value), axis, pairs)

    def wait(self, *arrived):
        self.last = after(self.last, *arrived)


def kernel_params():
    return dict(
        compiler_params=pltpu.CompilerParams(vmem_limit_bytes=40 * 2**20),
        cost_estimate=pl.CostEstimate(flops=1, bytes_accessed=1, transcendentals=0),
    )


def pick_columns(store, expand, want_mine, want_other):
    depth, width = store.shape
    groups, lanes = want_mine.shape
    count = groups * lanes
    blocks = 8
    rows = depth // blocks

    def kernel(mine_held, other_held, mine_at, other_at, store_ref, expand_ref, mine_ref, first_ref, rest_ref, pick_mine, pick_other):
        step = pl.program_id(0)

        @pl.when(step == 0)
        def _():
            column = lax.broadcasted_iota(jnp.int32, (width, count), 0)
            pick_mine[...] = (column == mine_at[...]).astype(jnp.float32).astype(jnp.bfloat16)
            pick_other[...] = (column == other_at[...]).astype(jnp.float32).astype(jnp.bfloat16)

        def fill(out_ref, held, picker):
            for g in range(groups):
                at = slice(g * lanes, (g + 1) * lanes)

                @pl.when((held[g] > 0) & (step < blocks))
                def _():
                    out_ref[:, at] = narrow(store_ref[...], picker[:, at])

                @pl.when((held[g] > 0) & (step == blocks))
                def _():
                    product = lax.dot_general(
                        expand_ref[...], picker[:, at], (((0,), (0,)), ((), ())), preferred_element_type=jnp.float32
                    )
                    out_ref[:, at] = product.astype(jnp.bfloat16)

                @pl.when(held[g] == 0)
                def _():
                    out_ref[:, at] = jnp.zeros((rows, lanes), jnp.bfloat16)

        fill(mine_ref, mine_held, pick_mine)

        @pl.when(step < 3)
        def _():
            fill(first_ref, other_held, pick_other)

        @pl.when(step >= 3)
        def _():
            fill(rest_ref, other_held, pick_other)

    out = lambda thirds: jax.ShapeDtypeStruct((3 * rows * thirds, count), jnp.bfloat16)
    index = pl.BlockSpec((1, count), lambda i, *held: (0, 0))
    return pl.pallas_call(
        kernel,
        grid_spec=pltpu.PrefetchScalarGridSpec(
            num_scalar_prefetch=2,
            grid=(blocks + 1,),
            in_specs=[
                index,
                index,
                pl.BlockSpec((rows, width), lambda i, *held: (jnp.minimum(i, blocks - 1), 0)),
                pl.BlockSpec(expand.shape, lambda i, *held: (0, 0)),
            ],
            out_specs=[
                pl.BlockSpec((rows, count), lambda i, *held: (i, 0)),
                pl.BlockSpec((rows, count), lambda i, *held: (jnp.minimum(i, 2), 0)),
                pl.BlockSpec((rows, count), lambda i, *held: (jnp.maximum(i - 3, 0), 0)),
            ],
            scratch_shapes=[pltpu.VMEM((width, count), jnp.bfloat16)] * 2,
        ),
        out_shape=[out(3), out(1), out(2)],
        **kernel_params(),
    )(
        jnp.any(want_mine >= 0, axis=1).astype(jnp.int32),
        jnp.any(want_other >= 0, axis=1).astype(jnp.int32),
        want_mine.reshape(1, -1),
        want_other.reshape(1, -1),
        store,
        expand,
    )


def place_rows(rows, target, placed_rows):
    count, depth = rows.shape
    blocks = 4
    width = depth // blocks

    def kernel(target_at, rows_ref, early_ref, late_ref, place):
        step = pl.program_id(0)

        @pl.when(step == 0)
        def _():
            hit = lax.broadcasted_iota(jnp.int32, (placed_rows, count), 0) == target_at[...]
            place[...] = hit.astype(jnp.float32).astype(jnp.bfloat16)

        placed = narrow(place[...], rows_ref[...])

        @pl.when(step < blocks - 1)
        def _():
            early_ref[...] = placed

        @pl.when(step == blocks - 1)
        def _():
            late_ref[...] = placed

    return pl.pallas_call(
        kernel,
        grid=(blocks,),
        in_specs=[pl.BlockSpec((1, count), lambda j: (0, 0)), pl.BlockSpec((count, width), lambda j: (0, j))],
        out_specs=[
            pl.BlockSpec((placed_rows, width), lambda j: (0, jnp.minimum(j, blocks - 2))),
            pl.BlockSpec((placed_rows, width), lambda j: (0, 0)),
        ],
        out_shape=[
            jax.ShapeDtypeStruct((placed_rows, depth - width), jnp.bfloat16),
            jax.ShapeDtypeStruct((placed_rows, width), jnp.bfloat16),
        ],
        scratch_shapes=[pltpu.VMEM((placed_rows, count), jnp.bfloat16)],
        **kernel_params(),
    )(target[None], rows)


def base_halves(rows, weight):
    count, depth = rows.shape
    width = weight.shape[1]
    half = width // 2
    blocks = 8
    part = depth // blocks

    def kernel(tp_at, rows_ref, weight_ref, own_ref, other_ref, total):
        step = pl.program_id(0)
        product = matmul(rows_ref[...], weight_ref[...])

        @pl.when(step == 0)
        def _():
            total[...] = product

        @pl.when(step > 0)
        def _():
            total[...] += product

        @pl.when(step == blocks - 1)
        def _():
            first = pl.multiple_of(tp_at[0] * half, 128)
            second = pl.multiple_of((1 - tp_at[0]) * half, 128)
            own_ref[...] = total[:, pl.ds(first, half)]
            other_ref[...] = total[:, pl.ds(second, half)]

    out = pl.BlockSpec((count, half), lambda k, at: (0, 0))
    return pl.pallas_call(
        kernel,
        grid_spec=pltpu.PrefetchScalarGridSpec(
            num_scalar_prefetch=1,
            grid=(blocks,),
            in_specs=[
                pl.BlockSpec((count, part), lambda k, at: (0, k)),
                pl.BlockSpec((part, width), lambda k, at: (k, 0)),
            ],
            out_specs=[out, out],
            scratch_shapes=[pltpu.VMEM((count, width), jnp.float32)],
        ),
        out_shape=[jax.ShapeDtypeStruct((count, half), jnp.float32)] * 2,
        **kernel_params(),
    )(lax.axis_index("tp").astype(jnp.int32)[None], rows, weight)


def hot_expand(z_own, z_got, factors, head):
    kept = factors[0].shape[1]
    near = kept // R
    count = z_own.shape[0] // HCAP

    def kernel(own_ref, got_ref, first_ref, second_ref, out_ref):
        z = (own_ref[...] + got_ref[...]).astype(jnp.bfloat16).astype(jnp.float32).reshape(count, 1, HCAP, kept)
        shape = (count, near, HCAP, kept)
        same = lax.broadcasted_iota(jnp.int32, shape, 3) // R == lax.broadcasted_iota(jnp.int32, shape, 1)
        spread = jnp.where(same, jnp.broadcast_to(z, shape), 0.0).astype(jnp.bfloat16)
        product = lax.dot_general(
            spread.reshape(count * near * HCAP, kept),
            first_ref[-head:] + second_ref[-head:],
            (((1,), (1,)), ((), ())),
            preferred_element_type=jnp.float32,
        )
        out_ref[...] = product.astype(jnp.bfloat16)

    return pl.pallas_call(
        kernel,
        out_shape=jax.ShapeDtypeStruct((count * near * HCAP, head), jnp.bfloat16),
        **kernel_params(),
    )(z_own, z_got, *factors)


def add_hot(partial, target, delta):
    count = partial.shape[0]
    hot_rows = delta.shape[0]

    def kernel(partial_ref, target_ref, delta_ref, out_ref):
        hit = lax.broadcasted_iota(jnp.int32, (count, hot_rows), 1) == target_ref[...]
        place = hit.astype(jnp.float32).astype(jnp.bfloat16)
        out_ref[...] = (partial_ref[...] + matmul(place, delta_ref[...])).astype(jnp.bfloat16)

    return pl.pallas_call(
        kernel,
        out_shape=jax.ShapeDtypeStruct(partial.shape, jnp.bfloat16),
        **kernel_params(),
    )(partial, target[:, None], delta)


def on_device(
    activations, value_weight, shrink_store, expand_store, adapter_row, token_adapter, hot_ids
):
    step_count, token_count, depth = activations.shape
    adapter_count = adapter_row.shape[0]
    hot_count = hot_ids.shape[1]
    per_dev = expand_store.shape[0] // R
    head_part = expand_store.shape[1]
    far_count = lax.axis_size("z_high")
    group_count = 8
    dp_count = far_count * group_count
    me = lax.axis_index(DP)
    z_at, x_at, core_at = lax.axis_index("z_low"), lax.axis_index("x"), lax.axis_index("core")
    none_code = adapter_count + hot_count
    rows = activations.reshape(step_count * token_count, depth)

    near = step_count // 2
    names = jnp.arange(adapter_count, dtype=jnp.int32)
    chain = Chain()

    cold_row = jnp.sum(jnp.where((token_adapter - hot_count)[:, :, None] == names, adapter_row, 0), axis=-1)
    is_hot = token_adapter < hot_count
    is_cold = (token_adapter < none_code) & jnp.logical_not(is_hot)
    owner = cold_row // per_dev
    group = jnp.where(is_hot, token_adapter, jnp.where(is_cold, hot_count + owner, -1))
    at = jnp.arange(token_count, dtype=jnp.int32)
    before = (group[:, :, None] == group[:, None, :]) & (at[None, :] < at[:, None])
    rank = jnp.sum(before.astype(jnp.int32), axis=-1)
    step_at = jnp.arange(step_count, dtype=jnp.int32)[:, None]
    hot_rows = hot_count * step_count * HCAP
    cold_rows = dp_count * step_count * CAP
    server = (step_at // near) * hot_count + token_adapter
    hot_target = (server * near + step_at % near) * HCAP + rank
    cold_target = (owner * step_count + step_at) * CAP + rank
    hot_target = jnp.where(is_hot, hot_target, -1).reshape(-1)
    cold_target = jnp.where(is_cold, cold_target, -1).reshape(-1)

    early = 3 * depth // 4

    def exchange(block):
        block = chain.hold(block.reshape(group_count, near * HCAP, -1))
        return lax.all_to_all(block, GROUP, split_axis=0, concat_axis=0, tiled=True).reshape(hot_rows, -1)

    hot_first_part, hot_last_part = place_rows(rows, hot_target, hot_rows)
    hot_early = exchange(hot_first_part)

    hot_row = jnp.sum(jnp.where(hot_ids[:, :, None] == names, adapter_row, 0), axis=-1)
    hot_first = jnp.where(hot_row // per_dev == me, (hot_row % per_dev) * R, -R * per_dev)
    column = jnp.arange(per_dev * R, dtype=jnp.int32)
    lane = jnp.arange(R, dtype=jnp.int32)
    entry = jnp.arange(hot_count, dtype=jnp.int32)

    def wanted(core):
        firsts = []
        for x in (x_at, 1 - x_at):
            of_steps = jnp.sum(jnp.where(entry == 2 * x + core, hot_first, 0), axis=1)
            firsts += [jnp.where(z_at == 0, of_steps[:near], of_steps[near:])]
            firsts += [jnp.where(z_at == 0, of_steps[near:], of_steps[:near])]
        return jnp.stack([(f[:, None] + lane).reshape(-1) for f in firsts])

    want_mine, want_other = wanted(core_at), wanted(1 - core_at)
    kept = near * R
    chunk_count = 3
    part = (depth + head_part) // chunk_count

    hops = [("x", SWAP), ("z_low", SWAP)]
    bit = 1
    while bit < far_count:
        hops.append(("z_high", [(i, i ^ bit) for i in range(far_count)]))
        bit *= 2
    mine, swapped, got, held = {}, {}, {}, {}

    def operand(c, stage):
        if stage == 0:
            return mine[c][:, 2 * kept:] + swapped[c][:, 2 * kept:]
        if stage == 1:
            return mine[c][:, kept:2 * kept] + swapped[c][:, kept:2 * kept] + got[c, 0][:, kept:]
        if stage == 2:
            held[c] = mine[c][:, :kept] + swapped[c][:, :kept] + got[c, 0][:, :kept] + got[c, 1]
        else:
            held[c] = held[c] + got[c, stage - 1]
        return held[c]

    def send(c, stage):
        got[c, stage] = chain.permute(operand(c, stage), *hops[stage])

    mine_all, other_first, other_rest = pick_columns(
        after(shrink_store, chain.last), expand_store, want_mine, want_other
    )
    mine[0], swapped[0] = mine_all[:part], chain.permute(other_first, "core", SWAP)
    rest_swapped = chain.permute(other_rest, "core", SWAP)
    first, hot_early = lax.optimization_barrier((operand(0, 0), hot_early))
    got[0, 0] = chain.permute(first, *hops[0])
    done = {"hot_late": exchange(hot_last_part)}

    def cold_tokens_out():
        cold_at = after(cold_target, chain.last)
        cold_hit = jnp.arange(cold_rows, dtype=jnp.int32)[:, None] == cold_at
        tag = jnp.sum(jnp.where(cold_hit, (cold_row % per_dev + 1).reshape(-1), 0), axis=-1)
        tag = jnp.broadcast_to(tag.astype(jnp.bfloat16)[:, None], (cold_rows, TAG))
        packet = jnp.concatenate([narrow(pick(cold_hit), rows), tag], axis=1)
        packet = chain.hold(packet.reshape(dp_count, step_count * CAP, depth + TAG))
        packet = lax.all_to_all(packet, DP, split_axis=0, concat_axis=0, tiled=True)
        done["packet"] = packet.reshape(cold_rows, depth + TAG)

    def base_product():
        weight = after(value_weight, chain.last)
        if lax.axis_size("tp") == 2:
            done["base_own"], done["base_other"] = base_halves(rows, weight)
        else:
            done["base_own"], done["base_other"] = jnp.zeros((1, 1), jnp.float32), matmul(rows, weight)

    def base_over_tp():
        if lax.axis_size("tp") == 2:
            done["base_got"] = chain.permute(done["base_other"], "tp", SWAP)
        else:
            whole = chain.hold(done["base_other"])
            done["base_got"] = lax.psum_scatter(whole, "tp", scatter_dimension=1, tiled=True)

    def cold_shrink():
        tag_in = done["packet"][:, depth:depth + 1].astype(jnp.int32)
        chosen = (column // R + 1)[None, :] == tag_in
        product = matmul(done["packet"][:, :depth], after(shrink_store, chain.last))
        done["z_part"] = jnp.where(chosen, product, 0.0)

    def cold_over_tp():
        done["z_cold"] = sum_over_tp(chain.hold(done["z_part"]))

    def cold_expand():
        done["delta"] = narrow(done["z_cold"].astype(jnp.bfloat16), after(expand_store, chain.last))

    def cold_back():
        delta = chain.hold(done["delta"].reshape(dp_count, step_count * CAP, head_part))
        delta = lax.all_to_all(delta, DP, split_axis=0, concat_axis=0, tiled=True)
        done["delta_cold"] = delta.reshape(cold_rows, head_part)

    def all_but_hot():
        place_cold = pick(jnp.arange(cold_rows, dtype=jnp.int32)[:, None] == cold_target)
        partial = lax.dot_general(
            place_cold, done["delta_cold"], (((0,), (0,)), ((), ())), preferred_element_type=jnp.float32
        )
        done["partial"] = partial + done["base_own"] + done["base_got"]

    between = {
        1: [cold_tokens_out, base_product],
        2: [base_over_tp],
        3: [cold_shrink, cold_over_tp],
        4: [cold_expand, cold_back, all_but_hot],
    }
    awaited = {1: ["hot_late", "base_own", "base_other"], 2: ["packet"], 3: ["z_cold", "base_got"]}
    for slot in range(chunk_count + len(hops) - 1):
        if slot > 0:
            if slot < chunk_count:
                mine[slot] = after(mine_all, chain.last)[slot * part:(slot + 1) * part]
                swapped[slot] = after(rest_swapped, chain.last)[(slot - 1) * part:slot * part]
            for stage in sorted(range(len(hops)), key=lambda stage: stage == 1):
                if 0 <= slot - stage < chunk_count:
                    send(slot - stage, stage)
        for work in between.get(slot, []):
            work()
        here = [(slot - stage, stage) for stage in range(len(hops)) if 0 <= slot - stage < chunk_count]
        names_here = awaited.get(slot, [])
        arrived = lax.optimization_barrier(
            (chain.last, *[got[at] for at in here], *[done[name] for name in names_here])
        )
        chain.last = arrived[0]
        got.update(zip(here, arrived[1:]))
        done.update(zip(names_here, arrived[1 + len(here):]))
    partial = done["partial"]

    dense = None
    for c in range(chunk_count):
        last = min((c + 1) * part, depth)
        hot_in = hot_early[:, c * part:last] if last <= early else done["hot_late"]
        for piece in (held[c], got[c, len(hops) - 1]):
            product = matmul(hot_in, piece[:last - c * part])
            dense = product if dense is None else dense + product
    dense = dense.reshape(group_count, near, HCAP, kept)
    at_step = jnp.arange(kept) // R
    z_part = sum(jnp.where(at_step == i, dense[:, i], 0.0) for i in range(near)).reshape(group_count * HCAP, kept)
    if lax.axis_size("tp") == 2:
        z_got = lax.ppermute(z_part, "tp", SWAP)
    else:
        z_part = lax.psum(z_part, "tp")
        z_got = jnp.zeros_like(z_part)
    delta_hot = hot_expand(z_part, z_got, (held[c], got[c, len(hops) - 1]), head_part).reshape(group_count, near * HCAP, head_part)
    delta_hot = lax.all_to_all(delta_hot, GROUP, split_axis=0, concat_axis=0, tiled=True)
    added = add_hot(partial, hot_target, delta_hot.reshape(hot_rows, head_part))
    return added.reshape(step_count, token_count, head_part)


def solution(mesh):
    tp_count, dp_count = mesh.shape["tp"], mesh.shape["dp"]
    fine = Mesh(mesh.devices.reshape(tp_count, dp_count // 8, 2, 2, 2), ("tp", *DP))
    placed = (
        P(None, DP, "tp"),
        P("tp", None),
        P("tp", DP),
        P(DP, "tp"),
        P(),
        P(None, DP),
        P(),
    )
    return jax.shard_map(
        on_device, mesh=fine, in_specs=placed, out_specs=P(None, DP, "tp"), check_vma=False
    )
```

```python
import jax
import jax.numpy as jnp
from jax import lax
from jax.experimental import pallas as pl
from jax.experimental.pallas import tpu as pltpu
from jax.sharding import Mesh, PartitionSpec as P

R = 64
CAP = 2
HCAP = 16
TAG = 128
DP = ("z_high", "z_low", "x", "core")
GROUP = ("z_low", "x", "core")
SWAP = [(0, 1), (1, 0)]


def pick(flags):
    return flags.astype(jnp.bfloat16)


def matmul(a, b):
    return jnp.dot(a, b, preferred_element_type=jnp.float32)


def narrow(a, b):
    return matmul(a, b).astype(jnp.bfloat16)


def sum_over_tp(part):
    if lax.axis_size("tp") == 2:
        return part + lax.ppermute(part, "tp", SWAP)
    return lax.psum(part, "tp")


def after(value, *others):
    return lax.optimization_barrier((value, *others))[0]


class Chain:
    def __init__(self):
        self.last = None

    def hold(self, value):
        self.last = value if self.last is None else after(value, self.last)
        return self.last

    def permute(self, value, axis, pairs):
        return lax.ppermute(self.hold(value), axis, pairs)

    def wait(self, *arrived):
        self.last = after(self.last, *arrived)


def kernel_params():
    return dict(
        compiler_params=pltpu.CompilerParams(vmem_limit_bytes=40 * 2**20),
        cost_estimate=pl.CostEstimate(flops=1, bytes_accessed=1, transcendentals=0),
    )


def pick_columns(store, expand, want_mine, want_other):
    depth, width = store.shape
    groups, lanes = want_mine.shape
    count = groups * lanes
    blocks = 8
    rows = depth // blocks

    def kernel(mine_held, other_held, mine_at, other_at, store_ref, expand_ref, mine_ref, first_ref, rest_ref, pick_mine, pick_other):
        step = pl.program_id(0)

        @pl.when(step == 0)
        def _():
            column = lax.broadcasted_iota(jnp.int32, (width, count), 0)
            pick_mine[...] = (column == mine_at[...]).astype(jnp.float32).astype(jnp.bfloat16)
            pick_other[...] = (column == other_at[...]).astype(jnp.float32).astype(jnp.bfloat16)

        def fill(out_ref, held, picker):
            for g in range(groups):
                at = slice(g * lanes, (g + 1) * lanes)

                @pl.when((held[g] > 0) & (step < blocks))
                def _():
                    out_ref[:, at] = narrow(store_ref[...], picker[:, at])

                @pl.when((held[g] > 0) & (step == blocks))
                def _():
                    product = lax.dot_general(
                        expand_ref[...], picker[:, at], (((0,), (0,)), ((), ())), preferred_element_type=jnp.float32
                    )
                    out_ref[:, at] = product.astype(jnp.bfloat16)

                @pl.when(held[g] == 0)
                def _():
                    out_ref[:, at] = jnp.zeros((rows, lanes), jnp.bfloat16)

        fill(mine_ref, mine_held, pick_mine)

        @pl.when(step < 3)
        def _():
            fill(first_ref, other_held, pick_other)

        @pl.when(step >= 3)
        def _():
            fill(rest_ref, other_held, pick_other)

    out = lambda thirds: jax.ShapeDtypeStruct((3 * rows * thirds, count), jnp.bfloat16)
    index = pl.BlockSpec((1, count), lambda i, *held: (0, 0))
    return pl.pallas_call(
        kernel,
        grid_spec=pltpu.PrefetchScalarGridSpec(
            num_scalar_prefetch=2,
            grid=(blocks + 1,),
            in_specs=[
                index,
                index,
                pl.BlockSpec((rows, width), lambda i, *held: (jnp.minimum(i, blocks - 1), 0)),
                pl.BlockSpec(expand.shape, lambda i, *held: (0, 0)),
            ],
            out_specs=[
                pl.BlockSpec((rows, count), lambda i, *held: (i, 0)),
                pl.BlockSpec((rows, count), lambda i, *held: (jnp.minimum(i, 2), 0)),
                pl.BlockSpec((rows, count), lambda i, *held: (jnp.maximum(i - 3, 0), 0)),
            ],
            scratch_shapes=[pltpu.VMEM((width, count), jnp.bfloat16)] * 2,
        ),
        out_shape=[out(3), out(1), out(2)],
        **kernel_params(),
    )(
        jnp.any(want_mine >= 0, axis=1).astype(jnp.int32),
        jnp.any(want_other >= 0, axis=1).astype(jnp.int32),
        want_mine.reshape(1, -1),
        want_other.reshape(1, -1),
        store,
        expand,
    )


def place_rows(rows, hot_target, cold_target, tag, hot_rows, cold_rows):
    count, depth = rows.shape
    blocks = 4
    width = depth // blocks

    def kernel(hot_at, cold_at, tag_at, rows_ref, early_ref, late_ref, cold_ref, place_hot, place_cold):
        step = pl.program_id(0)

        @pl.when(step == 0)
        def _():
            hot_hit = lax.broadcasted_iota(jnp.int32, (hot_rows, count), 0) == hot_at[...]
            cold_hit = lax.broadcasted_iota(jnp.int32, (cold_rows, count), 0) == cold_at[...]
            place_hot[...] = hot_hit.astype(jnp.float32).astype(jnp.bfloat16)
            place_cold[...] = cold_hit.astype(jnp.float32).astype(jnp.bfloat16)
            tags = jnp.sum(jnp.where(cold_hit, tag_at[...].astype(jnp.float32), 0.0), axis=1, keepdims=True)
            cold_ref[:, depth:] = jnp.broadcast_to(tags, (cold_rows, TAG)).astype(jnp.bfloat16)

        block = rows_ref[...]
        placed = narrow(place_hot[...], block)
        cold_ref[:, pl.ds(pl.multiple_of(step * width, 128), width)] = narrow(place_cold[...], block)

        @pl.when(step < blocks - 1)
        def _():
            early_ref[...] = placed

        @pl.when(step == blocks - 1)
        def _():
            late_ref[...] = placed

    index = pl.BlockSpec((1, count), lambda j: (0, 0))
    return pl.pallas_call(
        kernel,
        grid=(blocks,),
        in_specs=[index, index, index, pl.BlockSpec((count, width), lambda j: (0, j))],
        out_specs=[
            pl.BlockSpec((hot_rows, width), lambda j: (0, jnp.minimum(j, blocks - 2))),
            pl.BlockSpec((hot_rows, width), lambda j: (0, 0)),
            pl.BlockSpec((cold_rows, depth + TAG), lambda j: (0, 0)),
        ],
        out_shape=[
            jax.ShapeDtypeStruct((hot_rows, depth - width), jnp.bfloat16),
            jax.ShapeDtypeStruct((hot_rows, width), jnp.bfloat16),
            jax.ShapeDtypeStruct((cold_rows, depth + TAG), jnp.bfloat16),
        ],
        scratch_shapes=[pltpu.VMEM((hot_rows, count), jnp.bfloat16), pltpu.VMEM((cold_rows, count), jnp.bfloat16)],
        **kernel_params(),
    )(hot_target[None], cold_target[None], tag[None], rows)


def base_halves(rows, weight):
    count, depth = rows.shape
    width = weight.shape[1]
    half = width // 2
    blocks = 8
    part = depth // blocks

    def kernel(tp_at, rows_ref, weight_ref, own_ref, other_ref, total):
        step = pl.program_id(0)
        product = matmul(rows_ref[...], weight_ref[...])

        @pl.when(step == 0)
        def _():
            total[...] = product

        @pl.when(step > 0)
        def _():
            total[...] += product

        @pl.when(step == blocks - 1)
        def _():
            first = pl.multiple_of(tp_at[0] * half, 128)
            second = pl.multiple_of((1 - tp_at[0]) * half, 128)
            own_ref[...] = total[:, pl.ds(first, half)]
            other_ref[...] = total[:, pl.ds(second, half)]

    out = pl.BlockSpec((count, half), lambda k, at: (0, 0))
    return pl.pallas_call(
        kernel,
        grid_spec=pltpu.PrefetchScalarGridSpec(
            num_scalar_prefetch=1,
            grid=(blocks,),
            in_specs=[
                pl.BlockSpec((count, part), lambda k, at: (0, k)),
                pl.BlockSpec((part, width), lambda k, at: (k, 0)),
            ],
            out_specs=[out, out],
            scratch_shapes=[pltpu.VMEM((count, width), jnp.float32)],
        ),
        out_shape=[jax.ShapeDtypeStruct((count, half), jnp.float32)] * 2,
        **kernel_params(),
    )(lax.axis_index("tp").astype(jnp.int32)[None], rows, weight)


def hot_expand(z_own, z_got, factors, head):
    kept = factors[0].shape[1]
    near = kept // R
    count = z_own.shape[0] // HCAP

    def kernel(own_ref, got_ref, first_ref, second_ref, out_ref):
        z = (own_ref[...] + got_ref[...]).astype(jnp.bfloat16).astype(jnp.float32).reshape(count, 1, HCAP, kept)
        shape = (count, near, HCAP, kept)
        same = lax.broadcasted_iota(jnp.int32, shape, 3) // R == lax.broadcasted_iota(jnp.int32, shape, 1)
        spread = jnp.where(same, jnp.broadcast_to(z, shape), 0.0).astype(jnp.bfloat16)
        product = lax.dot_general(
            spread.reshape(count * near * HCAP, kept),
            first_ref[-head:] + second_ref[-head:],
            (((1,), (1,)), ((), ())),
            preferred_element_type=jnp.float32,
        )
        out_ref[...] = product.astype(jnp.bfloat16)

    return pl.pallas_call(
        kernel,
        out_shape=jax.ShapeDtypeStruct((count * near * HCAP, head), jnp.bfloat16),
        **kernel_params(),
    )(z_own, z_got, *factors)


def add_hot(partial, target, delta):
    count = partial.shape[0]
    hot_rows = delta.shape[0]

    def kernel(partial_ref, target_ref, delta_ref, out_ref):
        hit = lax.broadcasted_iota(jnp.int32, (count, hot_rows), 1) == target_ref[...]
        place = hit.astype(jnp.float32).astype(jnp.bfloat16)
        out_ref[...] = (partial_ref[...] + matmul(place, delta_ref[...])).astype(jnp.bfloat16)

    return pl.pallas_call(
        kernel,
        out_shape=jax.ShapeDtypeStruct(partial.shape, jnp.bfloat16),
        **kernel_params(),
    )(partial, target[:, None], delta)


def on_device(
    activations, value_weight, shrink_store, expand_store, adapter_row, token_adapter, hot_ids
):
    step_count, token_count, depth = activations.shape
    adapter_count = adapter_row.shape[0]
    hot_count = hot_ids.shape[1]
    per_dev = expand_store.shape[0] // R
    head_part = expand_store.shape[1]
    far_count = lax.axis_size("z_high")
    group_count = 8
    dp_count = far_count * group_count
    me = lax.axis_index(DP)
    z_at, x_at, core_at = lax.axis_index("z_low"), lax.axis_index("x"), lax.axis_index("core")
    none_code = adapter_count + hot_count
    rows = activations.reshape(step_count * token_count, depth)

    near = step_count // 2
    names = jnp.arange(adapter_count, dtype=jnp.int32)
    chain = Chain()

    cold_row = jnp.sum(jnp.where((token_adapter - hot_count)[:, :, None] == names, adapter_row, 0), axis=-1)
    is_hot = token_adapter < hot_count
    is_cold = (token_adapter < none_code) & jnp.logical_not(is_hot)
    owner = cold_row // per_dev
    group = jnp.where(is_hot, token_adapter, jnp.where(is_cold, hot_count + owner, -1))
    at = jnp.arange(token_count, dtype=jnp.int32)
    before = (group[:, :, None] == group[:, None, :]) & (at[None, :] < at[:, None])
    rank = jnp.sum(before.astype(jnp.int32), axis=-1)
    step_at = jnp.arange(step_count, dtype=jnp.int32)[:, None]
    hot_rows = hot_count * step_count * HCAP
    cold_rows = dp_count * step_count * CAP
    server = (step_at // near) * hot_count + token_adapter
    hot_target = (server * near + step_at % near) * HCAP + rank
    cold_target = (owner * step_count + step_at) * CAP + rank
    hot_target = jnp.where(is_hot, hot_target, -1).reshape(-1)
    cold_target = jnp.where(is_cold, cold_target, -1).reshape(-1)

    early = 3 * depth // 4

    def exchange(block):
        block = chain.hold(block.reshape(group_count, near * HCAP, -1))
        return lax.all_to_all(block, GROUP, split_axis=0, concat_axis=0, tiled=True).reshape(hot_rows, -1)

    hot_first_part, hot_last_part, packet = place_rows(
        rows, hot_target, cold_target, (cold_row % per_dev + 1).reshape(-1), hot_rows, cold_rows
    )
    hot_early = exchange(hot_first_part)

    hot_row = jnp.sum(jnp.where(hot_ids[:, :, None] == names, adapter_row, 0), axis=-1)
    hot_first = jnp.where(hot_row // per_dev == me, (hot_row % per_dev) * R, -R * per_dev)
    column = jnp.arange(per_dev * R, dtype=jnp.int32)
    lane = jnp.arange(R, dtype=jnp.int32)
    entry = jnp.arange(hot_count, dtype=jnp.int32)

    def wanted(core):
        firsts = []
        for x in (x_at, 1 - x_at):
            of_steps = jnp.sum(jnp.where(entry == 2 * x + core, hot_first, 0), axis=1)
            firsts += [jnp.where(z_at == 0, of_steps[:near], of_steps[near:])]
            firsts += [jnp.where(z_at == 0, of_steps[near:], of_steps[:near])]
        return jnp.stack([(f[:, None] + lane).reshape(-1) for f in firsts])

    want_mine, want_other = wanted(core_at), wanted(1 - core_at)
    kept = near * R
    chunk_count = 3
    part = (depth + head_part) // chunk_count

    hops = [("x", SWAP), ("z_low", SWAP)]
    bit = 1
    while bit < far_count:
        hops.append(("z_high", [(i, i ^ bit) for i in range(far_count)]))
        bit *= 2
    mine, swapped, got, held = {}, {}, {}, {}

    def operand(c, stage):
        if stage == 0:
            return mine[c][:, 2 * kept:] + swapped[c][:, 2 * kept:]
        if stage == 1:
            return mine[c][:, kept:2 * kept] + swapped[c][:, kept:2 * kept] + got[c, 0][:, kept:]
        if stage == 2:
            held[c] = mine[c][:, :kept] + swapped[c][:, :kept] + got[c, 0][:, :kept] + got[c, 1]
        else:
            held[c] = held[c] + got[c, stage - 1]
        return held[c]

    def send(c, stage):
        got[c, stage] = chain.permute(operand(c, stage), *hops[stage])

    mine_all, other_first, other_rest = pick_columns(
        after(shrink_store, chain.last), expand_store, want_mine, want_other
    )
    mine[0], swapped[0] = mine_all[:part], chain.permute(other_first, "core", SWAP)
    rest_swapped = chain.permute(other_rest, "core", SWAP)
    first, hot_early = lax.optimization_barrier((operand(0, 0), hot_early))
    got[0, 0] = chain.permute(first, *hops[0])
    done = {"hot_late": exchange(hot_last_part)}

    def cold_tokens_out():
        sent = chain.hold(packet.reshape(dp_count, step_count * CAP, depth + TAG))
        sent = lax.all_to_all(sent, DP, split_axis=0, concat_axis=0, tiled=True)
        done["packet"] = sent.reshape(cold_rows, depth + TAG)

    def base_product():
        weight = after(value_weight, chain.last)
        if lax.axis_size("tp") == 2:
            done["base_own"], done["base_other"] = base_halves(rows, weight)
        else:
            done["base_own"], done["base_other"] = jnp.zeros((1, 1), jnp.float32), matmul(rows, weight)

    def base_over_tp():
        if lax.axis_size("tp") == 2:
            done["base_got"] = chain.permute(done["base_other"], "tp", SWAP)
        else:
            whole = chain.hold(done["base_other"])
            done["base_got"] = lax.psum_scatter(whole, "tp", scatter_dimension=1, tiled=True)

    def cold_shrink():
        tag_in = done["packet"][:, depth:depth + 1].astype(jnp.int32)
        chosen = (column // R + 1)[None, :] == tag_in
        product = matmul(done["packet"][:, :depth], after(shrink_store, chain.last))
        done["z_part"] = jnp.where(chosen, product, 0.0)

    def cold_over_tp():
        done["z_cold"] = sum_over_tp(chain.hold(done["z_part"]))

    def cold_expand():
        done["delta"] = narrow(done["z_cold"].astype(jnp.bfloat16), after(expand_store, chain.last))

    def cold_back():
        delta = chain.hold(done["delta"].reshape(dp_count, step_count * CAP, head_part))
        delta = lax.all_to_all(delta, DP, split_axis=0, concat_axis=0, tiled=True)
        done["delta_cold"] = delta.reshape(cold_rows, head_part)

    def all_but_hot():
        place_cold = pick(jnp.arange(cold_rows, dtype=jnp.int32)[:, None] == cold_target)
        partial = lax.dot_general(
            place_cold, done["delta_cold"], (((0,), (0,)), ((), ())), preferred_element_type=jnp.float32
        )
        done["partial"] = partial + done["base_own"] + done["base_got"]

    between = {
        0: [base_product],
        1: [cold_tokens_out],
        2: [base_over_tp],
        3: [cold_shrink, cold_over_tp],
        4: [cold_expand, cold_back, all_but_hot],
    }
    awaited = {0: ["base_own", "base_other"], 1: ["hot_late"], 2: ["packet"], 3: ["z_cold", "base_got"]}
    for slot in range(chunk_count + len(hops) - 1):
        if slot > 0:
            if slot < chunk_count:
                mine[slot] = after(mine_all, chain.last)[slot * part:(slot + 1) * part]
                swapped[slot] = after(rest_swapped, chain.last)[(slot - 1) * part:slot * part]
            for stage in sorted(range(len(hops)), key=lambda stage: stage == 1):
                if 0 <= slot - stage < chunk_count:
                    send(slot - stage, stage)
        for work in between.get(slot, []):
            work()
        here = [(slot - stage, stage) for stage in range(len(hops)) if 0 <= slot - stage < chunk_count]
        names_here = awaited.get(slot, [])
        arrived = lax.optimization_barrier(
            (chain.last, *[got[at] for at in here], *[done[name] for name in names_here])
        )
        chain.last = arrived[0]
        got.update(zip(here, arrived[1:]))
        done.update(zip(names_here, arrived[1 + len(here):]))
    partial = done["partial"]

    dense = None
    for c in range(chunk_count):
        last = min((c + 1) * part, depth)
        hot_in = hot_early[:, c * part:last] if last <= early else done["hot_late"]
        for piece in (held[c], got[c, len(hops) - 1]):
            product = matmul(hot_in, piece[:last - c * part])
            dense = product if dense is None else dense + product
    dense = dense.reshape(group_count, near, HCAP, kept)
    at_step = jnp.arange(kept) // R
    z_part = sum(jnp.where(at_step == i, dense[:, i], 0.0) for i in range(near)).reshape(group_count * HCAP, kept)
    if lax.axis_size("tp") == 2:
        z_got = lax.ppermute(z_part, "tp", SWAP)
    else:
        z_part = lax.psum(z_part, "tp")
        z_got = jnp.zeros_like(z_part)
    delta_hot = hot_expand(z_part, z_got, (held[c], got[c, len(hops) - 1]), head_part).reshape(group_count, near * HCAP, head_part)
    delta_hot = lax.all_to_all(delta_hot, GROUP, split_axis=0, concat_axis=0, tiled=True)
    added = add_hot(partial, hot_target, delta_hot.reshape(hot_rows, head_part))
    return added.reshape(step_count, token_count, head_part)


def solution(mesh):
    tp_count, dp_count = mesh.shape["tp"], mesh.shape["dp"]
    fine = Mesh(mesh.devices.reshape(tp_count, dp_count // 8, 2, 2, 2), ("tp", *DP))
    placed = (
        P(None, DP, "tp"),
        P("tp", None),
        P("tp", DP),
        P(DP, "tp"),
        P(),
        P(None, DP),
        P(),
    )
    return jax.shard_map(
        on_device, mesh=fine, in_specs=placed, out_specs=P(None, DP, "tp"), check_vma=False
    )
```

```python
import jax
import jax.numpy as jnp
from jax import lax
from jax.experimental import pallas as pl
from jax.experimental.pallas import tpu as pltpu
from jax.sharding import Mesh, PartitionSpec as P

R = 64
CAP = 2
HCAP = 16
TAG = 128
DP = ("z_high", "z_low", "x", "core")
GROUP = ("z_low", "x", "core")
SWAP = [(0, 1), (1, 0)]


def pick(flags):
    return flags.astype(jnp.bfloat16)


def matmul(a, b):
    return jnp.dot(a, b, preferred_element_type=jnp.float32)


def narrow(a, b):
    return matmul(a, b).astype(jnp.bfloat16)


def sum_over_tp(part):
    if lax.axis_size("tp") == 2:
        return part + lax.ppermute(part, "tp", SWAP)
    return lax.psum(part, "tp")


def after(value, *others):
    return lax.optimization_barrier((value, *others))[0]


class Chain:
    def __init__(self):
        self.last = None

    def hold(self, value):
        self.last = value if self.last is None else after(value, self.last)
        return self.last

    def permute(self, value, axis, pairs):
        return lax.ppermute(self.hold(value), axis, pairs)

    def wait(self, *arrived):
        self.last = after(self.last, *arrived)


def kernel_params():
    return dict(
        compiler_params=pltpu.CompilerParams(vmem_limit_bytes=40 * 2**20),
        cost_estimate=pl.CostEstimate(flops=1, bytes_accessed=1, transcendentals=0),
    )


def pick_columns(store, expand, want_mine, want_other):
    depth, width = store.shape
    groups, lanes = want_mine.shape
    count = groups * lanes
    blocks = 8
    rows = depth // blocks

    def kernel(mine_held, other_held, mine_at, other_at, store_ref, expand_ref, mine_ref, first_ref, rest_ref, pick_mine, pick_other):
        step = pl.program_id(0)

        @pl.when(step == 0)
        def _():
            column = lax.broadcasted_iota(jnp.int32, (width, count), 0)
            pick_mine[...] = (column == mine_at[...]).astype(jnp.float32).astype(jnp.bfloat16)
            pick_other[...] = (column == other_at[...]).astype(jnp.float32).astype(jnp.bfloat16)

        def fill(out_ref, held, picker):
            for g in range(groups):
                at = slice(g * lanes, (g + 1) * lanes)

                @pl.when((held[g] > 0) & (step < blocks))
                def _():
                    out_ref[:, at] = narrow(store_ref[...], picker[:, at])

                @pl.when((held[g] > 0) & (step == blocks))
                def _():
                    product = lax.dot_general(
                        expand_ref[...], picker[:, at], (((0,), (0,)), ((), ())), preferred_element_type=jnp.float32
                    )
                    out_ref[:, at] = product.astype(jnp.bfloat16)

                @pl.when(held[g] == 0)
                def _():
                    out_ref[:, at] = jnp.zeros((rows, lanes), jnp.bfloat16)

        fill(mine_ref, mine_held, pick_mine)

        @pl.when(step < 3)
        def _():
            fill(first_ref, other_held, pick_other)

        @pl.when(step >= 3)
        def _():
            fill(rest_ref, other_held, pick_other)

    out = lambda thirds: jax.ShapeDtypeStruct((3 * rows * thirds, count), jnp.bfloat16)
    index = pl.BlockSpec((1, count), lambda i, *held: (0, 0))
    return pl.pallas_call(
        kernel,
        grid_spec=pltpu.PrefetchScalarGridSpec(
            num_scalar_prefetch=2,
            grid=(blocks + 1,),
            in_specs=[
                index,
                index,
                pl.BlockSpec((rows, width), lambda i, *held: (jnp.minimum(i, blocks - 1), 0)),
                pl.BlockSpec(expand.shape, lambda i, *held: (0, 0)),
            ],
            out_specs=[
                pl.BlockSpec((rows, count), lambda i, *held: (i, 0)),
                pl.BlockSpec((rows, count), lambda i, *held: (jnp.minimum(i, 2), 0)),
                pl.BlockSpec((rows, count), lambda i, *held: (jnp.maximum(i - 3, 0), 0)),
            ],
            scratch_shapes=[pltpu.VMEM((width, count), jnp.bfloat16)] * 2,
        ),
        out_shape=[out(3), out(1), out(2)],
        **kernel_params(),
    )(
        jnp.any(want_mine >= 0, axis=1).astype(jnp.int32),
        jnp.any(want_other >= 0, axis=1).astype(jnp.int32),
        want_mine.reshape(1, -1),
        want_other.reshape(1, -1),
        store,
        expand,
    )


def place_rows(rows, hot_target, cold_target, tag, hot_rows, cold_rows):
    count, depth = rows.shape
    blocks = 4
    width = depth // blocks

    def kernel(hot_at, cold_at, tag_at, rows_ref, early_ref, late_ref, cold_ref, place_hot, place_cold):
        step = pl.program_id(0)

        @pl.when(step == 0)
        def _():
            hot_hit = lax.broadcasted_iota(jnp.int32, (hot_rows, count), 0) == hot_at[...]
            cold_hit = lax.broadcasted_iota(jnp.int32, (cold_rows, count), 0) == cold_at[...]
            place_hot[...] = hot_hit.astype(jnp.float32).astype(jnp.bfloat16)
            place_cold[...] = cold_hit.astype(jnp.float32).astype(jnp.bfloat16)
            tags = jnp.sum(jnp.where(cold_hit, tag_at[...].astype(jnp.float32), 0.0), axis=1, keepdims=True)
            cold_ref[:, depth:] = jnp.broadcast_to(tags, (cold_rows, TAG)).astype(jnp.bfloat16)

        block = rows_ref[...]
        placed = narrow(place_hot[...], block)
        cold_ref[:, pl.ds(pl.multiple_of(step * width, 128), width)] = narrow(place_cold[...], block)

        @pl.when(step < blocks - 1)
        def _():
            early_ref[...] = placed

        @pl.when(step == blocks - 1)
        def _():
            late_ref[...] = placed

    index = pl.BlockSpec((1, count), lambda j: (0, 0))
    return pl.pallas_call(
        kernel,
        grid=(blocks,),
        in_specs=[index, index, index, pl.BlockSpec((count, width), lambda j: (0, j))],
        out_specs=[
            pl.BlockSpec((hot_rows, width), lambda j: (0, jnp.minimum(j, blocks - 2))),
            pl.BlockSpec((hot_rows, width), lambda j: (0, 0)),
            pl.BlockSpec((cold_rows, depth + TAG), lambda j: (0, 0)),
        ],
        out_shape=[
            jax.ShapeDtypeStruct((hot_rows, depth - width), jnp.bfloat16),
            jax.ShapeDtypeStruct((hot_rows, width), jnp.bfloat16),
            jax.ShapeDtypeStruct((cold_rows, depth + TAG), jnp.bfloat16),
        ],
        scratch_shapes=[pltpu.VMEM((hot_rows, count), jnp.bfloat16), pltpu.VMEM((cold_rows, count), jnp.bfloat16)],
        **kernel_params(),
    )(hot_target[None], cold_target[None], tag[None], rows)


def base_halves(rows, weight):
    count, depth = rows.shape
    width = weight.shape[1]
    half = width // 2
    blocks = 8
    part = depth // blocks

    def kernel(tp_at, rows_ref, weight_ref, own_ref, other_ref, total):
        step = pl.program_id(0)
        product = matmul(rows_ref[...], weight_ref[...])

        @pl.when(step == 0)
        def _():
            total[...] = product

        @pl.when(step > 0)
        def _():
            total[...] += product

        @pl.when(step == blocks - 1)
        def _():
            first = pl.multiple_of(tp_at[0] * half, 128)
            second = pl.multiple_of((1 - tp_at[0]) * half, 128)
            own_ref[...] = total[:, pl.ds(first, half)]
            other_ref[...] = total[:, pl.ds(second, half)]

    out = pl.BlockSpec((count, half), lambda k, at: (0, 0))
    return pl.pallas_call(
        kernel,
        grid_spec=pltpu.PrefetchScalarGridSpec(
            num_scalar_prefetch=1,
            grid=(blocks,),
            in_specs=[
                pl.BlockSpec((count, part), lambda k, at: (0, k)),
                pl.BlockSpec((part, width), lambda k, at: (k, 0)),
            ],
            out_specs=[out, out],
            scratch_shapes=[pltpu.VMEM((count, width), jnp.float32)],
        ),
        out_shape=[jax.ShapeDtypeStruct((count, half), jnp.float32)] * 2,
        **kernel_params(),
    )(lax.axis_index("tp").astype(jnp.int32)[None], rows, weight)


def hot_expand(z_own, z_got, factors, head):
    kept = factors[0].shape[1]
    near = kept // R
    count = z_own.shape[0] // HCAP

    def kernel(own_ref, got_ref, first_ref, second_ref, out_ref):
        z = (own_ref[...] + got_ref[...]).astype(jnp.bfloat16).astype(jnp.float32).reshape(count, 1, HCAP, kept)
        shape = (count, near, HCAP, kept)
        same = lax.broadcasted_iota(jnp.int32, shape, 3) // R == lax.broadcasted_iota(jnp.int32, shape, 1)
        spread = jnp.where(same, jnp.broadcast_to(z, shape), 0.0).astype(jnp.bfloat16)
        product = lax.dot_general(
            spread.reshape(count * near * HCAP, kept),
            first_ref[-head:] + second_ref[-head:],
            (((1,), (1,)), ((), ())),
            preferred_element_type=jnp.float32,
        )
        out_ref[...] = product.astype(jnp.bfloat16)

    return pl.pallas_call(
        kernel,
        out_shape=jax.ShapeDtypeStruct((count * near * HCAP, head), jnp.bfloat16),
        **kernel_params(),
    )(z_own, z_got, *factors)


def add_hot(partial, target, delta):
    count = partial.shape[0]
    hot_rows = delta.shape[0]

    def kernel(partial_ref, target_ref, delta_ref, out_ref):
        hit = lax.broadcasted_iota(jnp.int32, (count, hot_rows), 1) == target_ref[...]
        place = hit.astype(jnp.float32).astype(jnp.bfloat16)
        out_ref[...] = (partial_ref[...] + matmul(place, delta_ref[...])).astype(jnp.bfloat16)

    return pl.pallas_call(
        kernel,
        out_shape=jax.ShapeDtypeStruct(partial.shape, jnp.bfloat16),
        **kernel_params(),
    )(partial, target[:, None], delta)


def on_device(
    activations, value_weight, shrink_store, expand_store, adapter_row, token_adapter, hot_ids
):
    step_count, token_count, depth = activations.shape
    adapter_count = adapter_row.shape[0]
    hot_count = hot_ids.shape[1]
    per_dev = expand_store.shape[0] // R
    head_part = expand_store.shape[1]
    far_count = lax.axis_size("z_high")
    group_count = 8
    dp_count = far_count * group_count
    me = lax.axis_index(DP)
    z_at, x_at, core_at = lax.axis_index("z_low"), lax.axis_index("x"), lax.axis_index("core")
    none_code = adapter_count + hot_count
    rows = activations.reshape(step_count * token_count, depth)

    near = step_count // 2
    names = jnp.arange(adapter_count, dtype=jnp.int32)
    chain = Chain()

    cold_row = jnp.sum(jnp.where((token_adapter - hot_count)[:, :, None] == names, adapter_row, 0), axis=-1)
    is_hot = token_adapter < hot_count
    is_cold = (token_adapter < none_code) & jnp.logical_not(is_hot)
    owner = cold_row // per_dev
    group = jnp.where(is_hot, token_adapter, jnp.where(is_cold, hot_count + owner, -1))
    at = jnp.arange(token_count, dtype=jnp.int32)
    before = (group[:, :, None] == group[:, None, :]) & (at[None, :] < at[:, None])
    rank = jnp.sum(before.astype(jnp.int32), axis=-1)
    step_at = jnp.arange(step_count, dtype=jnp.int32)[:, None]
    hot_rows = hot_count * step_count * HCAP
    cold_rows = dp_count * step_count * CAP
    server = (step_at // near) * hot_count + token_adapter
    hot_target = (server * near + step_at % near) * HCAP + rank
    cold_target = (owner * step_count + step_at) * CAP + rank
    hot_target = jnp.where(is_hot, hot_target, -1).reshape(-1)
    cold_target = jnp.where(is_cold, cold_target, -1).reshape(-1)

    early = 3 * depth // 4

    def exchange(block):
        block = chain.hold(block.reshape(group_count, near * HCAP, -1))
        return lax.all_to_all(block, GROUP, split_axis=0, concat_axis=0, tiled=True).reshape(hot_rows, -1)

    hot_first_part, hot_last_part, packet = place_rows(
        rows, hot_target, cold_target, (cold_row % per_dev + 1).reshape(-1), hot_rows, cold_rows
    )
    hot_early = exchange(hot_first_part)

    hot_row = jnp.sum(jnp.where(hot_ids[:, :, None] == names, adapter_row, 0), axis=-1)
    hot_first = jnp.where(hot_row // per_dev == me, (hot_row % per_dev) * R, -R * per_dev)
    column = jnp.arange(per_dev * R, dtype=jnp.int32)
    lane = jnp.arange(R, dtype=jnp.int32)
    entry = jnp.arange(hot_count, dtype=jnp.int32)

    def wanted(core):
        firsts = []
        for x in (x_at, 1 - x_at):
            of_steps = jnp.sum(jnp.where(entry == 2 * x + core, hot_first, 0), axis=1)
            firsts += [jnp.where(z_at == 0, of_steps[:near], of_steps[near:])]
            firsts += [jnp.where(z_at == 0, of_steps[near:], of_steps[:near])]
        return jnp.stack([(f[:, None] + lane).reshape(-1) for f in firsts])

    want_mine, want_other = wanted(core_at), wanted(1 - core_at)
    kept = near * R
    chunk_count = 3
    part = (depth + head_part) // chunk_count

    hops = [("x", SWAP), ("z_low", SWAP)]
    bit = 1
    while bit < far_count:
        hops.append(("z_high", [(i, i ^ bit) for i in range(far_count)]))
        bit *= 2
    mine, swapped, got, held = {}, {}, {}, {}

    def operand(c, stage):
        if stage == 0:
            return mine[c][:, 2 * kept:] + swapped[c][:, 2 * kept:]
        if stage == 1:
            return mine[c][:, kept:2 * kept] + swapped[c][:, kept:2 * kept] + got[c, 0][:, kept:]
        if stage == 2:
            held[c] = mine[c][:, :kept] + swapped[c][:, :kept] + got[c, 0][:, :kept] + got[c, 1]
        else:
            held[c] = held[c] + got[c, stage - 1]
        return held[c]

    def send(c, stage):
        got[c, stage] = chain.permute(operand(c, stage), *hops[stage])

    mine_all, other_first, other_rest = pick_columns(
        after(shrink_store, chain.last), expand_store, want_mine, want_other
    )
    mine[0], swapped[0] = mine_all[:part], chain.permute(other_first, "core", SWAP)
    rest_swapped = chain.permute(other_rest, "core", SWAP)
    first, hot_early = lax.optimization_barrier((operand(0, 0), hot_early))
    got[0, 0] = chain.permute(first, *hops[0])
    done = {"hot_late": exchange(hot_last_part)}

    def cold_tokens_out():
        sent = chain.hold(packet.reshape(dp_count, step_count * CAP, depth + TAG))
        sent = lax.all_to_all(sent, DP, split_axis=0, concat_axis=0, tiled=True)
        done["packet"] = sent.reshape(cold_rows, depth + TAG)

    def base_product():
        weight = after(value_weight, chain.last)
        if lax.axis_size("tp") == 2:
            done["base_own"], done["base_other"] = base_halves(rows, weight)
        else:
            done["base_own"], done["base_other"] = jnp.zeros((1, 1), jnp.float32), matmul(rows, weight)

    def base_over_tp():
        if lax.axis_size("tp") == 2:
            done["base_got"] = chain.permute(done["base_other"], "tp", SWAP)
        else:
            whole = chain.hold(done["base_other"])
            done["base_got"] = lax.psum_scatter(whole, "tp", scatter_dimension=1, tiled=True)

    def cold_shrink():
        tag_in = done["packet"][:, depth:depth + 1].astype(jnp.int32)
        chosen = (column // R + 1)[None, :] == tag_in
        product = matmul(done["packet"][:, :depth], after(shrink_store, chain.last))
        done["z_part"] = jnp.where(chosen, product, 0.0)

    def cold_over_tp():
        done["z_cold"] = sum_over_tp(chain.hold(done["z_part"]))

    def cold_expand():
        done["delta"] = narrow(done["z_cold"].astype(jnp.bfloat16), after(expand_store, chain.last))

    def cold_back():
        delta = chain.hold(done["delta"].reshape(dp_count, step_count * CAP, head_part))
        delta = lax.all_to_all(delta, DP, split_axis=0, concat_axis=0, tiled=True)
        done["delta_cold"] = delta.reshape(cold_rows, head_part)

    def all_but_hot():
        place_cold = pick(jnp.arange(cold_rows, dtype=jnp.int32)[:, None] == cold_target)
        partial = lax.dot_general(
            place_cold, done["delta_cold"], (((0,), (0,)), ((), ())), preferred_element_type=jnp.float32
        )
        done["partial"] = partial + done["base_own"] + done["base_got"]

    between = {
        0: [cold_tokens_out],
        1: [base_product],
        2: [cold_shrink, cold_over_tp, base_over_tp],
        3: [cold_expand, cold_back],
        4: [all_but_hot],
    }
    awaited = {0: ["hot_late"], 1: ["packet", "base_own", "base_other"], 2: ["z_cold"], 3: ["base_got"]}
    for slot in range(chunk_count + len(hops) - 1):
        if slot > 0:
            if slot < chunk_count:
                mine[slot] = after(mine_all, chain.last)[slot * part:(slot + 1) * part]
                swapped[slot] = after(rest_swapped, chain.last)[(slot - 1) * part:slot * part]
            for stage in sorted(range(len(hops)), key=lambda stage: stage == 1):
                if 0 <= slot - stage < chunk_count:
                    send(slot - stage, stage)
        for work in between.get(slot, []):
            work()
        here = [(slot - stage, stage) for stage in range(len(hops)) if 0 <= slot - stage < chunk_count]
        names_here = awaited.get(slot, [])
        arrived = lax.optimization_barrier(
            (chain.last, *[got[at] for at in here], *[done[name] for name in names_here])
        )
        chain.last = arrived[0]
        got.update(zip(here, arrived[1:]))
        done.update(zip(names_here, arrived[1 + len(here):]))
    partial = done["partial"]

    dense = None
    for c in range(chunk_count):
        last = min((c + 1) * part, depth)
        hot_in = hot_early[:, c * part:last] if last <= early else done["hot_late"]
        for piece in (held[c], got[c, len(hops) - 1]):
            product = matmul(hot_in, piece[:last - c * part])
            dense = product if dense is None else dense + product
    dense = dense.reshape(group_count, near, HCAP, kept)
    at_step = jnp.arange(kept) // R
    z_part = sum(jnp.where(at_step == i, dense[:, i], 0.0) for i in range(near)).reshape(group_count * HCAP, kept)
    if lax.axis_size("tp") == 2:
        z_got = lax.ppermute(z_part, "tp", SWAP)
    else:
        z_part = lax.psum(z_part, "tp")
        z_got = jnp.zeros_like(z_part)
    delta_hot = hot_expand(z_part, z_got, (held[c], got[c, len(hops) - 1]), head_part).reshape(group_count, near * HCAP, head_part)
    delta_hot = lax.all_to_all(delta_hot, GROUP, split_axis=0, concat_axis=0, tiled=True)
    added = add_hot(partial, hot_target, delta_hot.reshape(hot_rows, head_part))
    return added.reshape(step_count, token_count, head_part)


def solution(mesh):
    tp_count, dp_count = mesh.shape["tp"], mesh.shape["dp"]
    fine = Mesh(mesh.devices.reshape(tp_count, dp_count // 8, 2, 2, 2), ("tp", *DP))
    placed = (
        P(None, DP, "tp"),
        P("tp", None),
        P("tp", DP),
        P(DP, "tp"),
        P(),
        P(None, DP),
        P(),
    )
    return jax.shard_map(
        on_device, mesh=fine, in_specs=placed, out_specs=P(None, DP, "tp"), check_vma=False
    )
```

```python
import jax
import jax.numpy as jnp
from jax import lax
from jax.experimental import pallas as pl
from jax.experimental.pallas import tpu as pltpu
from jax.sharding import Mesh, PartitionSpec as P

R = 64
CAP = 2
HCAP = 16
TAG = 128
DP = ("z_high", "z_low", "x", "core")
GROUP = ("z_low", "x", "core")
SWAP = [(0, 1), (1, 0)]


def pick(flags):
    return flags.astype(jnp.bfloat16)


def matmul(a, b):
    return jnp.dot(a, b, preferred_element_type=jnp.float32)


def narrow(a, b):
    return matmul(a, b).astype(jnp.bfloat16)


def sum_over_tp(part):
    if lax.axis_size("tp") == 2:
        return part + lax.ppermute(part, "tp", SWAP)
    return lax.psum(part, "tp")


def after(value, *others):
    return lax.optimization_barrier((value, *others))[0]


class Chain:
    def __init__(self):
        self.last = None

    def hold(self, value):
        self.last = value if self.last is None else after(value, self.last)
        return self.last

    def permute(self, value, axis, pairs):
        return lax.ppermute(self.hold(value), axis, pairs)

    def wait(self, *arrived):
        self.last = after(self.last, *arrived)


def kernel_params():
    return dict(
        compiler_params=pltpu.CompilerParams(vmem_limit_bytes=40 * 2**20),
        cost_estimate=pl.CostEstimate(flops=1, bytes_accessed=1, transcendentals=0),
    )


def pick_columns(store, expand, want_mine, want_other):
    depth, width = store.shape
    groups, lanes = want_mine.shape
    count = groups * lanes
    blocks = 8
    rows = depth // blocks

    def kernel(mine_held, other_held, mine_at, other_at, store_ref, expand_ref, mine_ref, first_ref, rest_ref, pick_mine, pick_other):
        step = pl.program_id(0)

        @pl.when(step == 0)
        def _():
            column = lax.broadcasted_iota(jnp.int32, (width, count), 0)
            pick_mine[...] = (column == mine_at[...]).astype(jnp.float32).astype(jnp.bfloat16)
            pick_other[...] = (column == other_at[...]).astype(jnp.float32).astype(jnp.bfloat16)

        def fill(out_ref, held, picker):
            for g in range(groups):
                at = slice(g * lanes, (g + 1) * lanes)

                @pl.when((held[g] > 0) & (step < blocks))
                def _():
                    out_ref[:, at] = narrow(store_ref[...], picker[:, at])

                @pl.when((held[g] > 0) & (step == blocks))
                def _():
                    product = lax.dot_general(
                        expand_ref[...], picker[:, at], (((0,), (0,)), ((), ())), preferred_element_type=jnp.float32
                    )
                    out_ref[:, at] = product.astype(jnp.bfloat16)

                @pl.when(held[g] == 0)
                def _():
                    out_ref[:, at] = jnp.zeros((rows, lanes), jnp.bfloat16)

        fill(mine_ref, mine_held, pick_mine)

        @pl.when(step < 3)
        def _():
            fill(first_ref, other_held, pick_other)

        @pl.when(step >= 3)
        def _():
            fill(rest_ref, other_held, pick_other)

    out = lambda thirds: jax.ShapeDtypeStruct((3 * rows * thirds, count), jnp.bfloat16)
    index = pl.BlockSpec((1, count), lambda i, *held: (0, 0))
    return pl.pallas_call(
        kernel,
        grid_spec=pltpu.PrefetchScalarGridSpec(
            num_scalar_prefetch=2,
            grid=(blocks + 1,),
            in_specs=[
                index,
                index,
                pl.BlockSpec((rows, width), lambda i, *held: (jnp.minimum(i, blocks - 1), 0)),
                pl.BlockSpec(expand.shape, lambda i, *held: (0, 0)),
            ],
            out_specs=[
                pl.BlockSpec((rows, count), lambda i, *held: (i, 0)),
                pl.BlockSpec((rows, count), lambda i, *held: (jnp.minimum(i, 2), 0)),
                pl.BlockSpec((rows, count), lambda i, *held: (jnp.maximum(i - 3, 0), 0)),
            ],
            scratch_shapes=[pltpu.VMEM((width, count), jnp.bfloat16)] * 2,
        ),
        out_shape=[out(3), out(1), out(2)],
        **kernel_params(),
    )(
        jnp.any(want_mine >= 0, axis=1).astype(jnp.int32),
        jnp.any(want_other >= 0, axis=1).astype(jnp.int32),
        want_mine.reshape(1, -1),
        want_other.reshape(1, -1),
        store,
        expand,
    )


def place_rows(rows, target, placed_rows):
    count, depth = rows.shape
    blocks = 4
    width = depth // blocks

    def kernel(target_at, rows_ref, out_ref, place):
        @pl.when(pl.program_id(0) == 0)
        def _():
            hit = lax.broadcasted_iota(jnp.int32, (placed_rows, count), 0) == target_at[...]
            place[...] = hit.astype(jnp.float32).astype(jnp.bfloat16)

        out_ref[...] = narrow(place[...], rows_ref[...])

    return pl.pallas_call(
        kernel,
        grid=(blocks,),
        in_specs=[pl.BlockSpec((1, count), lambda j: (0, 0)), pl.BlockSpec((count, width), lambda j: (0, j))],
        out_specs=pl.BlockSpec((placed_rows, width), lambda j: (0, j)),
        out_shape=jax.ShapeDtypeStruct((placed_rows, depth), jnp.bfloat16),
        scratch_shapes=[pltpu.VMEM((placed_rows, count), jnp.bfloat16)],
        **kernel_params(),
    )(target[None], rows)


def base_halves(rows, weight):
    count, depth = rows.shape
    width = weight.shape[1]
    half = width // 2
    blocks = 8
    part = depth // blocks

    def kernel(tp_at, rows_ref, weight_ref, own_ref, other_ref, total):
        step = pl.program_id(0)
        product = matmul(rows_ref[...], weight_ref[...])

        @pl.when(step == 0)
        def _():
            total[...] = product

        @pl.when(step > 0)
        def _():
            total[...] += product

        @pl.when(step == blocks - 1)
        def _():
            first = pl.multiple_of(tp_at[0] * half, 128)
            second = pl.multiple_of((1 - tp_at[0]) * half, 128)
            own_ref[...] = total[:, pl.ds(first, half)]
            other_ref[...] = total[:, pl.ds(second, half)]

    out = pl.BlockSpec((count, half), lambda k, at: (0, 0))
    return pl.pallas_call(
        kernel,
        grid_spec=pltpu.PrefetchScalarGridSpec(
            num_scalar_prefetch=1,
            grid=(blocks,),
            in_specs=[
                pl.BlockSpec((count, part), lambda k, at: (0, k)),
                pl.BlockSpec((part, width), lambda k, at: (k, 0)),
            ],
            out_specs=[out, out],
            scratch_shapes=[pltpu.VMEM((count, width), jnp.float32)],
        ),
        out_shape=[jax.ShapeDtypeStruct((count, half), jnp.float32)] * 2,
        **kernel_params(),
    )(lax.axis_index("tp").astype(jnp.int32)[None], rows, weight)


def hot_expand(z_own, z_got, factors, head):
    kept = factors[0].shape[1]
    near = kept // R
    count = z_own.shape[0] // HCAP

    def kernel(own_ref, got_ref, first_ref, second_ref, out_ref):
        z = (own_ref[...] + got_ref[...]).astype(jnp.bfloat16).astype(jnp.float32).reshape(count, 1, HCAP, kept)
        shape = (count, near, HCAP, kept)
        same = lax.broadcasted_iota(jnp.int32, shape, 3) // R == lax.broadcasted_iota(jnp.int32, shape, 1)
        spread = jnp.where(same, jnp.broadcast_to(z, shape), 0.0).astype(jnp.bfloat16)
        product = lax.dot_general(
            spread.reshape(count * near * HCAP, kept),
            first_ref[-head:] + second_ref[-head:],
            (((1,), (1,)), ((), ())),
            preferred_element_type=jnp.float32,
        )
        out_ref[...] = product.astype(jnp.bfloat16)

    return pl.pallas_call(
        kernel,
        out_shape=jax.ShapeDtypeStruct((count * near * HCAP, head), jnp.bfloat16),
        **kernel_params(),
    )(z_own, z_got, *factors)


def add_hot(partial, target, delta):
    count = partial.shape[0]
    hot_rows = delta.shape[0]

    def kernel(partial_ref, target_ref, delta_ref, out_ref):
        hit = lax.broadcasted_iota(jnp.int32, (count, hot_rows), 1) == target_ref[...]
        place = hit.astype(jnp.float32).astype(jnp.bfloat16)
        out_ref[...] = (partial_ref[...] + matmul(place, delta_ref[...])).astype(jnp.bfloat16)

    return pl.pallas_call(
        kernel,
        out_shape=jax.ShapeDtypeStruct(partial.shape, jnp.bfloat16),
        **kernel_params(),
    )(partial, target[:, None], delta)


def on_device(
    activations, value_weight, shrink_store, expand_store, adapter_row, token_adapter, hot_ids
):
    step_count, token_count, depth = activations.shape
    adapter_count = adapter_row.shape[0]
    hot_count = hot_ids.shape[1]
    per_dev = expand_store.shape[0] // R
    head_part = expand_store.shape[1]
    far_count = lax.axis_size("z_high")
    group_count = 8
    dp_count = far_count * group_count
    me = lax.axis_index(DP)
    z_at, x_at, core_at = lax.axis_index("z_low"), lax.axis_index("x"), lax.axis_index("core")
    none_code = adapter_count + hot_count
    rows = activations.reshape(step_count * token_count, depth)

    near = step_count // 2
    names = jnp.arange(adapter_count, dtype=jnp.int32)
    chain = Chain()

    hot_rows = hot_count * step_count * HCAP
    cold_rows = dp_count * step_count * CAP
    step_at = jnp.arange(step_count, dtype=jnp.int32)[:, None]
    at = jnp.arange(token_count, dtype=jnp.int32)

    def rank_in(group):
        before = (group[:, :, None] == group[:, None, :]) & (at[None, :] < at[:, None])
        return jnp.sum(before.astype(jnp.int32), axis=-1)

    is_hot = token_adapter < hot_count
    server = (step_at // near) * hot_count + token_adapter
    hot_target = (server * near + step_at % near) * HCAP + rank_in(token_adapter)
    hot_target = jnp.where(is_hot, hot_target, -1).reshape(-1)
    hot_out = chain.hold(place_rows(rows, hot_target, hot_rows).reshape(group_count, near * HCAP, depth))
    done = {"hot_in": lax.all_to_all(hot_out, GROUP, split_axis=0, concat_axis=0, tiled=True)}

    hot_row = jnp.sum(jnp.where(hot_ids[:, :, None] == names, adapter_row, 0), axis=-1)
    hot_first = jnp.where(hot_row // per_dev == me, (hot_row % per_dev) * R, -R * per_dev)
    column = jnp.arange(per_dev * R, dtype=jnp.int32)
    lane = jnp.arange(R, dtype=jnp.int32)
    entry = jnp.arange(hot_count, dtype=jnp.int32)

    def wanted(core):
        firsts = []
        for x in (x_at, 1 - x_at):
            of_steps = jnp.sum(jnp.where(entry == 2 * x + core, hot_first, 0), axis=1)
            firsts += [jnp.where(z_at == 0, of_steps[:near], of_steps[near:])]
            firsts += [jnp.where(z_at == 0, of_steps[near:], of_steps[:near])]
        return jnp.stack([(f[:, None] + lane).reshape(-1) for f in firsts])

    want_mine, want_other = wanted(core_at), wanted(1 - core_at)
    kept = near * R
    chunk_count = 3
    part = (depth + head_part) // chunk_count

    hops = [("x", SWAP), ("z_low", SWAP)]
    bit = 1
    while bit < far_count:
        hops.append(("z_high", [(i, i ^ bit) for i in range(far_count)]))
        bit *= 2
    mine, swapped, got, held = {}, {}, {}, {}

    def operand(c, stage):
        if stage == 0:
            return mine[c][:, 2 * kept:] + swapped[c][:, 2 * kept:]
        if stage == 1:
            return mine[c][:, kept:2 * kept] + swapped[c][:, kept:2 * kept] + got[c, 0][:, kept:]
        if stage == 2:
            held[c] = mine[c][:, :kept] + swapped[c][:, :kept] + got[c, 0][:, :kept] + got[c, 1]
        else:
            held[c] = held[c] + got[c, stage - 1]
        return held[c]

    def send(c, stage):
        got[c, stage] = chain.permute(operand(c, stage), *hops[stage])

    mine_all, other_first, other_rest = pick_columns(
        after(shrink_store, chain.last), expand_store, want_mine, want_other
    )
    mine[0], swapped[0] = mine_all[:part], chain.permute(other_first, "core", SWAP)
    rest_swapped = chain.permute(other_rest, "core", SWAP)
    send(0, 0)

    codes = after(token_adapter, chain.last)
    cold_row = jnp.sum(jnp.where((codes - hot_count)[:, :, None] == names, adapter_row, 0), axis=-1)
    is_cold = (codes < none_code) & (codes >= hot_count)
    owner = cold_row // per_dev
    cold_target = (owner * step_count + step_at) * CAP + rank_in(jnp.where(is_cold, owner, -1))
    cold_target = jnp.where(is_cold, cold_target, -1).reshape(-1)

    def cold_tokens_out():
        cold_hit = jnp.arange(cold_rows, dtype=jnp.int32)[:, None] == cold_target
        tag = jnp.sum(jnp.where(cold_hit, (cold_row % per_dev + 1).reshape(-1), 0), axis=-1)
        tag = jnp.broadcast_to(tag.astype(jnp.bfloat16)[:, None], (cold_rows, TAG))
        packet = jnp.concatenate([narrow(pick(cold_hit), rows), tag], axis=1)
        packet = chain.hold(packet.reshape(dp_count, step_count * CAP, depth + TAG))
        packet = lax.all_to_all(packet, DP, split_axis=0, concat_axis=0, tiled=True)
        done["packet"] = packet.reshape(cold_rows, depth + TAG)

    def base_product():
        weight = after(value_weight, chain.last)
        if lax.axis_size("tp") == 2:
            done["base_own"], done["base_other"] = base_halves(rows, weight)
        else:
            done["base_own"], done["base_other"] = jnp.zeros((1, 1), jnp.float32), matmul(rows, weight)

    def base_over_tp():
        if lax.axis_size("tp") == 2:
            done["base_got"] = chain.permute(done["base_other"], "tp", SWAP)
        else:
            whole = chain.hold(done["base_other"])
            done["base_got"] = lax.psum_scatter(whole, "tp", scatter_dimension=1, tiled=True)

    def cold_shrink():
        tag_in = done["packet"][:, depth:depth + 1].astype(jnp.int32)
        chosen = (column // R + 1)[None, :] == tag_in
        product = matmul(done["packet"][:, :depth], after(shrink_store, chain.last))
        done["z_part"] = jnp.where(chosen, product, 0.0)

    def cold_over_tp():
        done["z_cold"] = sum_over_tp(chain.hold(done["z_part"]))

    def cold_expand():
        done["delta"] = narrow(done["z_cold"].astype(jnp.bfloat16), after(expand_store, chain.last))

    def cold_back():
        delta = chain.hold(done["delta"].reshape(dp_count, step_count * CAP, head_part))
        delta = lax.all_to_all(delta, DP, split_axis=0, concat_axis=0, tiled=True)
        done["delta_cold"] = delta.reshape(cold_rows, head_part)

    def all_but_hot():
        place_cold = pick(jnp.arange(cold_rows, dtype=jnp.int32)[:, None] == cold_target)
        partial = lax.dot_general(
            place_cold, done["delta_cold"], (((0,), (0,)), ((), ())), preferred_element_type=jnp.float32
        )
        done["partial"] = partial + done["base_own"] + done["base_got"]

    between = {
        0: [cold_tokens_out],
        1: [base_product],
        2: [cold_shrink, cold_over_tp, base_over_tp],
        4: [cold_expand, cold_back, all_but_hot],
    }
    awaited = {0: ["hot_in"], 1: ["packet", "base_own", "base_other"], 2: ["z_cold"], 3: ["base_got"]}
    for slot in range(chunk_count + len(hops) - 1):
        if slot > 0:
            if slot < chunk_count:
                mine[slot] = after(mine_all, chain.last)[slot * part:(slot + 1) * part]
                swapped[slot] = after(rest_swapped, chain.last)[(slot - 1) * part:slot * part]
            for stage in sorted(range(len(hops)), key=lambda stage: stage == 1):
                if 0 <= slot - stage < chunk_count:
                    send(slot - stage, stage)
        for work in between.get(slot, []):
            work()
        here = [(slot - stage, stage) for stage in range(len(hops)) if 0 <= slot - stage < chunk_count]
        names_here = awaited.get(slot, [])
        arrived = lax.optimization_barrier(
            (chain.last, *[got[at] for at in here], *[done[name] for name in names_here])
        )
        chain.last = arrived[0]
        got.update(zip(here, arrived[1:]))
        done.update(zip(names_here, arrived[1 + len(here):]))
    partial = done["partial"]

    hot_in = done["hot_in"].reshape(hot_rows, depth)
    dense = None
    for c in range(chunk_count):
        last = min((c + 1) * part, depth)
        for piece in (held[c], got[c, len(hops) - 1]):
            product = matmul(hot_in[:, c * part:last], piece[:last - c * part])
            dense = product if dense is None else dense + product
    dense = dense.reshape(group_count, near, HCAP, kept)
    at_step = jnp.arange(kept) // R
    z_part = sum(jnp.where(at_step == i, dense[:, i], 0.0) for i in range(near)).reshape(group_count * HCAP, kept)
    if lax.axis_size("tp") == 2:
        z_got = lax.ppermute(z_part, "tp", SWAP)
    else:
        z_part = lax.psum(z_part, "tp")
        z_got = jnp.zeros_like(z_part)
    delta_hot = hot_expand(z_part, z_got, (held[c], got[c, len(hops) - 1]), head_part).reshape(group_count, near * HCAP, head_part)
    delta_hot = lax.all_to_all(delta_hot, GROUP, split_axis=0, concat_axis=0, tiled=True)
    added = add_hot(partial, hot_target, delta_hot.reshape(hot_rows, head_part))
    return added.reshape(step_count, token_count, head_part)


def solution(mesh):
    tp_count, dp_count = mesh.shape["tp"], mesh.shape["dp"]
    fine = Mesh(mesh.devices.reshape(tp_count, dp_count // 8, 2, 2, 2), ("tp", *DP))
    placed = (
        P(None, DP, "tp"),
        P("tp", None),
        P("tp", DP),
        P(DP, "tp"),
        P(),
        P(None, DP),
        P(),
    )
    return jax.shard_map(
        on_device, mesh=fine, in_specs=placed, out_specs=P(None, DP, "tp"), check_vma=False
    )
```

```python
import jax
import jax.numpy as jnp
from jax import lax
from jax.experimental import pallas as pl
from jax.experimental.pallas import tpu as pltpu
from jax.sharding import Mesh, PartitionSpec as P

R = 64
CAP = 2
HCAP = 16
TAG = 128
DP = ("z_high", "z_low", "x", "core")
GROUP = ("z_low", "x", "core")
SWAP = [(0, 1), (1, 0)]


def pick(flags):
    return flags.astype(jnp.bfloat16)


def matmul(a, b):
    return jnp.dot(a, b, preferred_element_type=jnp.float32)


def narrow(a, b):
    return matmul(a, b).astype(jnp.bfloat16)


def sum_over_tp(part):
    if lax.axis_size("tp") == 2:
        return part + lax.ppermute(part, "tp", SWAP)
    return lax.psum(part, "tp")


def after(value, *others):
    return lax.optimization_barrier((value, *others))[0]


class Chain:
    def __init__(self):
        self.last = None

    def hold(self, value):
        self.last = value if self.last is None else after(value, self.last)
        return self.last

    def permute(self, value, axis, pairs):
        return lax.ppermute(self.hold(value), axis, pairs)

    def wait(self, *arrived):
        self.last = after(self.last, *arrived)


def kernel_params():
    return dict(
        compiler_params=pltpu.CompilerParams(vmem_limit_bytes=40 * 2**20),
        cost_estimate=pl.CostEstimate(flops=1, bytes_accessed=1, transcendentals=0),
    )


def pick_columns(store, expand, want_mine, want_other):
    depth, width = store.shape
    groups, lanes = want_mine.shape
    count = groups * lanes
    blocks = 8
    rows = depth // blocks

    def kernel(mine_held, other_held, mine_at, other_at, store_ref, expand_ref, mine_ref, first_ref, rest_ref, pick_mine, pick_other):
        step = pl.program_id(0)

        @pl.when(step == 0)
        def _():
            column = lax.broadcasted_iota(jnp.int32, (width, count), 0)
            pick_mine[...] = (column == mine_at[...]).astype(jnp.float32).astype(jnp.bfloat16)
            pick_other[...] = (column == other_at[...]).astype(jnp.float32).astype(jnp.bfloat16)

        def fill(out_ref, held, picker):
            for g in range(groups):
                at = slice(g * lanes, (g + 1) * lanes)

                @pl.when((held[g] > 0) & (step < blocks))
                def _():
                    out_ref[:, at] = narrow(store_ref[...], picker[:, at])

                @pl.when((held[g] > 0) & (step == blocks))
                def _():
                    product = lax.dot_general(
                        expand_ref[...], picker[:, at], (((0,), (0,)), ((), ())), preferred_element_type=jnp.float32
                    )
                    out_ref[:, at] = product.astype(jnp.bfloat16)

                @pl.when(held[g] == 0)
                def _():
                    out_ref[:, at] = jnp.zeros((rows, lanes), jnp.bfloat16)

        fill(mine_ref, mine_held, pick_mine)

        @pl.when(step < 3)
        def _():
            fill(first_ref, other_held, pick_other)

        @pl.when(step >= 3)
        def _():
            fill(rest_ref, other_held, pick_other)

    out = lambda thirds: jax.ShapeDtypeStruct((3 * rows * thirds, count), jnp.bfloat16)
    index = pl.BlockSpec((1, count), lambda i, *held: (0, 0))
    return pl.pallas_call(
        kernel,
        grid_spec=pltpu.PrefetchScalarGridSpec(
            num_scalar_prefetch=2,
            grid=(blocks + 1,),
            in_specs=[
                index,
                index,
                pl.BlockSpec((rows, width), lambda i, *held: (jnp.minimum(i, blocks - 1), 0)),
                pl.BlockSpec(expand.shape, lambda i, *held: (0, 0)),
            ],
            out_specs=[
                pl.BlockSpec((rows, count), lambda i, *held: (i, 0)),
                pl.BlockSpec((rows, count), lambda i, *held: (jnp.minimum(i, 2), 0)),
                pl.BlockSpec((rows, count), lambda i, *held: (jnp.maximum(i - 3, 0), 0)),
            ],
            scratch_shapes=[pltpu.VMEM((width, count), jnp.bfloat16)] * 2,
        ),
        out_shape=[out(3), out(1), out(2)],
        **kernel_params(),
    )(
        jnp.any(want_mine >= 0, axis=1).astype(jnp.int32),
        jnp.any(want_other >= 0, axis=1).astype(jnp.int32),
        want_mine.reshape(1, -1),
        want_other.reshape(1, -1),
        store,
        expand,
    )


def place_rows(rows, hot_target, cold_target, tag, hot_rows, cold_rows):
    count, depth = rows.shape
    blocks = 4
    width = depth // blocks

    def kernel(hot_at, cold_at, tag_at, rows_ref, hot_ref, cold_ref, place_hot, place_cold):
        step = pl.program_id(0)

        @pl.when(step == 0)
        def _():
            hot_hit = lax.broadcasted_iota(jnp.int32, (hot_rows, count), 0) == hot_at[...]
            cold_hit = lax.broadcasted_iota(jnp.int32, (cold_rows, count), 0) == cold_at[...]
            place_hot[...] = hot_hit.astype(jnp.float32).astype(jnp.bfloat16)
            place_cold[...] = cold_hit.astype(jnp.float32).astype(jnp.bfloat16)
            tags = jnp.sum(jnp.where(cold_hit, tag_at[...].astype(jnp.float32), 0.0), axis=1, keepdims=True)
            cold_ref[:, depth:] = jnp.broadcast_to(tags, (cold_rows, TAG)).astype(jnp.bfloat16)

        block = rows_ref[...]
        hot_ref[...] = narrow(place_hot[...], block)
        cold_ref[:, pl.ds(pl.multiple_of(step * width, 128), width)] = narrow(place_cold[...], block)

    index = pl.BlockSpec((1, count), lambda j: (0, 0))
    return pl.pallas_call(
        kernel,
        grid=(blocks,),
        in_specs=[index, index, index, pl.BlockSpec((count, width), lambda j: (0, j))],
        out_specs=[
            pl.BlockSpec((hot_rows, width), lambda j: (0, j)),
            pl.BlockSpec((cold_rows, depth + TAG), lambda j: (0, 0)),
        ],
        out_shape=[
            jax.ShapeDtypeStruct((hot_rows, depth), jnp.bfloat16),
            jax.ShapeDtypeStruct((cold_rows, depth + TAG), jnp.bfloat16),
        ],
        scratch_shapes=[pltpu.VMEM((hot_rows, count), jnp.bfloat16), pltpu.VMEM((cold_rows, count), jnp.bfloat16)],
        **kernel_params(),
    )(hot_target[None], cold_target[None], tag[None], rows)


def base_halves(rows, weight):
    count, depth = rows.shape
    width = weight.shape[1]
    half = width // 2
    blocks = 8
    part = depth // blocks

    def kernel(tp_at, rows_ref, weight_ref, own_ref, other_ref, total):
        step = pl.program_id(0)
        product = matmul(rows_ref[...], weight_ref[...])

        @pl.when(step == 0)
        def _():
            total[...] = product

        @pl.when(step > 0)
        def _():
            total[...] += product

        @pl.when(step == blocks - 1)
        def _():
            first = pl.multiple_of(tp_at[0] * half, 128)
            second = pl.multiple_of((1 - tp_at[0]) * half, 128)
            own_ref[...] = total[:, pl.ds(first, half)]
            other_ref[...] = total[:, pl.ds(second, half)]

    out = pl.BlockSpec((count, half), lambda k, at: (0, 0))
    return pl.pallas_call(
        kernel,
        grid_spec=pltpu.PrefetchScalarGridSpec(
            num_scalar_prefetch=1,
            grid=(blocks,),
            in_specs=[
                pl.BlockSpec((count, part), lambda k, at: (0, k)),
                pl.BlockSpec((part, width), lambda k, at: (k, 0)),
            ],
            out_specs=[out, out],
            scratch_shapes=[pltpu.VMEM((count, width), jnp.float32)],
        ),
        out_shape=[jax.ShapeDtypeStruct((count, half), jnp.float32)] * 2,
        **kernel_params(),
    )(lax.axis_index("tp").astype(jnp.int32)[None], rows, weight)


def hot_expand(z_own, z_got, factors, head):
    kept = factors[0].shape[1]
    near = kept // R
    count = z_own.shape[0] // HCAP

    def kernel(own_ref, got_ref, first_ref, second_ref, out_ref):
        z = (own_ref[...] + got_ref[...]).astype(jnp.bfloat16).astype(jnp.float32).reshape(count, 1, HCAP, kept)
        shape = (count, near, HCAP, kept)
        same = lax.broadcasted_iota(jnp.int32, shape, 3) // R == lax.broadcasted_iota(jnp.int32, shape, 1)
        spread = jnp.where(same, jnp.broadcast_to(z, shape), 0.0).astype(jnp.bfloat16)
        product = lax.dot_general(
            spread.reshape(count * near * HCAP, kept),
            first_ref[-head:] + second_ref[-head:],
            (((1,), (1,)), ((), ())),
            preferred_element_type=jnp.float32,
        )
        out_ref[...] = product.astype(jnp.bfloat16)

    return pl.pallas_call(
        kernel,
        out_shape=jax.ShapeDtypeStruct((count * near * HCAP, head), jnp.bfloat16),
        **kernel_params(),
    )(z_own, z_got, *factors)


def add_hot(partial, target, delta):
    count = partial.shape[0]
    hot_rows = delta.shape[0]

    def kernel(partial_ref, target_ref, delta_ref, out_ref):
        hit = lax.broadcasted_iota(jnp.int32, (count, hot_rows), 1) == target_ref[...]
        place = hit.astype(jnp.float32).astype(jnp.bfloat16)
        out_ref[...] = (partial_ref[...] + matmul(place, delta_ref[...])).astype(jnp.bfloat16)

    return pl.pallas_call(
        kernel,
        out_shape=jax.ShapeDtypeStruct(partial.shape, jnp.bfloat16),
        **kernel_params(),
    )(partial, target[:, None], delta)


def on_device(
    activations, value_weight, shrink_store, expand_store, adapter_row, token_adapter, hot_ids
):
    step_count, token_count, depth = activations.shape
    adapter_count = adapter_row.shape[0]
    hot_count = hot_ids.shape[1]
    per_dev = expand_store.shape[0] // R
    head_part = expand_store.shape[1]
    far_count = lax.axis_size("z_high")
    group_count = 8
    dp_count = far_count * group_count
    me = lax.axis_index(DP)
    z_at, x_at, core_at = lax.axis_index("z_low"), lax.axis_index("x"), lax.axis_index("core")
    none_code = adapter_count + hot_count
    rows = activations.reshape(step_count * token_count, depth)

    near = step_count // 2
    names = jnp.arange(adapter_count, dtype=jnp.int32)
    chain = Chain()

    cold_row = jnp.sum(jnp.where((token_adapter - hot_count)[:, :, None] == names, adapter_row, 0), axis=-1)
    is_hot = token_adapter < hot_count
    is_cold = (token_adapter < none_code) & jnp.logical_not(is_hot)
    owner = cold_row // per_dev
    group = jnp.where(is_hot, token_adapter, jnp.where(is_cold, hot_count + owner, -1))
    at = jnp.arange(token_count, dtype=jnp.int32)
    before = (group[:, :, None] == group[:, None, :]) & (at[None, :] < at[:, None])
    rank = jnp.sum(before.astype(jnp.int32), axis=-1)
    step_at = jnp.arange(step_count, dtype=jnp.int32)[:, None]
    hot_rows = hot_count * step_count * HCAP
    cold_rows = dp_count * step_count * CAP
    server = (step_at // near) * hot_count + token_adapter
    hot_target = (server * near + step_at % near) * HCAP + rank
    cold_target = (owner * step_count + step_at) * CAP + rank
    hot_target = jnp.where(is_hot, hot_target, -1).reshape(-1)
    cold_target = jnp.where(is_cold, cold_target, -1).reshape(-1)

    hot_out, packet = place_rows(
        rows, hot_target, cold_target, (cold_row % per_dev + 1).reshape(-1), hot_rows, cold_rows
    )
    hot_out = chain.hold(hot_out.reshape(group_count, near * HCAP, depth))
    done = {"hot_in": lax.all_to_all(hot_out, GROUP, split_axis=0, concat_axis=0, tiled=True)}

    hot_row = jnp.sum(jnp.where(hot_ids[:, :, None] == names, adapter_row, 0), axis=-1)
    hot_first = jnp.where(hot_row // per_dev == me, (hot_row % per_dev) * R, -R * per_dev)
    column = jnp.arange(per_dev * R, dtype=jnp.int32)
    lane = jnp.arange(R, dtype=jnp.int32)
    entry = jnp.arange(hot_count, dtype=jnp.int32)

    def wanted(core):
        firsts = []
        for x in (x_at, 1 - x_at):
            of_steps = jnp.sum(jnp.where(entry == 2 * x + core, hot_first, 0), axis=1)
            firsts += [jnp.where(z_at == 0, of_steps[:near], of_steps[near:])]
            firsts += [jnp.where(z_at == 0, of_steps[near:], of_steps[:near])]
        return jnp.stack([(f[:, None] + lane).reshape(-1) for f in firsts])

    want_mine, want_other = wanted(core_at), wanted(1 - core_at)
    kept = near * R
    chunk_count = 3
    part = (depth + head_part) // chunk_count

    hops = [("x", SWAP), ("z_low", SWAP)]
    bit = 1
    while bit < far_count:
        hops.append(("z_high", [(i, i ^ bit) for i in range(far_count)]))
        bit *= 2
    mine, swapped, got, held = {}, {}, {}, {}

    def operand(c, stage):
        if stage == 0:
            return mine[c][:, 2 * kept:] + swapped[c][:, 2 * kept:]
        if stage == 1:
            return mine[c][:, kept:2 * kept] + swapped[c][:, kept:2 * kept] + got[c, 0][:, kept:]
        if stage == 2:
            held[c] = mine[c][:, :kept] + swapped[c][:, :kept] + got[c, 0][:, :kept] + got[c, 1]
        else:
            held[c] = held[c] + got[c, stage - 1]
        return held[c]

    def send(c, stage):
        got[c, stage] = chain.permute(operand(c, stage), *hops[stage])

    mine_all, other_first, other_rest = pick_columns(
        after(shrink_store, chain.last), expand_store, want_mine, want_other
    )
    mine[0], swapped[0] = mine_all[:part], chain.permute(other_first, "core", SWAP)
    rest_swapped = chain.permute(other_rest, "core", SWAP)
    send(0, 0)

    def cold_tokens_out():
        sent = chain.hold(packet.reshape(dp_count, step_count * CAP, depth + TAG))
        sent = lax.all_to_all(sent, DP, split_axis=0, concat_axis=0, tiled=True)
        done["packet"] = sent.reshape(cold_rows, depth + TAG)

    def base_product():
        weight = after(value_weight, chain.last)
        if lax.axis_size("tp") == 2:
            done["base_own"], done["base_other"] = base_halves(rows, weight)
        else:
            done["base_own"], done["base_other"] = jnp.zeros((1, 1), jnp.float32), matmul(rows, weight)

    def base_over_tp():
        if lax.axis_size("tp") == 2:
            done["base_got"] = chain.permute(done["base_other"], "tp", SWAP)
        else:
            whole = chain.hold(done["base_other"])
            done["base_got"] = lax.psum_scatter(whole, "tp", scatter_dimension=1, tiled=True)

    def cold_shrink():
        tag_in = done["packet"][:, depth:depth + 1].astype(jnp.int32)
        chosen = (column // R + 1)[None, :] == tag_in
        product = matmul(done["packet"][:, :depth], after(shrink_store, chain.last))
        done["z_part"] = jnp.where(chosen, product, 0.0)

    def cold_over_tp():
        done["z_cold"] = sum_over_tp(chain.hold(done["z_part"]))

    def cold_expand():
        done["delta"] = narrow(done["z_cold"].astype(jnp.bfloat16), after(expand_store, chain.last))

    def cold_back():
        delta = chain.hold(done["delta"].reshape(dp_count, step_count * CAP, head_part))
        delta = lax.all_to_all(delta, DP, split_axis=0, concat_axis=0, tiled=True)
        done["delta_cold"] = delta.reshape(cold_rows, head_part)

    def all_but_hot():
        place_cold = pick(jnp.arange(cold_rows, dtype=jnp.int32)[:, None] == cold_target)
        partial = lax.dot_general(
            place_cold, done["delta_cold"], (((0,), (0,)), ((), ())), preferred_element_type=jnp.float32
        )
        done["partial"] = partial + done["base_own"] + done["base_got"]

    between = {
        0: [cold_tokens_out],
        1: [base_product],
        2: [cold_shrink, cold_over_tp, base_over_tp],
        4: [cold_expand, cold_back, all_but_hot],
    }
    awaited = {0: ["hot_in"], 1: ["packet", "base_own", "base_other"], 2: ["z_cold"], 3: ["base_got"]}
    for slot in range(chunk_count + len(hops) - 1):
        if slot > 0:
            if slot < chunk_count:
                mine[slot] = after(mine_all, chain.last)[slot * part:(slot + 1) * part]
                swapped[slot] = after(rest_swapped, chain.last)[(slot - 1) * part:slot * part]
            for stage in sorted(range(len(hops)), key=lambda stage: stage == 1):
                if 0 <= slot - stage < chunk_count:
                    send(slot - stage, stage)
        for work in between.get(slot, []):
            work()
        here = [(slot - stage, stage) for stage in range(len(hops)) if 0 <= slot - stage < chunk_count]
        names_here = awaited.get(slot, [])
        arrived = lax.optimization_barrier(
            (chain.last, *[got[at] for at in here], *[done[name] for name in names_here])
        )
        chain.last = arrived[0]
        got.update(zip(here, arrived[1:]))
        done.update(zip(names_here, arrived[1 + len(here):]))
    partial = done["partial"]

    hot_in = done["hot_in"].reshape(hot_rows, depth)
    dense = None
    for c in range(chunk_count):
        last = min((c + 1) * part, depth)
        for piece in (held[c], got[c, len(hops) - 1]):
            product = matmul(hot_in[:, c * part:last], piece[:last - c * part])
            dense = product if dense is None else dense + product
    dense = dense.reshape(group_count, near, HCAP, kept)
    at_step = jnp.arange(kept) // R
    z_part = sum(jnp.where(at_step == i, dense[:, i], 0.0) for i in range(near)).reshape(group_count * HCAP, kept)
    if lax.axis_size("tp") == 2:
        z_got = lax.ppermute(z_part, "tp", SWAP)
    else:
        z_part = lax.psum(z_part, "tp")
        z_got = jnp.zeros_like(z_part)
    delta_hot = hot_expand(z_part, z_got, (held[c], got[c, len(hops) - 1]), head_part).reshape(group_count, near * HCAP, head_part)
    delta_hot = lax.all_to_all(delta_hot, GROUP, split_axis=0, concat_axis=0, tiled=True)
    added = add_hot(partial, hot_target, delta_hot.reshape(hot_rows, head_part))
    return added.reshape(step_count, token_count, head_part)


def solution(mesh):
    tp_count, dp_count = mesh.shape["tp"], mesh.shape["dp"]
    fine = Mesh(mesh.devices.reshape(tp_count, dp_count // 8, 2, 2, 2), ("tp", *DP))
    placed = (
        P(None, DP, "tp"),
        P("tp", None),
        P("tp", DP),
        P(DP, "tp"),
        P(),
        P(None, DP),
        P(),
    )
    return jax.shard_map(
        on_device, mesh=fine, in_specs=placed, out_specs=P(None, DP, "tp"), check_vma=False
    )
```

```python
import jax
import jax.numpy as jnp
from jax import lax
from jax.experimental import pallas as pl
from jax.experimental.pallas import tpu as pltpu
from jax.sharding import Mesh, PartitionSpec as P

R = 64
CAP = 2
HCAP = 16
TAG = 128
DP = ("z_high", "z_low", "x", "core")
GROUP = ("z_low", "x", "core")
SWAP = [(0, 1), (1, 0)]


def pick(flags):
    return flags.astype(jnp.bfloat16)


def matmul(a, b):
    return jnp.dot(a, b, preferred_element_type=jnp.float32)


def narrow(a, b):
    return matmul(a, b).astype(jnp.bfloat16)


def sum_over_tp(part):
    if lax.axis_size("tp") == 2:
        return part + lax.ppermute(part, "tp", SWAP)
    return lax.psum(part, "tp")


def after(value, *others):
    return lax.optimization_barrier((value, *others))[0]


class Chain:
    def __init__(self):
        self.last = None

    def hold(self, value):
        self.last = value if self.last is None else after(value, self.last)
        return self.last

    def permute(self, value, axis, pairs):
        return lax.ppermute(self.hold(value), axis, pairs)

    def wait(self, *arrived):
        self.last = after(self.last, *arrived)


def kernel_params():
    return dict(
        compiler_params=pltpu.CompilerParams(vmem_limit_bytes=40 * 2**20),
        cost_estimate=pl.CostEstimate(flops=1, bytes_accessed=1, transcendentals=0),
    )


def pick_columns(store, expand, want_mine, want_other):
    depth, width = store.shape
    groups, lanes = want_mine.shape
    count = groups * lanes
    blocks = 8
    rows = depth // blocks

    def kernel(mine_held, other_held, mine_at, other_at, store_ref, expand_ref, mine_ref, first_ref, rest_ref, pick_mine, pick_other):
        step = pl.program_id(0)

        @pl.when(step == 0)
        def _():
            column = lax.broadcasted_iota(jnp.int32, (width, count), 0)
            pick_mine[...] = (column == mine_at[...]).astype(jnp.float32).astype(jnp.bfloat16)
            pick_other[...] = (column == other_at[...]).astype(jnp.float32).astype(jnp.bfloat16)

        def fill(out_ref, held, picker):
            for g in range(groups):
                at = slice(g * lanes, (g + 1) * lanes)

                @pl.when((held[g] > 0) & (step < blocks))
                def _():
                    out_ref[:, at] = narrow(store_ref[...], picker[:, at])

                @pl.when((held[g] > 0) & (step == blocks))
                def _():
                    product = lax.dot_general(
                        expand_ref[...], picker[:, at], (((0,), (0,)), ((), ())), preferred_element_type=jnp.float32
                    )
                    out_ref[:, at] = product.astype(jnp.bfloat16)

                @pl.when(held[g] == 0)
                def _():
                    out_ref[:, at] = jnp.zeros((rows, lanes), jnp.bfloat16)

        fill(mine_ref, mine_held, pick_mine)

        @pl.when(step < 3)
        def _():
            fill(first_ref, other_held, pick_other)

        @pl.when(step >= 3)
        def _():
            fill(rest_ref, other_held, pick_other)

    out = lambda thirds: jax.ShapeDtypeStruct((3 * rows * thirds, count), jnp.bfloat16)
    index = pl.BlockSpec((1, count), lambda i, *held: (0, 0))
    return pl.pallas_call(
        kernel,
        grid_spec=pltpu.PrefetchScalarGridSpec(
            num_scalar_prefetch=2,
            grid=(blocks + 1,),
            in_specs=[
                index,
                index,
                pl.BlockSpec((rows, width), lambda i, *held: (jnp.minimum(i, blocks - 1), 0)),
                pl.BlockSpec(expand.shape, lambda i, *held: (0, 0)),
            ],
            out_specs=[
                pl.BlockSpec((rows, count), lambda i, *held: (i, 0)),
                pl.BlockSpec((rows, count), lambda i, *held: (jnp.minimum(i, 2), 0)),
                pl.BlockSpec((rows, count), lambda i, *held: (jnp.maximum(i - 3, 0), 0)),
            ],
            scratch_shapes=[pltpu.VMEM((width, count), jnp.bfloat16)] * 2,
        ),
        out_shape=[out(3), out(1), out(2)],
        **kernel_params(),
    )(
        jnp.any(want_mine >= 0, axis=1).astype(jnp.int32),
        jnp.any(want_other >= 0, axis=1).astype(jnp.int32),
        want_mine.reshape(1, -1),
        want_other.reshape(1, -1),
        store,
        expand,
    )


def place_rows(rows, hot_target, cold_target, tag, hot_rows, cold_rows):
    count, depth = rows.shape
    blocks = 4
    width = depth // blocks

    def kernel(hot_at, cold_at, tag_at, rows_ref, hot_ref, cold_ref, place_hot, place_cold):
        step = pl.program_id(0)

        @pl.when(step == 0)
        def _():
            hot_hit = lax.broadcasted_iota(jnp.int32, (hot_rows, count), 0) == hot_at[...]
            cold_hit = lax.broadcasted_iota(jnp.int32, (cold_rows, count), 0) == cold_at[...]
            place_hot[...] = hot_hit.astype(jnp.float32).astype(jnp.bfloat16)
            place_cold[...] = cold_hit.astype(jnp.float32).astype(jnp.bfloat16)
            tags = jnp.sum(jnp.where(cold_hit, tag_at[...].astype(jnp.float32), 0.0), axis=1, keepdims=True)
            cold_ref[:, depth:] = jnp.broadcast_to(tags, (cold_rows, TAG)).astype(jnp.bfloat16)

        block = rows_ref[...]
        hot_ref[...] = narrow(place_hot[...], block)
        cold_ref[:, pl.ds(pl.multiple_of(step * width, 128), width)] = narrow(place_cold[...], block)

    index = pl.BlockSpec((1, count), lambda j: (0, 0))
    return pl.pallas_call(
        kernel,
        grid=(blocks,),
        in_specs=[index, index, index, pl.BlockSpec((count, width), lambda j: (0, j))],
        out_specs=[
            pl.BlockSpec((hot_rows, width), lambda j: (0, j)),
            pl.BlockSpec((cold_rows, depth + TAG), lambda j: (0, 0)),
        ],
        out_shape=[
            jax.ShapeDtypeStruct((hot_rows, depth), jnp.bfloat16),
            jax.ShapeDtypeStruct((cold_rows, depth + TAG), jnp.bfloat16),
        ],
        scratch_shapes=[pltpu.VMEM((hot_rows, count), jnp.bfloat16), pltpu.VMEM((cold_rows, count), jnp.bfloat16)],
        **kernel_params(),
    )(hot_target[None], cold_target[None], tag[None], rows)


def base_halves(rows, weight):
    count, depth = rows.shape
    width = weight.shape[1]
    half = width // 2
    blocks = 8
    part = depth // blocks

    def kernel(tp_at, rows_ref, weight_ref, own_ref, other_ref, total):
        step = pl.program_id(0)
        product = matmul(rows_ref[...], weight_ref[...])

        @pl.when(step == 0)
        def _():
            total[...] = product

        @pl.when(step > 0)
        def _():
            total[...] += product

        @pl.when(step == blocks - 1)
        def _():
            first = pl.multiple_of(tp_at[0] * half, 128)
            second = pl.multiple_of((1 - tp_at[0]) * half, 128)
            own_ref[...] = total[:, pl.ds(first, half)]
            other_ref[...] = total[:, pl.ds(second, half)]

    out = pl.BlockSpec((count, half), lambda k, at: (0, 0))
    return pl.pallas_call(
        kernel,
        grid_spec=pltpu.PrefetchScalarGridSpec(
            num_scalar_prefetch=1,
            grid=(blocks,),
            in_specs=[
                pl.BlockSpec((count, part), lambda k, at: (0, k)),
                pl.BlockSpec((part, width), lambda k, at: (k, 0)),
            ],
            out_specs=[out, out],
            scratch_shapes=[pltpu.VMEM((count, width), jnp.float32)],
        ),
        out_shape=[jax.ShapeDtypeStruct((count, half), jnp.float32)] * 2,
        **kernel_params(),
    )(lax.axis_index("tp").astype(jnp.int32)[None], rows, weight)


def hot_expand(z_pieces, factors, head, cold=None):
    kept = factors[0].shape[1]
    near = kept // R
    count = z_pieces[0].shape[0] // HCAP
    served = near * HCAP
    more = () if cold is None else (cold,)
    block = served + 16 * len(more)

    def kernel(*refs):
        first_ref, second_ref = refs[len(z_pieces):len(z_pieces) + 2]
        out_ref = refs[-1]
        z = sum(ref[...] for ref in refs[:len(z_pieces)])
        z = z.astype(jnp.bfloat16).astype(jnp.float32).reshape(count, 1, HCAP, kept)
        shape = (count, near, HCAP, kept)
        same = lax.broadcasted_iota(jnp.int32, shape, 3) // R == lax.broadcasted_iota(jnp.int32, shape, 1)
        spread = jnp.where(same, jnp.broadcast_to(z, shape), 0.0).astype(jnp.bfloat16)
        product = lax.dot_general(
            spread.reshape(count * served, kept),
            first_ref[-head:] + second_ref[-head:],
            (((1,), (1,)), ((), ())),
            preferred_element_type=jnp.float32,
        ).astype(jnp.bfloat16)
        for k in range(count):
            out_ref[k * block:k * block + served] = product[k * served:(k + 1) * served]
            if more:
                out_ref[k * block + served:(k + 1) * block] = refs[-2][16 * k:16 * (k + 1)]

    return pl.pallas_call(
        kernel,
        out_shape=jax.ShapeDtypeStruct((count * block, head), jnp.bfloat16),
        **kernel_params(),
    )(*z_pieces, *factors, *more)


def add_rows(bases, target, delta):
    count = bases[0].shape[0]
    placed = delta.shape[0]

    def kernel(target_ref, delta_ref, *refs):
        hit = lax.broadcasted_iota(jnp.int32, (count, placed), 1) == target_ref[...]
        place = hit.astype(jnp.float32).astype(jnp.bfloat16)
        base = sum(ref[...] for ref in refs[:-1])
        refs[-1][...] = (base + matmul(place, delta_ref[...])).astype(jnp.bfloat16)

    return pl.pallas_call(
        kernel,
        out_shape=jax.ShapeDtypeStruct(bases[0].shape, jnp.bfloat16),
        **kernel_params(),
    )(target[:, None], delta, *bases)


def on_device(
    activations, value_weight, shrink_store, expand_store, adapter_row, token_adapter, hot_ids
):
    step_count, token_count, depth = activations.shape
    adapter_count = adapter_row.shape[0]
    hot_count = hot_ids.shape[1]
    per_dev = expand_store.shape[0] // R
    head_part = expand_store.shape[1]
    far_count = lax.axis_size("z_high")
    group_count = 8
    dp_count = far_count * group_count
    me = lax.axis_index(DP)
    z_at, x_at, core_at = lax.axis_index("z_low"), lax.axis_index("x"), lax.axis_index("core")
    none_code = adapter_count + hot_count
    paired = far_count == 2 and lax.axis_size("tp") == 2
    rows = activations.reshape(step_count * token_count, depth)

    near = step_count // 2
    names = jnp.arange(adapter_count, dtype=jnp.int32)
    chain = Chain()

    cold_row = jnp.sum(jnp.where((token_adapter - hot_count)[:, :, None] == names, adapter_row, 0), axis=-1)
    is_hot = token_adapter < hot_count
    is_cold = (token_adapter < none_code) & jnp.logical_not(is_hot)
    owner = cold_row // per_dev
    group = jnp.where(is_hot, token_adapter, jnp.where(is_cold, hot_count + owner, -1))
    at = jnp.arange(token_count, dtype=jnp.int32)
    before = (group[:, :, None] == group[:, None, :]) & (at[None, :] < at[:, None])
    rank = jnp.sum(before.astype(jnp.int32), axis=-1)
    step_at = jnp.arange(step_count, dtype=jnp.int32)[:, None]
    hot_rows = hot_count * step_count * HCAP
    cold_rows = dp_count * step_count * CAP
    server = (step_at // near) * hot_count + token_adapter
    hot_target = (server * near + step_at % near) * HCAP + rank
    cold_target = (owner * step_count + step_at) * CAP + rank
    hot_target = jnp.where(is_hot, hot_target, -1).reshape(-1)
    cold_target = jnp.where(is_cold, cold_target, -1).reshape(-1)

    hot_out, packet = place_rows(
        rows, hot_target, cold_target, (cold_row % per_dev + 1).reshape(-1), hot_rows, cold_rows
    )
    hot_out = chain.hold(hot_out.reshape(group_count, near * HCAP, depth))
    done = {"hot_in": lax.all_to_all(hot_out, GROUP, split_axis=0, concat_axis=0, tiled=True)}

    hot_row = jnp.sum(jnp.where(hot_ids[:, :, None] == names, adapter_row, 0), axis=-1)
    hot_first = jnp.where(hot_row // per_dev == me, (hot_row % per_dev) * R, -R * per_dev)
    column = jnp.arange(per_dev * R, dtype=jnp.int32)
    lane = jnp.arange(R, dtype=jnp.int32)
    entry = jnp.arange(hot_count, dtype=jnp.int32)

    def wanted(core):
        firsts = []
        for x in (x_at, 1 - x_at):
            of_steps = jnp.sum(jnp.where(entry == 2 * x + core, hot_first, 0), axis=1)
            firsts += [jnp.where(z_at == 0, of_steps[:near], of_steps[near:])]
            firsts += [jnp.where(z_at == 0, of_steps[near:], of_steps[:near])]
        return jnp.stack([(f[:, None] + lane).reshape(-1) for f in firsts])

    want_mine, want_other = wanted(core_at), wanted(1 - core_at)
    kept = near * R
    chunk_count = 3
    part = (depth + head_part) // chunk_count

    hops = [("x", SWAP), ("z_low", SWAP)]
    bit = 1
    while bit < far_count:
        hops.append(("z_high", [(i, i ^ bit) for i in range(far_count)]))
        bit *= 2
    mine, swapped, got, held = {}, {}, {}, {}

    def operand(c, stage):
        if stage == 0:
            return mine[c][:, 2 * kept:] + swapped[c][:, 2 * kept:]
        if stage == 1:
            return mine[c][:, kept:2 * kept] + swapped[c][:, kept:2 * kept] + got[c, 0][:, kept:]
        if stage == 2:
            held[c] = mine[c][:, :kept] + swapped[c][:, :kept] + got[c, 0][:, :kept] + got[c, 1]
        else:
            held[c] = held[c] + got[c, stage - 1]
        return held[c]

    def send(c, stage):
        got[c, stage] = chain.permute(operand(c, stage), *hops[stage])

    mine_all, other_first, other_rest = pick_columns(
        after(shrink_store, chain.last), expand_store, want_mine, want_other
    )
    mine[0], swapped[0] = mine_all[:part], chain.permute(other_first, "core", SWAP)
    rest_swapped = chain.permute(other_rest, "core", SWAP)
    send(0, 0)

    def cold_tokens_out():
        sent = chain.hold(packet.reshape(dp_count, step_count * CAP, depth + TAG))
        sent = lax.all_to_all(sent, DP, split_axis=0, concat_axis=0, tiled=True)
        done["packet"] = sent.reshape(cold_rows, depth + TAG)

    def base_product():
        weight = after(value_weight, chain.last)
        if lax.axis_size("tp") == 2:
            done["base_own"], done["base_other"] = base_halves(rows, weight)
        else:
            done["base_own"], done["base_other"] = jnp.zeros((1, 1), jnp.float32), matmul(rows, weight)

    def base_over_tp():
        if lax.axis_size("tp") == 2:
            done["base_got"] = chain.permute(done["base_other"], "tp", SWAP)
        else:
            whole = chain.hold(done["base_other"])
            done["base_got"] = lax.psum_scatter(whole, "tp", scatter_dimension=1, tiled=True)

    def cold_shrink():
        tag_in = done["packet"][:, depth:depth + 1].astype(jnp.int32)
        chosen = (column // R + 1)[None, :] == tag_in
        product = matmul(done["packet"][:, :depth], after(shrink_store, chain.last))
        done["z_part"] = jnp.where(chosen, product, 0.0)

    def cold_over_tp():
        done["z_cold"] = sum_over_tp(chain.hold(done["z_part"]))

    def cold_expand():
        done["delta"] = narrow(done["z_cold"].astype(jnp.bfloat16), after(expand_store, chain.last))

    def cold_far_out():
        far_at = lax.axis_index("z_high")
        halves = done["delta"].reshape(2, group_count * step_count * CAP, head_part)
        done["cold_near"] = jnp.where(far_at == 0, halves[0], halves[1])
        done["cold_far"] = chain.permute(jnp.where(far_at == 0, halves[1], halves[0]), "z_high", SWAP)

    def far_rows_out():
        last_rows = done["hot_in"].reshape(hot_rows, depth)[:, (chunk_count - 1) * part:]
        done["far_rows"] = chain.permute(last_rows, "z_high", SWAP)

    def cold_back():
        delta = chain.hold(done["delta"].reshape(dp_count, step_count * CAP, head_part))
        delta = lax.all_to_all(delta, DP, split_axis=0, concat_axis=0, tiled=True)
        done["delta_cold"] = delta.reshape(cold_rows, head_part)

    def all_but_hot():
        place_cold = pick(jnp.arange(cold_rows, dtype=jnp.int32)[:, None] == cold_target)
        partial = lax.dot_general(
            place_cold, done["delta_cold"], (((0,), (0,)), ((), ())), preferred_element_type=jnp.float32
        )
        done["partial"] = partial + done["base_own"] + done["base_got"]

    if paired:
        slots = chunk_count + 1
        between = {
            0: [cold_tokens_out],
            1: [far_rows_out, base_product],
            2: [cold_shrink, cold_over_tp, base_over_tp],
            3: [cold_expand, cold_far_out],
        }
        awaited = {
            0: ["hot_in"],
            1: ["packet", "base_own", "base_other", "far_rows"],
            2: ["z_cold"],
            3: ["base_got", "cold_far"],
        }
    else:
        slots = chunk_count + len(hops) - 1
        between = {
            0: [cold_tokens_out],
            1: [base_product],
            2: [cold_shrink, cold_over_tp, base_over_tp],
            4: [cold_expand, cold_back, all_but_hot],
        }
        awaited = {0: ["hot_in"], 1: ["packet", "base_own", "base_other"], 2: ["z_cold"], 3: ["base_got"]}
    for slot in range(slots):
        if slot > 0:
            if slot < chunk_count:
                mine[slot] = after(mine_all, chain.last)[slot * part:(slot + 1) * part]
                swapped[slot] = after(rest_swapped, chain.last)[(slot - 1) * part:slot * part]
            for stage in sorted(range(len(hops)), key=lambda stage: stage == 1):
                if 0 <= slot - stage < chunk_count:
                    send(slot - stage, stage)
        for work in between.get(slot, []):
            work()
        here = [(slot - stage, stage) for stage in range(len(hops)) if 0 <= slot - stage < chunk_count]
        names_here = awaited.get(slot, [])
        arrived = lax.optimization_barrier(
            (chain.last, *[got[at] for at in here], *[done[name] for name in names_here])
        )
        chain.last = arrived[0]
        got.update(zip(here, arrived[1:]))
        done.update(zip(names_here, arrived[1 + len(here):]))

    hot_in = done["hot_in"].reshape(hot_rows, depth)
    at_step = jnp.arange(kept) // R

    def own_columns(dense):
        dense = dense.reshape(group_count, near, HCAP, kept)
        return sum(jnp.where(at_step == i, dense[:, i], 0.0) for i in range(near)).reshape(group_count * HCAP, kept)

    dense = None
    for c in range(chunk_count - 1 if paired else chunk_count):
        last = min((c + 1) * part, depth)
        for piece in (held[c], got[c, len(hops) - 1]):
            product = matmul(hot_in[:, c * part:last], piece[:last - c * part])
            dense = product if dense is None else dense + product
    final = chunk_count - 1
    if paired:
        operand(final, 2)
        held[final] = chain.hold(held[final])
        expand_got = lax.ppermute(held[final][-head_part:], "z_high", SWAP)
        both = jnp.concatenate([hot_in[:, final * part:], done["far_rows"]], axis=0)
        products = matmul(both, held[final][:depth - final * part])
        z_own, z_far = own_columns(dense + products[:hot_rows]), own_columns(products[hot_rows:])
        z_pieces = (
            z_own,
            lax.ppermute(z_own, "tp", SWAP),
            lax.ppermute(z_far, "z_high", SWAP),
            lax.ppermute(z_far, ("tp", "z_high"), [(i, 3 - i) for i in range(4)]),
        )
        cold = jnp.concatenate(
            [done[name].reshape(group_count, step_count * CAP, head_part) for name in ("cold_near", "cold_far")], axis=1
        )
        delta = hot_expand(z_pieces, (held[final], expand_got), head_part, cold.reshape(-1, head_part))
        far_off = (owner // group_count != lax.axis_index("z_high")).astype(jnp.int32)
        cold_place = (far_off * step_count + step_at) * CAP + rank
        block = near * HCAP + 2 * step_count * CAP
        target = jnp.where(
            is_hot,
            server * block + (step_at % near) * HCAP + rank,
            owner % group_count * block + near * HCAP + cold_place,
        )
        target = jnp.where(is_hot | is_cold, target, -1).reshape(-1)
        bases = (done["base_own"], done["base_got"])
    else:
        z_pieces = (lax.psum(own_columns(dense), "tp"),)
        delta = hot_expand(z_pieces, (held[final], got[final, len(hops) - 1]), head_part)
        target = hot_target
        bases = (done["partial"],)
    delta = delta.reshape(group_count, -1, head_part)
    delta = lax.all_to_all(delta, GROUP, split_axis=0, concat_axis=0, tiled=True)
    added = add_rows(bases, target, delta.reshape(-1, head_part))
    return added.reshape(step_count, token_count, head_part)


def solution(mesh):
    tp_count, dp_count = mesh.shape["tp"], mesh.shape["dp"]
    fine = Mesh(mesh.devices.reshape(tp_count, dp_count // 8, 2, 2, 2), ("tp", *DP))
    placed = (
        P(None, DP, "tp"),
        P("tp", None),
        P("tp", DP),
        P(DP, "tp"),
        P(),
        P(None, DP),
        P(),
    )
    return jax.shard_map(
        on_device, mesh=fine, in_specs=placed, out_specs=P(None, DP, "tp"), check_vma=False
    )
```

```python
import jax
import jax.numpy as jnp
from jax import lax
from jax.experimental import pallas as pl
from jax.experimental.pallas import tpu as pltpu
from jax.sharding import Mesh, PartitionSpec as P

R = 64
CAP = 2
HCAP = 16
TAG = 128
DP = ("z_high", "z_low", "x", "core")
GROUP = ("z_low", "x", "core")
SWAP = [(0, 1), (1, 0)]


def pick(flags):
    return flags.astype(jnp.bfloat16)


def matmul(a, b):
    return jnp.dot(a, b, preferred_element_type=jnp.float32)


def narrow(a, b):
    return matmul(a, b).astype(jnp.bfloat16)


def sum_over_tp(part):
    if lax.axis_size("tp") == 2:
        return part + lax.ppermute(part, "tp", SWAP)
    return lax.psum(part, "tp")


def after(value, *others):
    return lax.optimization_barrier((value, *others))[0]


class Chain:
    def __init__(self):
        self.last = None

    def hold(self, value):
        self.last = value if self.last is None else after(value, self.last)
        return self.last

    def permute(self, value, axis, pairs):
        return lax.ppermute(self.hold(value), axis, pairs)

    def wait(self, *arrived):
        self.last = after(self.last, *arrived)


def kernel_params():
    return dict(
        compiler_params=pltpu.CompilerParams(vmem_limit_bytes=40 * 2**20),
        cost_estimate=pl.CostEstimate(flops=1, bytes_accessed=1, transcendentals=0),
    )


def pick_columns(store, expand, want_mine, want_other):
    depth, width = store.shape
    groups, lanes = want_mine.shape
    count = groups * lanes
    blocks = 8
    rows = depth // blocks

    def kernel(mine_held, other_held, mine_at, other_at, store_ref, expand_ref, mine_ref, first_ref, rest_ref, pick_mine, pick_other):
        step = pl.program_id(0)

        @pl.when(step == 0)
        def _():
            column = lax.broadcasted_iota(jnp.int32, (width, count), 0)
            pick_mine[...] = (column == mine_at[...]).astype(jnp.float32).astype(jnp.bfloat16)
            pick_other[...] = (column == other_at[...]).astype(jnp.float32).astype(jnp.bfloat16)

        def fill(out_ref, held, picker):
            for g in range(groups):
                at = slice(g * lanes, (g + 1) * lanes)

                @pl.when((held[g] > 0) & (step < blocks))
                def _():
                    out_ref[:, at] = narrow(store_ref[...], picker[:, at])

                @pl.when((held[g] > 0) & (step == blocks))
                def _():
                    product = lax.dot_general(
                        expand_ref[...], picker[:, at], (((0,), (0,)), ((), ())), preferred_element_type=jnp.float32
                    )
                    out_ref[:, at] = product.astype(jnp.bfloat16)

                @pl.when(held[g] == 0)
                def _():
                    out_ref[:, at] = jnp.zeros((rows, lanes), jnp.bfloat16)

        fill(mine_ref, mine_held, pick_mine)

        @pl.when(step < 3)
        def _():
            fill(first_ref, other_held, pick_other)

        @pl.when(step >= 3)
        def _():
            fill(rest_ref, other_held, pick_other)

    out = lambda thirds: jax.ShapeDtypeStruct((3 * rows * thirds, count), jnp.bfloat16)
    index = pl.BlockSpec((1, count), lambda i, *held: (0, 0))
    return pl.pallas_call(
        kernel,
        grid_spec=pltpu.PrefetchScalarGridSpec(
            num_scalar_prefetch=2,
            grid=(blocks + 1,),
            in_specs=[
                index,
                index,
                pl.BlockSpec((rows, width), lambda i, *held: (jnp.minimum(i, blocks - 1), 0)),
                pl.BlockSpec(expand.shape, lambda i, *held: (0, 0)),
            ],
            out_specs=[
                pl.BlockSpec((rows, count), lambda i, *held: (i, 0)),
                pl.BlockSpec((rows, count), lambda i, *held: (jnp.minimum(i, 2), 0)),
                pl.BlockSpec((rows, count), lambda i, *held: (jnp.maximum(i - 3, 0), 0)),
            ],
            scratch_shapes=[pltpu.VMEM((width, count), jnp.bfloat16)] * 2,
        ),
        out_shape=[out(3), out(1), out(2)],
        **kernel_params(),
    )(
        jnp.any(want_mine >= 0, axis=1).astype(jnp.int32),
        jnp.any(want_other >= 0, axis=1).astype(jnp.int32),
        want_mine.reshape(1, -1),
        want_other.reshape(1, -1),
        store,
        expand,
    )


def place_cold(rows, target, tag, placed):
    count, depth = rows.shape
    blocks = 4
    width = depth // blocks

    def kernel(target_at, tag_at, rows_ref, out_ref, place):
        step = pl.program_id(0)

        @pl.when(step == 0)
        def _():
            hit = lax.broadcasted_iota(jnp.int32, (placed, count), 0) == target_at[...]
            place[...] = hit.astype(jnp.float32).astype(jnp.bfloat16)
            tags = jnp.sum(jnp.where(hit, tag_at[...].astype(jnp.float32), 0.0), axis=1, keepdims=True)
            out_ref[:, depth:] = jnp.broadcast_to(tags, (placed, TAG)).astype(jnp.bfloat16)

        out_ref[:, pl.ds(pl.multiple_of(step * width, 128), width)] = narrow(place[...], rows_ref[...])

    index = pl.BlockSpec((1, count), lambda j: (0, 0))
    return pl.pallas_call(
        kernel,
        grid=(blocks,),
        in_specs=[index, index, pl.BlockSpec((count, width), lambda j: (0, j))],
        out_specs=pl.BlockSpec((placed, depth + TAG), lambda j: (0, 0)),
        out_shape=jax.ShapeDtypeStruct((placed, depth + TAG), jnp.bfloat16),
        scratch_shapes=[pltpu.VMEM((placed, count), jnp.bfloat16)],
        **kernel_params(),
    )(target[None], tag[None], rows)


def base_halves(rows, weight):
    count, depth = rows.shape
    width = weight.shape[1]
    half = width // 2
    blocks = 8
    part = depth // blocks

    def kernel(tp_at, rows_ref, weight_ref, own_ref, other_ref, total):
        step = pl.program_id(0)
        product = matmul(rows_ref[...], weight_ref[...])

        @pl.when(step == 0)
        def _():
            total[...] = product

        @pl.when(step > 0)
        def _():
            total[...] += product

        @pl.when(step == blocks - 1)
        def _():
            first = pl.multiple_of(tp_at[0] * half, 128)
            second = pl.multiple_of((1 - tp_at[0]) * half, 128)
            own_ref[...] = total[:, pl.ds(first, half)]
            other_ref[...] = total[:, pl.ds(second, half)]

    out = pl.BlockSpec((count, half), lambda k, at: (0, 0))
    return pl.pallas_call(
        kernel,
        grid_spec=pltpu.PrefetchScalarGridSpec(
            num_scalar_prefetch=1,
            grid=(blocks,),
            in_specs=[
                pl.BlockSpec((count, part), lambda k, at: (0, k)),
                pl.BlockSpec((part, width), lambda k, at: (k, 0)),
            ],
            out_specs=[out, out],
            scratch_shapes=[pltpu.VMEM((count, width), jnp.float32)],
        ),
        out_shape=[jax.ShapeDtypeStruct((count, half), jnp.float32)] * 2,
        **kernel_params(),
    )(lax.axis_index("tp").astype(jnp.int32)[None], rows, weight)


def hot_expand(z_own, z_got, factors, head):
    kept = factors[0].shape[1]
    near = kept // R
    count = z_own.shape[0] // HCAP

    def kernel(own_ref, got_ref, first_ref, second_ref, out_ref):
        z = (own_ref[...] + got_ref[...]).astype(jnp.bfloat16).astype(jnp.float32).reshape(count, 1, HCAP, kept)
        shape = (count, near, HCAP, kept)
        same = lax.broadcasted_iota(jnp.int32, shape, 3) // R == lax.broadcasted_iota(jnp.int32, shape, 1)
        spread = jnp.where(same, jnp.broadcast_to(z, shape), 0.0).astype(jnp.bfloat16)
        product = lax.dot_general(
            spread.reshape(count * near * HCAP, kept),
            first_ref[-head:] + second_ref[-head:],
            (((1,), (1,)), ((), ())),
            preferred_element_type=jnp.float32,
        )
        out_ref[...] = product.astype(jnp.bfloat16)

    return pl.pallas_call(
        kernel,
        out_shape=jax.ShapeDtypeStruct((count * near * HCAP, head), jnp.bfloat16),
        **kernel_params(),
    )(z_own, z_got, *factors)


def add_hot(partial, target, delta):
    count = partial.shape[0]
    hot_rows = delta.shape[0]

    def kernel(partial_ref, target_ref, delta_ref, out_ref):
        hit = lax.broadcasted_iota(jnp.int32, (count, hot_rows), 1) == target_ref[...]
        place = hit.astype(jnp.float32).astype(jnp.bfloat16)
        out_ref[...] = (partial_ref[...] + matmul(place, delta_ref[...])).astype(jnp.bfloat16)

    return pl.pallas_call(
        kernel,
        out_shape=jax.ShapeDtypeStruct(partial.shape, jnp.bfloat16),
        **kernel_params(),
    )(partial, target[:, None], delta)


def on_device(
    activations, value_weight, shrink_store, expand_store, adapter_row, token_adapter, hot_ids
):
    step_count, token_count, depth = activations.shape
    adapter_count = adapter_row.shape[0]
    hot_count = hot_ids.shape[1]
    per_dev = expand_store.shape[0] // R
    head_part = expand_store.shape[1]
    far_count = lax.axis_size("z_high")
    group_count = 8
    dp_count = far_count * group_count
    me = lax.axis_index(DP)
    z_at, x_at, core_at = lax.axis_index("z_low"), lax.axis_index("x"), lax.axis_index("core")
    none_code = adapter_count + hot_count
    rows = activations.reshape(step_count * token_count, depth)

    near = step_count // 2
    names = jnp.arange(adapter_count, dtype=jnp.int32)
    chain = Chain()

    cold_row = jnp.sum(jnp.where((token_adapter - hot_count)[:, :, None] == names, adapter_row, 0), axis=-1)
    is_hot = token_adapter < hot_count
    is_cold = (token_adapter < none_code) & jnp.logical_not(is_hot)
    owner = cold_row // per_dev
    group = jnp.where(is_hot, token_adapter, jnp.where(is_cold, hot_count + owner, -1))
    at = jnp.arange(token_count, dtype=jnp.int32)
    before = (group[:, :, None] == group[:, None, :]) & (at[None, :] < at[:, None])
    rank = jnp.sum(before.astype(jnp.int32), axis=-1)
    step_at = jnp.arange(step_count, dtype=jnp.int32)[:, None]
    hot_rows = hot_count * step_count * HCAP
    cold_rows = dp_count * step_count * CAP
    server = (step_at // near) * hot_count + token_adapter
    hot_target = (server * near + step_at % near) * HCAP + rank
    cold_target = (owner * step_count + step_at) * CAP + rank
    hot_target = jnp.where(is_hot, hot_target, -1).reshape(-1)
    cold_target = jnp.where(is_cold, cold_target, -1).reshape(-1)

    place_hot = pick(jnp.arange(hot_rows, dtype=jnp.int32)[:, None] == hot_target)
    quarters = [slice(q * depth // 4, (q + 1) * depth // 4) for q in range(4)]
    hot_out = jnp.concatenate([narrow(place_hot, rows[:, q]) for q in quarters], axis=1)
    hot_out = chain.hold(hot_out.reshape(group_count, near * HCAP, depth))
    done = {"hot_in": lax.all_to_all(hot_out, GROUP, split_axis=0, concat_axis=0, tiled=True)}

    hot_ids = after(hot_ids, chain.last)
    hot_row = jnp.sum(jnp.where(hot_ids[:, :, None] == names, adapter_row, 0), axis=-1)
    hot_first = jnp.where(hot_row // per_dev == me, (hot_row % per_dev) * R, -R * per_dev)
    column = jnp.arange(per_dev * R, dtype=jnp.int32)
    lane = jnp.arange(R, dtype=jnp.int32)
    entry = jnp.arange(hot_count, dtype=jnp.int32)

    def wanted(core):
        firsts = []
        for x in (x_at, 1 - x_at):
            of_steps = jnp.sum(jnp.where(entry == 2 * x + core, hot_first, 0), axis=1)
            firsts += [jnp.where(z_at == 0, of_steps[:near], of_steps[near:])]
            firsts += [jnp.where(z_at == 0, of_steps[near:], of_steps[:near])]
        return jnp.stack([(f[:, None] + lane).reshape(-1) for f in firsts])

    want_mine, want_other = wanted(core_at), wanted(1 - core_at)
    kept = near * R
    chunk_count = 3
    part = (depth + head_part) // chunk_count

    hops = [("x", SWAP), ("z_low", SWAP)]
    bit = 1
    while bit < far_count:
        hops.append(("z_high", [(i, i ^ bit) for i in range(far_count)]))
        bit *= 2
    mine, swapped, got, held = {}, {}, {}, {}

    def operand(c, stage):
        if stage == 0:
            return mine[c][:, 2 * kept:] + swapped[c][:, 2 * kept:]
        if stage == 1:
            return mine[c][:, kept:2 * kept] + swapped[c][:, kept:2 * kept] + got[c, 0][:, kept:]
        if stage == 2:
            held[c] = mine[c][:, :kept] + swapped[c][:, :kept] + got[c, 0][:, :kept] + got[c, 1]
        else:
            held[c] = held[c] + got[c, stage - 1]
        return held[c]

    ready = {}

    def send(c, stage):
        value = ready[c] if stage == 0 and c in ready else operand(c, stage)
        got[c, stage] = chain.permute(value, *hops[stage])

    def view(c):
        mine[c] = after(mine_all, chain.last)[c * part:(c + 1) * part]
        swapped[c] = after(rest_swapped, chain.last)[(c - 1) * part:c * part]

    mine_all, other_first, other_rest = pick_columns(
        after(shrink_store, chain.last), expand_store, want_mine, want_other
    )
    mine[0], swapped[0] = mine_all[:part], chain.permute(other_first, "core", SWAP)
    rest_swapped = chain.permute(other_rest, "core", SWAP)
    send(0, 0)

    def cold_tokens_out():
        tag = (cold_row % per_dev + 1).reshape(-1)
        packet = place_cold(rows, after(cold_target, chain.last), tag, cold_rows)
        sent = chain.hold(packet.reshape(dp_count, step_count * CAP, depth + TAG))
        sent = lax.all_to_all(sent, DP, split_axis=0, concat_axis=0, tiled=True)
        done["packet"] = sent.reshape(cold_rows, depth + TAG)

    def base_product():
        weight = after(value_weight, chain.last)
        if lax.axis_size("tp") == 2:
            done["base_own"], done["base_other"] = base_halves(rows, weight)
        else:
            done["base_own"], done["base_other"] = jnp.zeros((1, 1), jnp.float32), matmul(rows, weight)

    def base_over_tp():
        if lax.axis_size("tp") == 2:
            done["base_got"] = chain.permute(done["base_other"], "tp", SWAP)
        else:
            whole = chain.hold(done["base_other"])
            done["base_got"] = lax.psum_scatter(whole, "tp", scatter_dimension=1, tiled=True)

    def cold_shrink():
        tag_in = done["packet"][:, depth:depth + 1].astype(jnp.int32)
        chosen = (column // R + 1)[None, :] == tag_in
        product = matmul(done["packet"][:, :depth], after(shrink_store, chain.last))
        done["z_part"] = jnp.where(chosen, product, 0.0)

    def cold_over_tp():
        done["z_cold"] = sum_over_tp(chain.hold(done["z_part"]))

    def cold_expand():
        done["delta"] = narrow(done["z_cold"].astype(jnp.bfloat16), after(expand_store, chain.last))

    def cold_back():
        delta = chain.hold(done["delta"].reshape(dp_count, step_count * CAP, head_part))
        delta = lax.all_to_all(delta, DP, split_axis=0, concat_axis=0, tiled=True)
        done["delta_cold"] = delta.reshape(cold_rows, head_part)

    def all_but_hot():
        place_cold = pick(jnp.arange(cold_rows, dtype=jnp.int32)[:, None] == cold_target)
        partial = lax.dot_general(
            place_cold, done["delta_cold"], (((0,), (0,)), ((), ())), preferred_element_type=jnp.float32
        )
        done["partial"] = partial + done["base_own"] + done["base_got"]

    between = {
        0: [cold_tokens_out],
        1: [base_product],
        2: [cold_shrink, cold_over_tp, base_over_tp],
        4: [cold_expand, cold_back, all_but_hot],
    }
    awaited = {0: ["hot_in"], 1: ["packet", "base_own", "base_other"], 2: ["z_cold"], 3: ["base_got"]}
    for slot in range(chunk_count + len(hops) - 1):
        if slot > 0:
            if slot == 1:
                view(1)
            for stage in sorted(range(len(hops)), key=lambda stage: stage == 1):
                if 0 <= slot - stage < chunk_count:
                    send(slot - stage, stage)
            if slot == 1:
                view(2)
                ready[2] = chain.hold(operand(2, 0))
        for work in between.get(slot, []):
            work()
        here = [(slot - stage, stage) for stage in range(len(hops)) if 0 <= slot - stage < chunk_count]
        names_here = awaited.get(slot, [])
        arrived = lax.optimization_barrier(
            (chain.last, *[got[at] for at in here], *[done[name] for name in names_here])
        )
        chain.last = arrived[0]
        got.update(zip(here, arrived[1:]))
        done.update(zip(names_here, arrived[1 + len(here):]))
    partial = done["partial"]

    hot_in = done["hot_in"].reshape(hot_rows, depth)
    dense = None
    for c in range(chunk_count):
        last = min((c + 1) * part, depth)
        for piece in (held[c], got[c, len(hops) - 1]):
            product = matmul(hot_in[:, c * part:last], piece[:last - c * part])
            dense = product if dense is None else dense + product
    dense = dense.reshape(group_count, near, HCAP, kept)
    at_step = jnp.arange(kept) // R
    z_part = sum(jnp.where(at_step == i, dense[:, i], 0.0) for i in range(near)).reshape(group_count * HCAP, kept)
    if lax.axis_size("tp") == 2:
        z_got = lax.ppermute(z_part, "tp", SWAP)
    else:
        z_part = lax.psum(z_part, "tp")
        z_got = jnp.zeros_like(z_part)
    delta_hot = hot_expand(z_part, z_got, (held[c], got[c, len(hops) - 1]), head_part).reshape(group_count, near * HCAP, head_part)
    delta_hot = lax.all_to_all(delta_hot, GROUP, split_axis=0, concat_axis=0, tiled=True)
    added = add_hot(partial, hot_target, delta_hot.reshape(hot_rows, head_part))
    return added.reshape(step_count, token_count, head_part)


def solution(mesh):
    tp_count, dp_count = mesh.shape["tp"], mesh.shape["dp"]
    fine = Mesh(mesh.devices.reshape(tp_count, dp_count // 8, 2, 2, 2), ("tp", *DP))
    placed = (
        P(None, DP, "tp"),
        P("tp", None),
        P("tp", DP),
        P(DP, "tp"),
        P(),
        P(None, DP),
        P(),
    )
    return jax.shard_map(
        on_device, mesh=fine, in_specs=placed, out_specs=P(None, DP, "tp"), check_vma=False
    )
```

```python
import jax
import jax.numpy as jnp
from jax import lax
from jax.experimental import pallas as pl
from jax.experimental.pallas import tpu as pltpu
from jax.sharding import Mesh, PartitionSpec as P

R = 64
CAP = 2
HCAP = 16
TAG = 128
DP = ("z_high", "z_low", "x", "core")
GROUP = ("z_low", "x", "core")
SWAP = [(0, 1), (1, 0)]


def pick(flags):
    return flags.astype(jnp.bfloat16)


def matmul(a, b):
    return jnp.dot(a, b, preferred_element_type=jnp.float32)


def narrow(a, b):
    return matmul(a, b).astype(jnp.bfloat16)


def after(value, *others):
    return lax.optimization_barrier((value, *others))[0]


class Chain:
    def __init__(self):
        self.last = None

    def hold(self, value):
        self.last = value if self.last is None else after(value, self.last)
        return self.last

    def permute(self, value, axis, pairs):
        return lax.ppermute(self.hold(value), axis, pairs)

    def wait(self, *arrived):
        self.last = after(self.last, *arrived)


def kernel_params():
    return dict(
        compiler_params=pltpu.CompilerParams(vmem_limit_bytes=40 * 2**20),
        cost_estimate=pl.CostEstimate(flops=1, bytes_accessed=1, transcendentals=0),
    )


def pick_columns(store, expand, want_mine, want_other):
    depth, width = store.shape
    groups, lanes = want_mine.shape
    count = groups * lanes
    blocks = 8
    rows = depth // blocks

    def kernel(mine_held, other_held, mine_at, other_at, store_ref, expand_ref, mine_ref, first_ref, rest_ref, pick_mine, pick_other):
        step = pl.program_id(0)

        @pl.when(step == 0)
        def _():
            column = lax.broadcasted_iota(jnp.int32, (width, count), 0)
            pick_mine[...] = (column == mine_at[...]).astype(jnp.float32).astype(jnp.bfloat16)
            pick_other[...] = (column == other_at[...]).astype(jnp.float32).astype(jnp.bfloat16)

        def fill(out_ref, held, picker):
            for g in range(groups):
                at = slice(g * lanes, (g + 1) * lanes)

                @pl.when((held[g] > 0) & (step < blocks))
                def _():
                    out_ref[:, at] = narrow(store_ref[...], picker[:, at])

                @pl.when((held[g] > 0) & (step == blocks))
                def _():
                    product = lax.dot_general(
                        expand_ref[...], picker[:, at], (((0,), (0,)), ((), ())), preferred_element_type=jnp.float32
                    )
                    out_ref[:, at] = product.astype(jnp.bfloat16)

                @pl.when(held[g] == 0)
                def _():
                    out_ref[:, at] = jnp.zeros((rows, lanes), jnp.bfloat16)

        fill(mine_ref, mine_held, pick_mine)

        @pl.when(step < 3)
        def _():
            fill(first_ref, other_held, pick_other)

        @pl.when(step >= 3)
        def _():
            fill(rest_ref, other_held, pick_other)

    out = lambda thirds: jax.ShapeDtypeStruct((3 * rows * thirds, count), jnp.bfloat16)
    index = pl.BlockSpec((1, count), lambda i, *held: (0, 0))
    return pl.pallas_call(
        kernel,
        grid_spec=pltpu.PrefetchScalarGridSpec(
            num_scalar_prefetch=2,
            grid=(blocks + 1,),
            in_specs=[
                index,
                index,
                pl.BlockSpec((rows, width), lambda i, *held: (jnp.minimum(i, blocks - 1), 0)),
                pl.BlockSpec(expand.shape, lambda i, *held: (0, 0)),
            ],
            out_specs=[
                pl.BlockSpec((rows, count), lambda i, *held: (i, 0)),
                pl.BlockSpec((rows, count), lambda i, *held: (jnp.minimum(i, 2), 0)),
                pl.BlockSpec((rows, count), lambda i, *held: (jnp.maximum(i - 3, 0), 0)),
            ],
            scratch_shapes=[pltpu.VMEM((width, count), jnp.bfloat16)] * 2,
        ),
        out_shape=[out(3), out(1), out(2)],
        **kernel_params(),
    )(
        jnp.any(want_mine >= 0, axis=1).astype(jnp.int32),
        jnp.any(want_other >= 0, axis=1).astype(jnp.int32),
        want_mine.reshape(1, -1),
        want_other.reshape(1, -1),
        store,
        expand,
    )


def place_rows(rows, hot_target, cold_target, tag, hot_rows, cold_rows):
    count, depth = rows.shape
    blocks = 4
    width = depth // blocks

    def kernel(hot_at, cold_at, tag_at, rows_ref, hot_ref, cold_ref, place_hot, place_cold):
        step = pl.program_id(0)

        @pl.when(step == 0)
        def _():
            hot_hit = lax.broadcasted_iota(jnp.int32, (hot_rows, count), 0) == hot_at[...]
            cold_hit = lax.broadcasted_iota(jnp.int32, (cold_rows, count), 0) == cold_at[...]
            place_hot[...] = hot_hit.astype(jnp.float32).astype(jnp.bfloat16)
            place_cold[...] = cold_hit.astype(jnp.float32).astype(jnp.bfloat16)
            tags = jnp.sum(jnp.where(cold_hit, tag_at[...].astype(jnp.float32), 0.0), axis=1, keepdims=True)
            cold_ref[:, depth:] = jnp.broadcast_to(tags, (cold_rows, TAG)).astype(jnp.bfloat16)

        block = rows_ref[...]
        hot_ref[...] = narrow(place_hot[...], block)
        cold_ref[:, pl.ds(pl.multiple_of(step * width, 128), width)] = narrow(place_cold[...], block)

    index = pl.BlockSpec((1, count), lambda j: (0, 0))
    return pl.pallas_call(
        kernel,
        grid=(blocks,),
        in_specs=[index, index, index, pl.BlockSpec((count, width), lambda j: (0, j))],
        out_specs=[
            pl.BlockSpec((hot_rows, width), lambda j: (0, j)),
            pl.BlockSpec((cold_rows, depth + TAG), lambda j: (0, 0)),
        ],
        out_shape=[
            jax.ShapeDtypeStruct((hot_rows, depth), jnp.bfloat16),
            jax.ShapeDtypeStruct((cold_rows, depth + TAG), jnp.bfloat16),
        ],
        scratch_shapes=[pltpu.VMEM((hot_rows, count), jnp.bfloat16), pltpu.VMEM((cold_rows, count), jnp.bfloat16)],
        **kernel_params(),
    )(hot_target[None], cold_target[None], tag[None], rows)


def base_halves(rows, weight):
    count, depth = rows.shape
    width = weight.shape[1]
    half = width // 2
    blocks = 8
    part = depth // blocks

    def kernel(tp_at, rows_ref, weight_ref, own_ref, other_ref, total):
        step = pl.program_id(0)
        product = matmul(rows_ref[...], weight_ref[...])

        @pl.when(step == 0)
        def _():
            total[...] = product

        @pl.when(step > 0)
        def _():
            total[...] += product

        @pl.when(step == blocks - 1)
        def _():
            first = pl.multiple_of(tp_at[0] * half, 128)
            second = pl.multiple_of((1 - tp_at[0]) * half, 128)
            own_ref[...] = total[:, pl.ds(first, half)]
            other_ref[...] = total[:, pl.ds(second, half)]

    out = pl.BlockSpec((count, half), lambda k, at: (0, 0))
    return pl.pallas_call(
        kernel,
        grid_spec=pltpu.PrefetchScalarGridSpec(
            num_scalar_prefetch=1,
            grid=(blocks,),
            in_specs=[
                pl.BlockSpec((count, part), lambda k, at: (0, k)),
                pl.BlockSpec((part, width), lambda k, at: (k, 0)),
            ],
            out_specs=[out, out],
            scratch_shapes=[pltpu.VMEM((count, width), jnp.float32)],
        ),
        out_shape=[jax.ShapeDtypeStruct((count, half), jnp.float32)] * 2,
        **kernel_params(),
    )(lax.axis_index("tp").astype(jnp.int32)[None], rows, weight)


def hot_expand(z_own, z_got, factors, head):
    kept = factors[0].shape[1]
    near = kept // R
    count = z_own.shape[0] // HCAP

    def kernel(own_ref, got_ref, first_ref, second_ref, out_ref):
        z = (own_ref[...] + got_ref[...]).astype(jnp.bfloat16).astype(jnp.float32).reshape(count, 1, HCAP, kept)
        shape = (count, near, HCAP, kept)
        same = lax.broadcasted_iota(jnp.int32, shape, 3) // R == lax.broadcasted_iota(jnp.int32, shape, 1)
        spread = jnp.where(same, jnp.broadcast_to(z, shape), 0.0).astype(jnp.bfloat16)
        product = lax.dot_general(
            spread.reshape(count * near * HCAP, kept),
            first_ref[-head:] + second_ref[-head:],
            (((1,), (1,)), ((), ())),
            preferred_element_type=jnp.float32,
        )
        out_ref[...] = product.astype(jnp.bfloat16)

    return pl.pallas_call(
        kernel,
        out_shape=jax.ShapeDtypeStruct((count * near * HCAP, head), jnp.bfloat16),
        **kernel_params(),
    )(z_own, z_got, *factors)


def add_hot(partial, target, delta):
    count = partial.shape[0]
    hot_rows = delta.shape[0]

    def kernel(partial_ref, target_ref, delta_ref, out_ref):
        hit = lax.broadcasted_iota(jnp.int32, (count, hot_rows), 1) == target_ref[...]
        place = hit.astype(jnp.float32).astype(jnp.bfloat16)
        out_ref[...] = (partial_ref[...] + matmul(place, delta_ref[...])).astype(jnp.bfloat16)

    return pl.pallas_call(
        kernel,
        out_shape=jax.ShapeDtypeStruct(partial.shape, jnp.bfloat16),
        **kernel_params(),
    )(partial, target[:, None], delta)


def on_device(
    activations, value_weight, shrink_store, expand_store, adapter_row, token_adapter, hot_ids
):
    step_count, token_count, depth = activations.shape
    adapter_count = adapter_row.shape[0]
    hot_count = hot_ids.shape[1]
    per_dev = expand_store.shape[0] // R
    head_part = expand_store.shape[1]
    far_count = lax.axis_size("z_high")
    group_count = 8
    dp_count = far_count * group_count
    me = lax.axis_index(DP)
    z_at, x_at, core_at = lax.axis_index("z_low"), lax.axis_index("x"), lax.axis_index("core")
    none_code = adapter_count + hot_count
    rows = activations.reshape(step_count * token_count, depth)

    near = step_count // 2
    names = jnp.arange(adapter_count, dtype=jnp.int32)
    chain = Chain()

    cold_row = jnp.sum(jnp.where((token_adapter - hot_count)[:, :, None] == names, adapter_row, 0), axis=-1)
    is_hot = token_adapter < hot_count
    is_cold = (token_adapter < none_code) & jnp.logical_not(is_hot)
    owner = cold_row // per_dev
    group = jnp.where(is_hot, token_adapter, jnp.where(is_cold, hot_count + owner, -1))
    at = jnp.arange(token_count, dtype=jnp.int32)
    before = (group[:, :, None] == group[:, None, :]) & (at[None, :] < at[:, None])
    rank = jnp.sum(before.astype(jnp.int32), axis=-1)
    step_at = jnp.arange(step_count, dtype=jnp.int32)[:, None]
    hot_rows = hot_count * step_count * HCAP
    cold_rows = dp_count * step_count * CAP
    server = (step_at // near) * hot_count + token_adapter
    hot_target = (server * near + step_at % near) * HCAP + rank
    cold_target = (owner * step_count + step_at) * CAP + rank
    hot_target = jnp.where(is_hot, hot_target, -1).reshape(-1)
    cold_target = jnp.where(is_cold, cold_target, -1).reshape(-1)

    hot_out, packet = place_rows(
        rows, hot_target, cold_target, (cold_row % per_dev + 1).reshape(-1), hot_rows, cold_rows
    )
    hot_out = chain.hold(hot_out.reshape(group_count, near * HCAP, depth))
    done = {"hot_in": lax.all_to_all(hot_out, GROUP, split_axis=0, concat_axis=0, tiled=True)}

    hot_row = jnp.sum(jnp.where(hot_ids[:, :, None] == names, adapter_row, 0), axis=-1)
    hot_first = jnp.where(hot_row // per_dev == me, (hot_row % per_dev) * R, -R * per_dev)
    column = jnp.arange(per_dev * R, dtype=jnp.int32)
    lane = jnp.arange(R, dtype=jnp.int32)
    entry = jnp.arange(hot_count, dtype=jnp.int32)

    def wanted(core):
        firsts = []
        for x in (x_at, 1 - x_at):
            of_steps = jnp.sum(jnp.where(entry == 2 * x + core, hot_first, 0), axis=1)
            firsts += [jnp.where(z_at == 0, of_steps[:near], of_steps[near:])]
            firsts += [jnp.where(z_at == 0, of_steps[near:], of_steps[:near])]
        return jnp.stack([(f[:, None] + lane).reshape(-1) for f in firsts])

    want_mine, want_other = wanted(core_at), wanted(1 - core_at)
    kept = near * R
    chunk_count = 3
    part = (depth + head_part) // chunk_count

    hops = [("x", SWAP), ("z_low", SWAP)]
    bit = 1
    while bit < far_count:
        hops.append(("z_high", [(i, i ^ bit) for i in range(far_count)]))
        bit *= 2
    mine, swapped, got, held = {}, {}, {}, {}

    def operand(c, stage):
        if stage == 0:
            return mine[c][:, 2 * kept:] + swapped[c][:, 2 * kept:]
        if stage == 1:
            return mine[c][:, kept:2 * kept] + swapped[c][:, kept:2 * kept] + got[c, 0][:, kept:]
        if stage == 2:
            held[c] = mine[c][:, :kept] + swapped[c][:, :kept] + got[c, 0][:, :kept] + got[c, 1]
        else:
            held[c] = held[c] + got[c, stage - 1]
        return held[c]

    def send(c, stage):
        got[c, stage] = chain.permute(operand(c, stage), *hops[stage])

    def view(c):
        mine[c] = after(mine_all, chain.last)[c * part:(c + 1) * part]
        swapped[c] = after(rest_swapped, chain.last)[(c - 1) * part:c * part]

    mine_all, other_first, other_rest = pick_columns(
        after(shrink_store, chain.last), expand_store, want_mine, want_other
    )
    mine[0], swapped[0] = mine_all[:part], chain.permute(other_first, "core", SWAP)
    rest_swapped = chain.permute(other_rest, "core", SWAP)
    send(0, 0)

    def cold_tokens_out():
        sent = chain.hold(packet.reshape(dp_count, step_count * CAP, depth + TAG))
        sent = lax.all_to_all(sent, DP, split_axis=0, concat_axis=0, tiled=True)
        done["packet"] = sent.reshape(cold_rows, depth + TAG)

    def base_product():
        weight = after(value_weight, chain.last)
        if lax.axis_size("tp") == 2:
            done["base_own"], done["base_other"] = base_halves(rows, weight)
        else:
            done["base_own"], done["base_other"] = jnp.zeros((1, 1), jnp.float32), matmul(rows, weight)

    def base_over_tp():
        if lax.axis_size("tp") == 2:
            done["base_got"] = chain.permute(done["base_other"], "tp", SWAP)
        else:
            whole = chain.hold(done["base_other"])
            done["base_got"] = lax.psum_scatter(whole, "tp", scatter_dimension=1, tiled=True)

    def cold_shrink():
        tag_in = done["packet"][:, depth:depth + 1].astype(jnp.int32)
        chosen = (column // R + 1)[None, :] == tag_in
        product = matmul(done["packet"][:, :depth], after(shrink_store, chain.last))
        done["z_part"] = jnp.where(chosen, product, 0.0)

    def cold_over_tp():
        z_part = chain.hold(done["z_part"])
        if lax.axis_size("tp") == 2:
            done["z_got"] = lax.ppermute(z_part, "tp", SWAP)
        else:
            done["z_part"], done["z_got"] = jnp.zeros_like(z_part), lax.psum(z_part, "tp")

    def cold_expand():
        z_cold = (done["z_part"] + done["z_got"]).astype(jnp.bfloat16)
        done["delta"] = narrow(z_cold, after(expand_store, chain.last))

    def cold_back():
        delta = chain.hold(done["delta"].reshape(dp_count, step_count * CAP, head_part))
        delta = lax.all_to_all(delta, DP, split_axis=0, concat_axis=0, tiled=True)
        done["delta_cold"] = delta.reshape(cold_rows, head_part)

    def all_but_hot():
        place_cold = pick(jnp.arange(cold_rows, dtype=jnp.int32)[:, None] == cold_target)
        partial = lax.dot_general(
            place_cold, done["delta_cold"], (((0,), (0,)), ((), ())), preferred_element_type=jnp.float32
        )
        done["partial"] = partial + done["base_own"] + done["base_got"]

    cold_tokens_out()
    chain.last, got[0, 0], done["hot_in"] = lax.optimization_barrier((chain.last, got[0, 0], done["hot_in"]))
    view(1)
    send(1, 0)
    send(0, 1)
    view(2)
    send(2, 0)
    if far_count == 2:
        send(0, 2)
        base_product()
        send(1, 1)
        chain.wait(got[0, 2], done["packet"], done["base_own"], done["base_other"])
        cold_shrink()
        cold_over_tp()
        base_over_tp()
        send(1, 2)
        send(2, 1)
        chain.last, _, done["z_got"] = lax.optimization_barrier((chain.last, got[1, 2], done["z_got"]))
        cold_expand()
        send(2, 2)
        cold_back()
    else:
        base_product()
        for c in range(chunk_count):
            for stage in range(1, len(hops)):
                if (c, stage) != (0, 1):
                    send(c, stage)
        base_over_tp()
        cold_shrink()
        cold_over_tp()
        cold_expand()
        cold_back()
    all_but_hot()
    partial = done["partial"]

    hot_in = done["hot_in"].reshape(hot_rows, depth)
    dense = None
    for c in range(chunk_count):
        last = min((c + 1) * part, depth)
        for piece in (held[c], got[c, len(hops) - 1]):
            product = matmul(hot_in[:, c * part:last], piece[:last - c * part])
            dense = product if dense is None else dense + product
    dense = dense.reshape(group_count, near, HCAP, kept)
    at_step = jnp.arange(kept) // R
    z_part = sum(jnp.where(at_step == i, dense[:, i], 0.0) for i in range(near)).reshape(group_count * HCAP, kept)
    if lax.axis_size("tp") == 2:
        z_got = lax.ppermute(z_part, "tp", SWAP)
    else:
        z_part = lax.psum(z_part, "tp")
        z_got = jnp.zeros_like(z_part)
    delta_hot = hot_expand(z_part, z_got, (held[c], got[c, len(hops) - 1]), head_part).reshape(group_count, near * HCAP, head_part)
    delta_hot = lax.all_to_all(delta_hot, GROUP, split_axis=0, concat_axis=0, tiled=True)
    added = add_hot(partial, hot_target, delta_hot.reshape(hot_rows, head_part))
    return added.reshape(step_count, token_count, head_part)


def solution(mesh):
    tp_count, dp_count = mesh.shape["tp"], mesh.shape["dp"]
    fine = Mesh(mesh.devices.reshape(tp_count, dp_count // 8, 2, 2, 2), ("tp", *DP))
    placed = (
        P(None, DP, "tp"),
        P("tp", None),
        P("tp", DP),
        P(DP, "tp"),
        P(),
        P(None, DP),
        P(),
    )
    return jax.shard_map(
        on_device, mesh=fine, in_specs=placed, out_specs=P(None, DP, "tp"), check_vma=False
    )
```

```python
import jax
import jax.numpy as jnp
from jax import lax
from jax.experimental import pallas as pl
from jax.experimental.pallas import tpu as pltpu
from jax.sharding import Mesh, PartitionSpec as P

R = 64
CAP = 2
HCAP = 16
TAG = 128
DP = ("z_high", "z_low", "x", "core")
GROUP = ("z_low", "x", "core")
SWAP = [(0, 1), (1, 0)]


def pick(flags):
    return flags.astype(jnp.bfloat16)


def matmul(a, b):
    return jnp.dot(a, b, preferred_element_type=jnp.float32)


def narrow(a, b):
    return matmul(a, b).astype(jnp.bfloat16)


def after(value, *others):
    return lax.optimization_barrier((value, *others))[0]


class Chain:
    def __init__(self):
        self.last = None

    def hold(self, value):
        self.last = value if self.last is None else after(value, self.last)
        return self.last

    def permute(self, value, axis, pairs):
        return lax.ppermute(self.hold(value), axis, pairs)

    def wait(self, *arrived):
        self.last = after(self.last, *arrived)


def kernel_params():
    return dict(
        compiler_params=pltpu.CompilerParams(vmem_limit_bytes=40 * 2**20),
        cost_estimate=pl.CostEstimate(flops=1, bytes_accessed=1, transcendentals=0),
    )


def pick_columns(store, expand, want_mine, want_other):
    depth, width = store.shape
    groups, lanes = want_mine.shape
    count = groups * lanes
    blocks = 8
    rows = depth // blocks

    def kernel(mine_held, other_held, mine_at, other_at, store_ref, expand_ref, mine_ref, first_ref, rest_ref, pick_mine, pick_other):
        step = pl.program_id(0)

        @pl.when(step == 0)
        def _():
            column = lax.broadcasted_iota(jnp.int32, (width, count), 0)
            pick_mine[...] = (column == mine_at[...]).astype(jnp.float32).astype(jnp.bfloat16)
            pick_other[...] = (column == other_at[...]).astype(jnp.float32).astype(jnp.bfloat16)

        def fill(out_ref, held, picker):
            for g in range(groups):
                at = slice(g * lanes, (g + 1) * lanes)

                @pl.when((held[g] > 0) & (step < blocks))
                def _():
                    out_ref[:, at] = narrow(store_ref[...], picker[:, at])

                @pl.when((held[g] > 0) & (step == blocks))
                def _():
                    product = lax.dot_general(
                        expand_ref[...], picker[:, at], (((0,), (0,)), ((), ())), preferred_element_type=jnp.float32
                    )
                    out_ref[:, at] = product.astype(jnp.bfloat16)

                @pl.when(held[g] == 0)
                def _():
                    out_ref[:, at] = jnp.zeros((rows, lanes), jnp.bfloat16)

        fill(mine_ref, mine_held, pick_mine)

        @pl.when(step < 3)
        def _():
            fill(first_ref, other_held, pick_other)

        @pl.when(step >= 3)
        def _():
            fill(rest_ref, other_held, pick_other)

    out = lambda thirds: jax.ShapeDtypeStruct((3 * rows * thirds, count), jnp.bfloat16)
    index = pl.BlockSpec((1, count), lambda i, *held: (0, 0))
    return pl.pallas_call(
        kernel,
        grid_spec=pltpu.PrefetchScalarGridSpec(
            num_scalar_prefetch=2,
            grid=(blocks + 1,),
            in_specs=[
                index,
                index,
                pl.BlockSpec((rows, width), lambda i, *held: (jnp.minimum(i, blocks - 1), 0)),
                pl.BlockSpec(expand.shape, lambda i, *held: (0, 0)),
            ],
            out_specs=[
                pl.BlockSpec((rows, count), lambda i, *held: (i, 0)),
                pl.BlockSpec((rows, count), lambda i, *held: (jnp.minimum(i, 2), 0)),
                pl.BlockSpec((rows, count), lambda i, *held: (jnp.maximum(i - 3, 0), 0)),
            ],
            scratch_shapes=[pltpu.VMEM((width, count), jnp.bfloat16)] * 2,
        ),
        out_shape=[out(3), out(1), out(2)],
        **kernel_params(),
    )(
        jnp.any(want_mine >= 0, axis=1).astype(jnp.int32),
        jnp.any(want_other >= 0, axis=1).astype(jnp.int32),
        want_mine.reshape(1, -1),
        want_other.reshape(1, -1),
        store,
        expand,
    )


def place_rows(rows, hot_target, cold_target, tag, hot_rows, cold_rows):
    count, depth = rows.shape
    blocks = 4
    width = depth // blocks

    def kernel(hot_at, cold_at, tag_at, rows_ref, hot_ref, cold_ref, place_hot, place_cold):
        step = pl.program_id(0)

        @pl.when(step == 0)
        def _():
            hot_hit = lax.broadcasted_iota(jnp.int32, (hot_rows, count), 0) == hot_at[...]
            cold_hit = lax.broadcasted_iota(jnp.int32, (cold_rows, count), 0) == cold_at[...]
            place_hot[...] = hot_hit.astype(jnp.float32).astype(jnp.bfloat16)
            place_cold[...] = cold_hit.astype(jnp.float32).astype(jnp.bfloat16)
            tags = jnp.sum(jnp.where(cold_hit, tag_at[...].astype(jnp.float32), 0.0), axis=1, keepdims=True)
            cold_ref[:, depth:] = jnp.broadcast_to(tags, (cold_rows, TAG)).astype(jnp.bfloat16)

        block = rows_ref[...]
        hot_ref[...] = narrow(place_hot[...], block)
        cold_ref[:, pl.ds(pl.multiple_of(step * width, 128), width)] = narrow(place_cold[...], block)

    index = pl.BlockSpec((1, count), lambda j: (0, 0))
    return pl.pallas_call(
        kernel,
        grid=(blocks,),
        in_specs=[index, index, index, pl.BlockSpec((count, width), lambda j: (0, j))],
        out_specs=[
            pl.BlockSpec((hot_rows, width), lambda j: (0, j)),
            pl.BlockSpec((cold_rows, depth + TAG), lambda j: (0, 0)),
        ],
        out_shape=[
            jax.ShapeDtypeStruct((hot_rows, depth), jnp.bfloat16),
            jax.ShapeDtypeStruct((cold_rows, depth + TAG), jnp.bfloat16),
        ],
        scratch_shapes=[pltpu.VMEM((hot_rows, count), jnp.bfloat16), pltpu.VMEM((cold_rows, count), jnp.bfloat16)],
        **kernel_params(),
    )(hot_target[None], cold_target[None], tag[None], rows)


def base_halves(rows, weight):
    count, depth = rows.shape
    width = weight.shape[1]
    half = width // 2
    blocks = 8
    part = depth // blocks

    def kernel(tp_at, rows_ref, weight_ref, own_ref, other_ref, total):
        step = pl.program_id(0)
        product = matmul(rows_ref[...], weight_ref[...])

        @pl.when(step == 0)
        def _():
            total[...] = product

        @pl.when(step > 0)
        def _():
            total[...] += product

        @pl.when(step == blocks - 1)
        def _():
            first = pl.multiple_of(tp_at[0] * half, 128)
            second = pl.multiple_of((1 - tp_at[0]) * half, 128)
            own_ref[...] = total[:, pl.ds(first, half)]
            other_ref[...] = total[:, pl.ds(second, half)]

    out = pl.BlockSpec((count, half), lambda k, at: (0, 0))
    return pl.pallas_call(
        kernel,
        grid_spec=pltpu.PrefetchScalarGridSpec(
            num_scalar_prefetch=1,
            grid=(blocks,),
            in_specs=[
                pl.BlockSpec((count, part), lambda k, at: (0, k)),
                pl.BlockSpec((part, width), lambda k, at: (k, 0)),
            ],
            out_specs=[out, out],
            scratch_shapes=[pltpu.VMEM((count, width), jnp.float32)],
        ),
        out_shape=[jax.ShapeDtypeStruct((count, half), jnp.float32)] * 2,
        **kernel_params(),
    )(lax.axis_index("tp").astype(jnp.int32)[None], rows, weight)


def hot_expand(z_own, z_got, factors, head):
    kept = factors[0].shape[1]
    near = kept // R
    count = z_own.shape[0] // HCAP

    def kernel(own_ref, got_ref, first_ref, second_ref, out_ref):
        z = (own_ref[...] + got_ref[...]).astype(jnp.bfloat16).astype(jnp.float32).reshape(count, 1, HCAP, kept)
        shape = (count, near, HCAP, kept)
        same = lax.broadcasted_iota(jnp.int32, shape, 3) // R == lax.broadcasted_iota(jnp.int32, shape, 1)
        spread = jnp.where(same, jnp.broadcast_to(z, shape), 0.0).astype(jnp.bfloat16)
        product = lax.dot_general(
            spread.reshape(count * near * HCAP, kept),
            first_ref[-head:] + second_ref[-head:],
            (((1,), (1,)), ((), ())),
            preferred_element_type=jnp.float32,
        )
        out_ref[...] = product.astype(jnp.bfloat16)

    return pl.pallas_call(
        kernel,
        out_shape=jax.ShapeDtypeStruct((count * near * HCAP, head), jnp.bfloat16),
        **kernel_params(),
    )(z_own, z_got, *factors)


def add_hot(partial, target, delta):
    count = partial.shape[0]
    hot_rows = delta.shape[0]

    def kernel(partial_ref, target_ref, delta_ref, out_ref):
        hit = lax.broadcasted_iota(jnp.int32, (count, hot_rows), 1) == target_ref[...]
        place = hit.astype(jnp.float32).astype(jnp.bfloat16)
        out_ref[...] = (partial_ref[...] + matmul(place, delta_ref[...])).astype(jnp.bfloat16)

    return pl.pallas_call(
        kernel,
        out_shape=jax.ShapeDtypeStruct(partial.shape, jnp.bfloat16),
        **kernel_params(),
    )(partial, target[:, None], delta)


def on_device(
    activations, value_weight, shrink_store, expand_store, adapter_row, token_adapter, hot_ids
):
    step_count, token_count, depth = activations.shape
    adapter_count = adapter_row.shape[0]
    hot_count = hot_ids.shape[1]
    per_dev = expand_store.shape[0] // R
    head_part = expand_store.shape[1]
    far_count = lax.axis_size("z_high")
    group_count = 8
    dp_count = far_count * group_count
    me = lax.axis_index(DP)
    z_at, x_at, core_at = lax.axis_index("z_low"), lax.axis_index("x"), lax.axis_index("core")
    none_code = adapter_count + hot_count
    rows = activations.reshape(step_count * token_count, depth)

    near = step_count // 2
    names = jnp.arange(adapter_count, dtype=jnp.int32)
    chain = Chain()

    cold_row = jnp.sum(jnp.where((token_adapter - hot_count)[:, :, None] == names, adapter_row, 0), axis=-1)
    is_hot = token_adapter < hot_count
    is_cold = (token_adapter < none_code) & jnp.logical_not(is_hot)
    owner = cold_row // per_dev
    group = jnp.where(is_hot, token_adapter, jnp.where(is_cold, hot_count + owner, -1))
    at = jnp.arange(token_count, dtype=jnp.int32)
    before = (group[:, :, None] == group[:, None, :]) & (at[None, :] < at[:, None])
    rank = jnp.sum(before.astype(jnp.int32), axis=-1)
    step_at = jnp.arange(step_count, dtype=jnp.int32)[:, None]
    hot_rows = hot_count * step_count * HCAP
    cold_rows = dp_count * step_count * CAP
    server = (step_at // near) * hot_count + token_adapter
    hot_target = (server * near + step_at % near) * HCAP + rank
    cold_target = (owner * step_count + step_at) * CAP + rank
    hot_target = jnp.where(is_hot, hot_target, -1).reshape(-1)
    cold_target = jnp.where(is_cold, cold_target, -1).reshape(-1)

    hot_out, packet = place_rows(
        rows, hot_target, cold_target, (cold_row % per_dev + 1).reshape(-1), hot_rows, cold_rows
    )
    hot_out = chain.hold(hot_out.reshape(group_count, near * HCAP, depth))
    done = {"hot_in": lax.all_to_all(hot_out, GROUP, split_axis=0, concat_axis=0, tiled=True)}

    hot_row = jnp.sum(jnp.where(hot_ids[:, :, None] == names, adapter_row, 0), axis=-1)
    hot_first = jnp.where(hot_row // per_dev == me, (hot_row % per_dev) * R, -R * per_dev)
    column = jnp.arange(per_dev * R, dtype=jnp.int32)
    lane = jnp.arange(R, dtype=jnp.int32)
    entry = jnp.arange(hot_count, dtype=jnp.int32)

    def wanted(core):
        firsts = []
        for x in (x_at, 1 - x_at):
            of_steps = jnp.sum(jnp.where(entry == 2 * x + core, hot_first, 0), axis=1)
            firsts += [jnp.where(z_at == 0, of_steps[:near], of_steps[near:])]
            firsts += [jnp.where(z_at == 0, of_steps[near:], of_steps[:near])]
        return jnp.stack([(f[:, None] + lane).reshape(-1) for f in firsts])

    want_mine, want_other = wanted(core_at), wanted(1 - core_at)
    kept = near * R
    chunk_count = 3
    part = (depth + head_part) // chunk_count

    hops = [("x", SWAP), ("z_low", SWAP)]
    bit = 1
    while bit < far_count:
        hops.append(("z_high", [(i, i ^ bit) for i in range(far_count)]))
        bit *= 2
    mine, swapped, got, held = {}, {}, {}, {}

    def operand(c, stage):
        if stage == 0:
            return mine[c][:, 2 * kept:] + swapped[c][:, 2 * kept:]
        if stage == 1:
            return mine[c][:, kept:2 * kept] + swapped[c][:, kept:2 * kept] + got[c, 0][:, kept:]
        if stage == 2:
            held[c] = mine[c][:, :kept] + swapped[c][:, :kept] + got[c, 0][:, :kept] + got[c, 1]
        else:
            held[c] = held[c] + got[c, stage - 1]
        return held[c]

    def send(c, stage):
        got[c, stage] = chain.permute(operand(c, stage), *hops[stage])

    def view(c):
        mine[c] = after(mine_all, chain.last)[c * part:(c + 1) * part]
        swapped[c] = after(rest_swapped, chain.last)[(c - 1) * part:c * part]

    mine_all, other_first, other_rest = pick_columns(
        after(shrink_store, chain.last), expand_store, want_mine, want_other
    )
    mine[0], swapped[0] = mine_all[:part], chain.permute(other_first, "core", SWAP)
    rest_swapped = chain.permute(other_rest, "core", SWAP)
    send(0, 0)

    def cold_tokens_out():
        sent = chain.hold(packet.reshape(dp_count, step_count * CAP, depth + TAG))
        sent = lax.all_to_all(sent, DP, split_axis=0, concat_axis=0, tiled=True)
        done["packet"] = sent.reshape(cold_rows, depth + TAG)

    def base_product():
        weight = after(value_weight, chain.last)
        if lax.axis_size("tp") == 2:
            done["base_own"], done["base_other"] = base_halves(rows, weight)
        else:
            done["base_own"], done["base_other"] = jnp.zeros((1, 1), jnp.float32), matmul(rows, weight)

    def base_over_tp():
        if lax.axis_size("tp") == 2:
            done["base_got"] = chain.permute(done["base_other"], "tp", SWAP)
        else:
            whole = chain.hold(done["base_other"])
            done["base_got"] = lax.psum_scatter(whole, "tp", scatter_dimension=1, tiled=True)

    def cold_shrink():
        tag_in = done["packet"][:, depth:depth + 1].astype(jnp.int32)
        chosen = (column // R + 1)[None, :] == tag_in
        product = matmul(done["packet"][:, :depth], after(shrink_store, chain.last))
        done["z_part"] = jnp.where(chosen, product, 0.0)

    def cold_over_tp():
        z_part = chain.hold(done["z_part"])
        if lax.axis_size("tp") == 2:
            done["z_got"] = lax.ppermute(z_part, "tp", SWAP)
        else:
            done["z_part"], done["z_got"] = jnp.zeros_like(z_part), lax.psum(z_part, "tp")

    def cold_expand():
        z_cold = (done["z_part"] + done["z_got"]).astype(jnp.bfloat16)
        done["delta"] = narrow(z_cold, after(expand_store, chain.last))

    def cold_back():
        delta = chain.hold(done["delta"].reshape(dp_count, step_count * CAP, head_part))
        delta = lax.all_to_all(delta, DP, split_axis=0, concat_axis=0, tiled=True)
        done["delta_cold"] = delta.reshape(cold_rows, head_part)

    def all_but_hot():
        place_cold = pick(jnp.arange(cold_rows, dtype=jnp.int32)[:, None] == cold_target)
        partial = lax.dot_general(
            place_cold, done["delta_cold"], (((0,), (0,)), ((), ())), preferred_element_type=jnp.float32
        )
        done["partial"] = partial + done["base_own"] + done["base_got"]

    cold_tokens_out()
    chain.last, got[0, 0], done["hot_in"] = lax.optimization_barrier((chain.last, got[0, 0], done["hot_in"]))
    view(1)
    send(1, 0)
    send(0, 1)
    view(2)
    send(2, 0)
    if far_count == 2:
        send(0, 2)
        base_product()
        names_here = ["packet", "base_own", "base_other"]
        arrived = lax.optimization_barrier((chain.last, got[1, 0], *[done[name] for name in names_here]))
        chain.last, got[1, 0] = arrived[:2]
        done.update(zip(names_here, arrived[2:]))
        send(1, 1)
        chain.wait(got[0, 2])
        cold_shrink()
        cold_over_tp()
        base_over_tp()
        send(1, 2)
        got[2, 0] = after(got[2, 0], chain.last)
        send(2, 1)
        chain.last, _, done["z_got"] = lax.optimization_barrier((chain.last, got[1, 2], done["z_got"]))
        cold_expand()
        send(2, 2)
        cold_back()
    else:
        base_product()
        for c in range(chunk_count):
            for stage in range(1, len(hops)):
                if (c, stage) != (0, 1):
                    send(c, stage)
        base_over_tp()
        cold_shrink()
        cold_over_tp()
        cold_expand()
        cold_back()
    all_but_hot()
    partial = done["partial"]

    hot_in = done["hot_in"].reshape(hot_rows, depth)
    dense = None
    for c in range(chunk_count):
        last = min((c + 1) * part, depth)
        for piece in (held[c], got[c, len(hops) - 1]):
            product = matmul(hot_in[:, c * part:last], piece[:last - c * part])
            dense = product if dense is None else dense + product
    dense = dense.reshape(group_count, near, HCAP, kept)
    at_step = jnp.arange(kept) // R
    z_part = sum(jnp.where(at_step == i, dense[:, i], 0.0) for i in range(near)).reshape(group_count * HCAP, kept)
    if lax.axis_size("tp") == 2:
        z_got = lax.ppermute(z_part, "tp", SWAP)
    else:
        z_part = lax.psum(z_part, "tp")
        z_got = jnp.zeros_like(z_part)
    delta_hot = hot_expand(z_part, z_got, (held[c], got[c, len(hops) - 1]), head_part).reshape(group_count, near * HCAP, head_part)
    delta_hot = lax.all_to_all(delta_hot, GROUP, split_axis=0, concat_axis=0, tiled=True)
    added = add_hot(partial, hot_target, delta_hot.reshape(hot_rows, head_part))
    return added.reshape(step_count, token_count, head_part)


def solution(mesh):
    tp_count, dp_count = mesh.shape["tp"], mesh.shape["dp"]
    fine = Mesh(mesh.devices.reshape(tp_count, dp_count // 8, 2, 2, 2), ("tp", *DP))
    placed = (
        P(None, DP, "tp"),
        P("tp", None),
        P("tp", DP),
        P(DP, "tp"),
        P(),
        P(None, DP),
        P(),
    )
    return jax.shard_map(
        on_device, mesh=fine, in_specs=placed, out_specs=P(None, DP, "tp"), check_vma=False
    )
```

```python
import jax
import jax.numpy as jnp
from jax import lax
from jax.experimental import pallas as pl
from jax.experimental.pallas import tpu as pltpu
from jax.sharding import Mesh, PartitionSpec as P

R = 64
CAP = 2
HCAP = 16
TAG = 128
DP = ("z_high", "z_low", "x", "core")
GROUP = ("z_low", "x", "core")
SWAP = [(0, 1), (1, 0)]


def pick(flags):
    return flags.astype(jnp.bfloat16)


def matmul(a, b):
    return jnp.dot(a, b, preferred_element_type=jnp.float32)


def narrow(a, b):
    return matmul(a, b).astype(jnp.bfloat16)


def after(value, *others):
    return lax.optimization_barrier((value, *others))[0]


class Chain:
    def __init__(self):
        self.last = None

    def hold(self, value):
        self.last = value if self.last is None else after(value, self.last)
        return self.last

    def permute(self, value, axis, pairs):
        return lax.ppermute(self.hold(value), axis, pairs)

    def wait(self, *arrived):
        self.last = after(self.last, *arrived)


def kernel_params():
    return dict(
        compiler_params=pltpu.CompilerParams(vmem_limit_bytes=40 * 2**20),
        cost_estimate=pl.CostEstimate(flops=1, bytes_accessed=1, transcendentals=0),
    )


def pick_columns(store, expand, want_mine, want_other):
    depth, width = store.shape
    groups, lanes = want_mine.shape
    count = groups * lanes
    blocks = 8
    rows = depth // blocks

    def kernel(mine_held, other_held, mine_at, other_at, store_ref, expand_ref, mine_ref, first_ref, rest_ref, pick_mine, pick_other):
        step = pl.program_id(0)

        @pl.when(step == 0)
        def _():
            column = lax.broadcasted_iota(jnp.int32, (width, count), 0)
            pick_mine[...] = (column == mine_at[...]).astype(jnp.float32).astype(jnp.bfloat16)
            pick_other[...] = (column == other_at[...]).astype(jnp.float32).astype(jnp.bfloat16)

        def fill(out_ref, held, picker):
            for g in range(groups):
                at = slice(g * lanes, (g + 1) * lanes)

                @pl.when((held[g] > 0) & (step < blocks))
                def _():
                    out_ref[:, at] = narrow(store_ref[...], picker[:, at])

                @pl.when((held[g] > 0) & (step == blocks))
                def _():
                    product = lax.dot_general(
                        expand_ref[...], picker[:, at], (((0,), (0,)), ((), ())), preferred_element_type=jnp.float32
                    )
                    out_ref[:, at] = product.astype(jnp.bfloat16)

                @pl.when(held[g] == 0)
                def _():
                    out_ref[:, at] = jnp.zeros((rows, lanes), jnp.bfloat16)

        fill(mine_ref, mine_held, pick_mine)

        @pl.when(step < 3)
        def _():
            fill(first_ref, other_held, pick_other)

        @pl.when(step >= 3)
        def _():
            fill(rest_ref, other_held, pick_other)

    out = lambda thirds: jax.ShapeDtypeStruct((3 * rows * thirds, count), jnp.bfloat16)
    index = pl.BlockSpec((1, count), lambda i, *held: (0, 0))
    return pl.pallas_call(
        kernel,
        grid_spec=pltpu.PrefetchScalarGridSpec(
            num_scalar_prefetch=2,
            grid=(blocks + 1,),
            in_specs=[
                index,
                index,
                pl.BlockSpec((rows, width), lambda i, *held: (jnp.minimum(i, blocks - 1), 0)),
                pl.BlockSpec(expand.shape, lambda i, *held: (0, 0)),
            ],
            out_specs=[
                pl.BlockSpec((rows, count), lambda i, *held: (i, 0)),
                pl.BlockSpec((rows, count), lambda i, *held: (jnp.minimum(i, 2), 0)),
                pl.BlockSpec((rows, count), lambda i, *held: (jnp.maximum(i - 3, 0), 0)),
            ],
            scratch_shapes=[pltpu.VMEM((width, count), jnp.bfloat16)] * 2,
        ),
        out_shape=[out(3), out(1), out(2)],
        **kernel_params(),
    )(
        jnp.any(want_mine >= 0, axis=1).astype(jnp.int32),
        jnp.any(want_other >= 0, axis=1).astype(jnp.int32),
        want_mine.reshape(1, -1),
        want_other.reshape(1, -1),
        store,
        expand,
    )


def place_rows(rows, hot_target, cold_target, tag, hot_rows, cold_rows):
    count, depth = rows.shape
    blocks = 4
    width = depth // blocks

    def kernel(hot_at, cold_at, tag_at, rows_ref, hot_ref, cold_ref, place_hot, place_cold):
        step = pl.program_id(0)

        @pl.when(step == 0)
        def _():
            hot_hit = lax.broadcasted_iota(jnp.int32, (hot_rows, count), 0) == hot_at[...]
            cold_hit = lax.broadcasted_iota(jnp.int32, (cold_rows, count), 0) == cold_at[...]
            place_hot[...] = hot_hit.astype(jnp.float32).astype(jnp.bfloat16)
            place_cold[...] = cold_hit.astype(jnp.float32).astype(jnp.bfloat16)
            tags = jnp.sum(jnp.where(cold_hit, tag_at[...].astype(jnp.float32), 0.0), axis=1, keepdims=True)
            cold_ref[:, depth:] = jnp.broadcast_to(tags, (cold_rows, TAG)).astype(jnp.bfloat16)

        block = rows_ref[...]
        hot_ref[...] = narrow(place_hot[...], block)
        cold_ref[:, pl.ds(pl.multiple_of(step * width, 128), width)] = narrow(place_cold[...], block)

    index = pl.BlockSpec((1, count), lambda j: (0, 0))
    return pl.pallas_call(
        kernel,
        grid=(blocks,),
        in_specs=[index, index, index, pl.BlockSpec((count, width), lambda j: (0, j))],
        out_specs=[
            pl.BlockSpec((hot_rows, width), lambda j: (0, j)),
            pl.BlockSpec((cold_rows, depth + TAG), lambda j: (0, 0)),
        ],
        out_shape=[
            jax.ShapeDtypeStruct((hot_rows, depth), jnp.bfloat16),
            jax.ShapeDtypeStruct((cold_rows, depth + TAG), jnp.bfloat16),
        ],
        scratch_shapes=[pltpu.VMEM((hot_rows, count), jnp.bfloat16), pltpu.VMEM((cold_rows, count), jnp.bfloat16)],
        **kernel_params(),
    )(hot_target[None], cold_target[None], tag[None], rows)


def base_halves(rows, weight):
    count, depth = rows.shape
    width = weight.shape[1]
    half = width // 2
    blocks = 8
    part = depth // blocks

    def kernel(tp_at, rows_ref, weight_ref, own_ref, other_ref, total):
        step = pl.program_id(0)
        product = matmul(rows_ref[...], weight_ref[...])

        @pl.when(step == 0)
        def _():
            total[...] = product

        @pl.when(step > 0)
        def _():
            total[...] += product

        @pl.when(step == blocks - 1)
        def _():
            first = pl.multiple_of(tp_at[0] * half, 128)
            second = pl.multiple_of((1 - tp_at[0]) * half, 128)
            own_ref[...] = total[:, pl.ds(first, half)]
            other_ref[...] = total[:, pl.ds(second, half)]

    out = pl.BlockSpec((count, half), lambda k, at: (0, 0))
    return pl.pallas_call(
        kernel,
        grid_spec=pltpu.PrefetchScalarGridSpec(
            num_scalar_prefetch=1,
            grid=(blocks,),
            in_specs=[
                pl.BlockSpec((count, part), lambda k, at: (0, k)),
                pl.BlockSpec((part, width), lambda k, at: (k, 0)),
            ],
            out_specs=[out, out],
            scratch_shapes=[pltpu.VMEM((count, width), jnp.float32)],
        ),
        out_shape=[jax.ShapeDtypeStruct((count, half), jnp.float32)] * 2,
        **kernel_params(),
    )(lax.axis_index("tp").astype(jnp.int32)[None], rows, weight)


def hot_expand(z_own, z_got, factors, head):
    kept = factors[0].shape[1]
    near = kept // R
    count = z_own.shape[0] // HCAP

    def kernel(own_ref, got_ref, first_ref, second_ref, out_ref):
        z = (own_ref[...] + got_ref[...]).astype(jnp.bfloat16).astype(jnp.float32).reshape(count, 1, HCAP, kept)
        shape = (count, near, HCAP, kept)
        same = lax.broadcasted_iota(jnp.int32, shape, 3) // R == lax.broadcasted_iota(jnp.int32, shape, 1)
        spread = jnp.where(same, jnp.broadcast_to(z, shape), 0.0).astype(jnp.bfloat16)
        product = lax.dot_general(
            spread.reshape(count * near * HCAP, kept),
            first_ref[-head:] + second_ref[-head:],
            (((1,), (1,)), ((), ())),
            preferred_element_type=jnp.float32,
        )
        out_ref[...] = product.astype(jnp.bfloat16)

    return pl.pallas_call(
        kernel,
        out_shape=jax.ShapeDtypeStruct((count * near * HCAP, head), jnp.bfloat16),
        **kernel_params(),
    )(z_own, z_got, *factors)


def add_hot(partial, target, delta):
    count = partial.shape[0]
    hot_rows = delta.shape[0]

    def kernel(partial_ref, target_ref, delta_ref, out_ref):
        hit = lax.broadcasted_iota(jnp.int32, (count, hot_rows), 1) == target_ref[...]
        place = hit.astype(jnp.float32).astype(jnp.bfloat16)
        out_ref[...] = (partial_ref[...] + matmul(place, delta_ref[...])).astype(jnp.bfloat16)

    return pl.pallas_call(
        kernel,
        out_shape=jax.ShapeDtypeStruct(partial.shape, jnp.bfloat16),
        **kernel_params(),
    )(partial, target[:, None], delta)


def on_device(
    activations, value_weight, shrink_store, expand_store, adapter_row, token_adapter, hot_ids
):
    step_count, token_count, depth = activations.shape
    adapter_count = adapter_row.shape[0]
    hot_count = hot_ids.shape[1]
    per_dev = expand_store.shape[0] // R
    head_part = expand_store.shape[1]
    far_count = lax.axis_size("z_high")
    group_count = 8
    dp_count = far_count * group_count
    me = lax.axis_index(DP)
    z_at, x_at, core_at = lax.axis_index("z_low"), lax.axis_index("x"), lax.axis_index("core")
    none_code = adapter_count + hot_count
    rows = activations.reshape(step_count * token_count, depth)

    near = step_count // 2
    names = jnp.arange(adapter_count, dtype=jnp.int32)
    chain = Chain()

    cold_row = jnp.sum(jnp.where((token_adapter - hot_count)[:, :, None] == names, adapter_row, 0), axis=-1)
    is_hot = token_adapter < hot_count
    is_cold = (token_adapter < none_code) & jnp.logical_not(is_hot)
    owner = cold_row // per_dev
    group = jnp.where(is_hot, token_adapter, jnp.where(is_cold, hot_count + owner, -1))
    at = jnp.arange(token_count, dtype=jnp.int32)
    before = (group[:, :, None] == group[:, None, :]) & (at[None, :] < at[:, None])
    rank = jnp.sum(before.astype(jnp.int32), axis=-1)
    step_at = jnp.arange(step_count, dtype=jnp.int32)[:, None]
    hot_rows = hot_count * step_count * HCAP
    cold_rows = dp_count * step_count * CAP
    server = (step_at // near) * hot_count + token_adapter
    hot_target = (server * near + step_at % near) * HCAP + rank
    cold_target = (owner * step_count + step_at) * CAP + rank
    hot_target = jnp.where(is_hot, hot_target, -1).reshape(-1)
    cold_target = jnp.where(is_cold, cold_target, -1).reshape(-1)

    hot_out, packet = place_rows(
        rows, hot_target, cold_target, (cold_row % per_dev + 1).reshape(-1), hot_rows, cold_rows
    )
    hot_out = chain.hold(hot_out.reshape(group_count, near * HCAP, depth))
    done = {"hot_in": lax.all_to_all(hot_out, GROUP, split_axis=0, concat_axis=0, tiled=True)}

    hot_row = jnp.sum(jnp.where(hot_ids[:, :, None] == names, adapter_row, 0), axis=-1)
    hot_first = jnp.where(hot_row // per_dev == me, (hot_row % per_dev) * R, -R * per_dev)
    column = jnp.arange(per_dev * R, dtype=jnp.int32)
    lane = jnp.arange(R, dtype=jnp.int32)
    entry = jnp.arange(hot_count, dtype=jnp.int32)

    def wanted(core):
        firsts = []
        for x in (x_at, 1 - x_at):
            of_steps = jnp.sum(jnp.where(entry == 2 * x + core, hot_first, 0), axis=1)
            firsts += [jnp.where(z_at == 0, of_steps[:near], of_steps[near:])]
            firsts += [jnp.where(z_at == 0, of_steps[near:], of_steps[:near])]
        return jnp.stack([(f[:, None] + lane).reshape(-1) for f in firsts])

    want_mine, want_other = wanted(core_at), wanted(1 - core_at)
    kept = near * R
    chunk_count = 3
    part = (depth + head_part) // chunk_count

    hops = [("x", SWAP), ("z_low", SWAP)]
    bit = 1
    while bit < far_count:
        hops.append(("z_high", [(i, i ^ bit) for i in range(far_count)]))
        bit *= 2
    mine, swapped, got, held = {}, {}, {}, {}

    def operand(c, stage):
        if stage == 0:
            return mine[c][:, 2 * kept:] + swapped[c][:, 2 * kept:]
        if stage == 1:
            return mine[c][:, kept:2 * kept] + swapped[c][:, kept:2 * kept] + got[c, 0][:, kept:]
        if stage == 2:
            held[c] = mine[c][:, :kept] + swapped[c][:, :kept] + got[c, 0][:, :kept] + got[c, 1]
        else:
            held[c] = held[c] + got[c, stage - 1]
        return held[c]

    def send(c, stage):
        got[c, stage] = chain.permute(operand(c, stage), *hops[stage])

    def view(c):
        mine[c] = after(mine_all, chain.last)[c * part:(c + 1) * part]
        swapped[c] = after(rest_swapped, chain.last)[(c - 1) * part:c * part]

    mine_all, other_first, other_rest = pick_columns(
        after(shrink_store, chain.last), expand_store, want_mine, want_other
    )
    mine[0], swapped[0] = mine_all[:part], chain.permute(other_first, "core", SWAP)
    rest_swapped = chain.permute(other_rest, "core", SWAP)
    send(0, 0)

    def cold_tokens_out():
        sent = chain.hold(packet.reshape(dp_count, step_count * CAP, depth + TAG))
        sent = lax.all_to_all(sent, DP, split_axis=0, concat_axis=0, tiled=True)
        done["packet"] = sent.reshape(cold_rows, depth + TAG)

    def base_product():
        weight = after(value_weight, chain.last)
        if lax.axis_size("tp") == 2:
            done["base_own"], done["base_other"] = base_halves(rows, weight)
        else:
            done["base_own"], done["base_other"] = jnp.zeros((1, 1), jnp.float32), matmul(rows, weight)

    def base_over_tp():
        if lax.axis_size("tp") == 2:
            done["base_got"] = chain.permute(done["base_other"], "tp", SWAP)
        else:
            whole = chain.hold(done["base_other"])
            done["base_got"] = lax.psum_scatter(whole, "tp", scatter_dimension=1, tiled=True)

    def cold_shrink():
        tag_in = done["packet"][:, depth:depth + 1].astype(jnp.int32)
        chosen = (column // R + 1)[None, :] == tag_in
        product = matmul(done["packet"][:, :depth], after(shrink_store, chain.last))
        done["z_part"] = jnp.where(chosen, product, 0.0)

    def cold_over_tp():
        z_part = chain.hold(done["z_part"])
        if lax.axis_size("tp") == 2:
            done["z_got"] = lax.ppermute(z_part, "tp", SWAP)
        else:
            done["z_part"], done["z_got"] = jnp.zeros_like(z_part), lax.psum(z_part, "tp")

    def cold_expand():
        z_cold = (done["z_part"] + done["z_got"]).astype(jnp.bfloat16)
        done["delta"] = narrow(z_cold, after(expand_store, chain.last))

    def cold_back():
        delta = chain.hold(done["delta"].reshape(dp_count, step_count * CAP, head_part))
        delta = lax.all_to_all(delta, DP, split_axis=0, concat_axis=0, tiled=True)
        done["delta_cold"] = delta.reshape(cold_rows, head_part)

    def all_but_hot():
        place_cold = pick(jnp.arange(cold_rows, dtype=jnp.int32)[:, None] == cold_target)
        partial = lax.dot_general(
            place_cold, done["delta_cold"], (((0,), (0,)), ((), ())), preferred_element_type=jnp.float32
        )
        done["partial"] = partial + done["base_own"] + done["base_got"]

    cold_tokens_out()
    chain.last, got[0, 0], done["hot_in"] = lax.optimization_barrier((chain.last, got[0, 0], done["hot_in"]))
    view(1)
    send(1, 0)
    send(0, 1)
    view(2)
    send(2, 0)
    if far_count == 2:
        send(0, 2)
        chain.last, got[1, 0], done["packet"] = lax.optimization_barrier((chain.last, got[1, 0], done["packet"]))
        send(1, 1)
        chain.wait(got[0, 2])
        cold_shrink()
        cold_over_tp()
        send(1, 2)
        got[2, 0] = after(got[2, 0], chain.last)
        send(2, 1)
        base_product()
        names_here = ["z_got", "base_own", "base_other"]
        arrived = lax.optimization_barrier((chain.last, got[1, 2], *[done[name] for name in names_here]))
        chain.last = arrived[0]
        done.update(zip(names_here, arrived[2:]))
        cold_expand()
        send(2, 2)
        base_over_tp()
        cold_back()
    else:
        base_product()
        for c in range(chunk_count):
            for stage in range(1, len(hops)):
                if (c, stage) != (0, 1):
                    send(c, stage)
        base_over_tp()
        cold_shrink()
        cold_over_tp()
        cold_expand()
        cold_back()
    all_but_hot()
    partial = done["partial"]

    hot_in = done["hot_in"].reshape(hot_rows, depth)
    dense = None
    for c in range(chunk_count):
        last = min((c + 1) * part, depth)
        for piece in (held[c], got[c, len(hops) - 1]):
            product = matmul(hot_in[:, c * part:last], piece[:last - c * part])
            dense = product if dense is None else dense + product
    dense = dense.reshape(group_count, near, HCAP, kept)
    at_step = jnp.arange(kept) // R
    z_part = sum(jnp.where(at_step == i, dense[:, i], 0.0) for i in range(near)).reshape(group_count * HCAP, kept)
    if lax.axis_size("tp") == 2:
        z_got = lax.ppermute(z_part, "tp", SWAP)
    else:
        z_part = lax.psum(z_part, "tp")
        z_got = jnp.zeros_like(z_part)
    delta_hot = hot_expand(z_part, z_got, (held[c], got[c, len(hops) - 1]), head_part).reshape(group_count, near * HCAP, head_part)
    delta_hot = lax.all_to_all(delta_hot, GROUP, split_axis=0, concat_axis=0, tiled=True)
    added = add_hot(partial, hot_target, delta_hot.reshape(hot_rows, head_part))
    return added.reshape(step_count, token_count, head_part)


def solution(mesh):
    tp_count, dp_count = mesh.shape["tp"], mesh.shape["dp"]
    fine = Mesh(mesh.devices.reshape(tp_count, dp_count // 8, 2, 2, 2), ("tp", *DP))
    placed = (
        P(None, DP, "tp"),
        P("tp", None),
        P("tp", DP),
        P(DP, "tp"),
        P(),
        P(None, DP),
        P(),
    )
    return jax.shard_map(
        on_device, mesh=fine, in_specs=placed, out_specs=P(None, DP, "tp"), check_vma=False
    )
```

```python
import jax
import jax.numpy as jnp
from jax import lax
from jax.experimental import pallas as pl
from jax.experimental.pallas import tpu as pltpu
from jax.sharding import Mesh, PartitionSpec as P

R = 64
CAP = 2
HCAP = 16
TAG = 128
DP = ("z_high", "z_low", "x", "core")
GROUP = ("z_low", "x", "core")
SWAP = [(0, 1), (1, 0)]


def pick(flags):
    return flags.astype(jnp.bfloat16)


def matmul(a, b):
    return jnp.dot(a, b, preferred_element_type=jnp.float32)


def narrow(a, b):
    return matmul(a, b).astype(jnp.bfloat16)


def after(value, *others):
    return lax.optimization_barrier((value, *others))[0]


class Chain:
    def __init__(self):
        self.last = None

    def hold(self, value):
        self.last = value if self.last is None else after(value, self.last)
        return self.last

    def permute(self, value, axis, pairs):
        return lax.ppermute(self.hold(value), axis, pairs)

    def wait(self, *arrived):
        self.last = after(self.last, *arrived)


def kernel_params():
    return dict(
        compiler_params=pltpu.CompilerParams(vmem_limit_bytes=40 * 2**20),
        cost_estimate=pl.CostEstimate(flops=1, bytes_accessed=1, transcendentals=0),
    )


def pick_columns(store, expand, want_mine, want_other):
    depth, width = store.shape
    groups, lanes = want_mine.shape
    count = groups * lanes
    blocks = 8
    rows = depth // blocks

    def kernel(mine_held, other_held, mine_at, other_at, store_ref, expand_ref, mine_ref, first_ref, rest_ref, pick_mine, pick_other):
        step = pl.program_id(0)

        @pl.when(step == 0)
        def _():
            column = lax.broadcasted_iota(jnp.int32, (width, count), 0)
            pick_mine[...] = (column == mine_at[...]).astype(jnp.float32).astype(jnp.bfloat16)
            pick_other[...] = (column == other_at[...]).astype(jnp.float32).astype(jnp.bfloat16)

        def fill(out_ref, held, picker):
            for g in range(groups):
                at = slice(g * lanes, (g + 1) * lanes)

                @pl.when((held[g] > 0) & (step < blocks))
                def _():
                    out_ref[:, at] = narrow(store_ref[...], picker[:, at])

                @pl.when((held[g] > 0) & (step == blocks))
                def _():
                    product = lax.dot_general(
                        expand_ref[...], picker[:, at], (((0,), (0,)), ((), ())), preferred_element_type=jnp.float32
                    )
                    out_ref[:, at] = product.astype(jnp.bfloat16)

                @pl.when(held[g] == 0)
                def _():
                    out_ref[:, at] = jnp.zeros((rows, lanes), jnp.bfloat16)

        fill(mine_ref, mine_held, pick_mine)

        @pl.when(step < 3)
        def _():
            fill(first_ref, other_held, pick_other)

        @pl.when(step >= 3)
        def _():
            fill(rest_ref, other_held, pick_other)

    out = lambda thirds: jax.ShapeDtypeStruct((3 * rows * thirds, count), jnp.bfloat16)
    index = pl.BlockSpec((1, count), lambda i, *held: (0, 0))
    return pl.pallas_call(
        kernel,
        grid_spec=pltpu.PrefetchScalarGridSpec(
            num_scalar_prefetch=2,
            grid=(blocks + 1,),
            in_specs=[
                index,
                index,
                pl.BlockSpec((rows, width), lambda i, *held: (jnp.minimum(i, blocks - 1), 0)),
                pl.BlockSpec(expand.shape, lambda i, *held: (0, 0)),
            ],
            out_specs=[
                pl.BlockSpec((rows, count), lambda i, *held: (i, 0)),
                pl.BlockSpec((rows, count), lambda i, *held: (jnp.minimum(i, 2), 0)),
                pl.BlockSpec((rows, count), lambda i, *held: (jnp.maximum(i - 3, 0), 0)),
            ],
            scratch_shapes=[pltpu.VMEM((width, count), jnp.bfloat16)] * 2,
        ),
        out_shape=[out(3), out(1), out(2)],
        **kernel_params(),
    )(
        jnp.any(want_mine >= 0, axis=1).astype(jnp.int32),
        jnp.any(want_other >= 0, axis=1).astype(jnp.int32),
        want_mine.reshape(1, -1),
        want_other.reshape(1, -1),
        store,
        expand,
    )


def place_rows(rows, hot_target, cold_target, tag, hot_rows, cold_rows):
    count, depth = rows.shape
    blocks = 4
    width = depth // blocks

    def kernel(hot_at, cold_at, tag_at, rows_ref, hot_ref, cold_ref, place_hot, place_cold):
        step = pl.program_id(0)

        @pl.when(step == 0)
        def _():
            hot_hit = lax.broadcasted_iota(jnp.int32, (hot_rows, count), 0) == hot_at[...]
            cold_hit = lax.broadcasted_iota(jnp.int32, (cold_rows, count), 0) == cold_at[...]
            place_hot[...] = hot_hit.astype(jnp.float32).astype(jnp.bfloat16)
            place_cold[...] = cold_hit.astype(jnp.float32).astype(jnp.bfloat16)
            tags = jnp.sum(jnp.where(cold_hit, tag_at[...].astype(jnp.float32), 0.0), axis=1, keepdims=True)
            cold_ref[:, depth:] = jnp.broadcast_to(tags, (cold_rows, TAG)).astype(jnp.bfloat16)

        block = rows_ref[...]
        hot_ref[...] = narrow(place_hot[...], block)
        cold_ref[:, pl.ds(pl.multiple_of(step * width, 128), width)] = narrow(place_cold[...], block)

    index = pl.BlockSpec((1, count), lambda j: (0, 0))
    return pl.pallas_call(
        kernel,
        grid=(blocks,),
        in_specs=[index, index, index, pl.BlockSpec((count, width), lambda j: (0, j))],
        out_specs=[
            pl.BlockSpec((hot_rows, width), lambda j: (0, j)),
            pl.BlockSpec((cold_rows, depth + TAG), lambda j: (0, 0)),
        ],
        out_shape=[
            jax.ShapeDtypeStruct((hot_rows, depth), jnp.bfloat16),
            jax.ShapeDtypeStruct((cold_rows, depth + TAG), jnp.bfloat16),
        ],
        scratch_shapes=[pltpu.VMEM((hot_rows, count), jnp.bfloat16), pltpu.VMEM((cold_rows, count), jnp.bfloat16)],
        **kernel_params(),
    )(hot_target[None], cold_target[None], tag[None], rows)


def base_halves(rows, weight):
    count, depth = rows.shape
    width = weight.shape[1]
    half = width // 2
    blocks = 8
    part = depth // blocks

    def kernel(tp_at, rows_ref, weight_ref, own_ref, other_ref, total):
        step = pl.program_id(0)
        product = matmul(rows_ref[...], weight_ref[...])

        @pl.when(step == 0)
        def _():
            total[...] = product

        @pl.when(step > 0)
        def _():
            total[...] += product

        @pl.when(step == blocks - 1)
        def _():
            first = pl.multiple_of(tp_at[0] * half, 128)
            second = pl.multiple_of((1 - tp_at[0]) * half, 128)
            own_ref[...] = total[:, pl.ds(first, half)]
            other_ref[...] = total[:, pl.ds(second, half)]

    out = pl.BlockSpec((count, half), lambda k, at: (0, 0))
    return pl.pallas_call(
        kernel,
        grid_spec=pltpu.PrefetchScalarGridSpec(
            num_scalar_prefetch=1,
            grid=(blocks,),
            in_specs=[
                pl.BlockSpec((count, part), lambda k, at: (0, k)),
                pl.BlockSpec((part, width), lambda k, at: (k, 0)),
            ],
            out_specs=[out, out],
            scratch_shapes=[pltpu.VMEM((count, width), jnp.float32)],
        ),
        out_shape=[jax.ShapeDtypeStruct((count, half), jnp.float32)] * 2,
        **kernel_params(),
    )(lax.axis_index("tp").astype(jnp.int32)[None], rows, weight)


def hot_expand(z_own, z_got, factors, head):
    kept = factors[0].shape[1]
    near = kept // R
    count = z_own.shape[0] // HCAP

    def kernel(own_ref, got_ref, first_ref, second_ref, out_ref):
        z = (own_ref[...] + got_ref[...]).astype(jnp.bfloat16).astype(jnp.float32).reshape(count, 1, HCAP, kept)
        shape = (count, near, HCAP, kept)
        same = lax.broadcasted_iota(jnp.int32, shape, 3) // R == lax.broadcasted_iota(jnp.int32, shape, 1)
        spread = jnp.where(same, jnp.broadcast_to(z, shape), 0.0).astype(jnp.bfloat16)
        product = lax.dot_general(
            spread.reshape(count * near * HCAP, kept),
            first_ref[-head:] + second_ref[-head:],
            (((1,), (1,)), ((), ())),
            preferred_element_type=jnp.float32,
        )
        out_ref[...] = product.astype(jnp.bfloat16)

    return pl.pallas_call(
        kernel,
        out_shape=jax.ShapeDtypeStruct((count * near * HCAP, head), jnp.bfloat16),
        **kernel_params(),
    )(z_own, z_got, *factors)


def add_hot(partial, target, delta):
    count = partial.shape[0]
    hot_rows = delta.shape[0]

    def kernel(partial_ref, target_ref, delta_ref, out_ref):
        hit = lax.broadcasted_iota(jnp.int32, (count, hot_rows), 1) == target_ref[...]
        place = hit.astype(jnp.float32).astype(jnp.bfloat16)
        out_ref[...] = (partial_ref[...] + matmul(place, delta_ref[...])).astype(jnp.bfloat16)

    return pl.pallas_call(
        kernel,
        out_shape=jax.ShapeDtypeStruct(partial.shape, jnp.bfloat16),
        **kernel_params(),
    )(partial, target[:, None], delta)


def on_device(
    activations, value_weight, shrink_store, expand_store, adapter_row, token_adapter, hot_ids
):
    step_count, token_count, depth = activations.shape
    adapter_count = adapter_row.shape[0]
    hot_count = hot_ids.shape[1]
    per_dev = expand_store.shape[0] // R
    head_part = expand_store.shape[1]
    far_count = lax.axis_size("z_high")
    group_count = 8
    dp_count = far_count * group_count
    me = lax.axis_index(DP)
    z_at, x_at, core_at = lax.axis_index("z_low"), lax.axis_index("x"), lax.axis_index("core")
    none_code = adapter_count + hot_count
    rows = activations.reshape(step_count * token_count, depth)

    near = step_count // 2
    names = jnp.arange(adapter_count, dtype=jnp.int32)
    chain = Chain()

    cold_row = jnp.sum(jnp.where((token_adapter - hot_count)[:, :, None] == names, adapter_row, 0), axis=-1)
    is_hot = token_adapter < hot_count
    is_cold = (token_adapter < none_code) & jnp.logical_not(is_hot)
    owner = cold_row // per_dev
    group = jnp.where(is_hot, token_adapter, jnp.where(is_cold, hot_count + owner, -1))
    at = jnp.arange(token_count, dtype=jnp.int32)
    before = (group[:, :, None] == group[:, None, :]) & (at[None, :] < at[:, None])
    rank = jnp.sum(before.astype(jnp.int32), axis=-1)
    step_at = jnp.arange(step_count, dtype=jnp.int32)[:, None]
    hot_rows = hot_count * step_count * HCAP
    cold_rows = dp_count * step_count * CAP
    server = (step_at // near) * hot_count + token_adapter
    hot_target = (server * near + step_at % near) * HCAP + rank
    cold_target = (owner * step_count + step_at) * CAP + rank
    hot_target = jnp.where(is_hot, hot_target, -1).reshape(-1)
    cold_target = jnp.where(is_cold, cold_target, -1).reshape(-1)

    hot_out, packet = place_rows(
        rows, hot_target, cold_target, (cold_row % per_dev + 1).reshape(-1), hot_rows, cold_rows
    )
    hot_out = chain.hold(hot_out.reshape(group_count, near * HCAP, depth))
    done = {"hot_in": lax.all_to_all(hot_out, GROUP, split_axis=0, concat_axis=0, tiled=True)}

    hot_row = jnp.sum(jnp.where(hot_ids[:, :, None] == names, adapter_row, 0), axis=-1)
    hot_first = jnp.where(hot_row // per_dev == me, (hot_row % per_dev) * R, -R * per_dev)
    column = jnp.arange(per_dev * R, dtype=jnp.int32)
    lane = jnp.arange(R, dtype=jnp.int32)
    entry = jnp.arange(hot_count, dtype=jnp.int32)

    def wanted(core):
        firsts = []
        for x in (x_at, 1 - x_at):
            of_steps = jnp.sum(jnp.where(entry == 2 * x + core, hot_first, 0), axis=1)
            firsts += [jnp.where(z_at == 0, of_steps[:near], of_steps[near:])]
            firsts += [jnp.where(z_at == 0, of_steps[near:], of_steps[:near])]
        return jnp.stack([(f[:, None] + lane).reshape(-1) for f in firsts])

    want_mine, want_other = wanted(core_at), wanted(1 - core_at)
    kept = near * R
    chunk_count = 3
    part = (depth + head_part) // chunk_count

    hops = [("x", SWAP), ("z_low", SWAP)]
    bit = 1
    while bit < far_count:
        hops.append(("z_high", [(i, i ^ bit) for i in range(far_count)]))
        bit *= 2
    mine, swapped, got, held = {}, {}, {}, {}

    def operand(c, stage):
        if stage == 0:
            return mine[c][:, 2 * kept:] + swapped[c][:, 2 * kept:]
        if stage == 1:
            return mine[c][:, kept:2 * kept] + swapped[c][:, kept:2 * kept] + got[c, 0][:, kept:]
        if stage == 2:
            held[c] = mine[c][:, :kept] + swapped[c][:, :kept] + got[c, 0][:, :kept] + got[c, 1]
        else:
            held[c] = held[c] + got[c, stage - 1]
        return held[c]

    def send(c, stage):
        got[c, stage] = chain.permute(operand(c, stage), *hops[stage])

    def view(c):
        mine[c] = after(mine_all, chain.last)[c * part:(c + 1) * part]
        swapped[c] = after(rest_swapped, chain.last)[(c - 1) * part:c * part]

    mine_all, other_first, other_rest = pick_columns(
        after(shrink_store, chain.last), expand_store, want_mine, want_other
    )
    mine[0], swapped[0] = mine_all[:part], chain.permute(other_first, "core", SWAP)
    rest_swapped = chain.permute(other_rest, "core", SWAP)
    send(0, 0)

    def cold_tokens_out():
        sent = chain.hold(packet.reshape(dp_count, step_count * CAP, depth + TAG))
        sent = lax.all_to_all(sent, DP, split_axis=0, concat_axis=0, tiled=True)
        done["packet"] = sent.reshape(cold_rows, depth + TAG)

    def base_product():
        weight = after(value_weight, chain.last)
        if lax.axis_size("tp") == 2:
            done["base_own"], done["base_other"] = base_halves(rows, weight)
        else:
            done["base_own"], done["base_other"] = jnp.zeros((1, 1), jnp.float32), matmul(rows, weight)

    def base_over_tp():
        if lax.axis_size("tp") == 2:
            done["base_got"] = chain.permute(done["base_other"], "tp", SWAP)
        else:
            whole = chain.hold(done["base_other"])
            done["base_got"] = lax.psum_scatter(whole, "tp", scatter_dimension=1, tiled=True)

    def cold_shrink():
        tag_in = done["packet"][:, depth:depth + 1].astype(jnp.int32)
        chosen = (column // R + 1)[None, :] == tag_in
        product = matmul(done["packet"][:, :depth], after(shrink_store, chain.last))
        done["z_part"] = jnp.where(chosen, product, 0.0)

    def cold_over_tp():
        z_part = chain.hold(done["z_part"])
        if lax.axis_size("tp") == 2:
            done["z_got"] = lax.ppermute(z_part, "tp", SWAP)
        else:
            done["z_part"], done["z_got"] = jnp.zeros_like(z_part), lax.psum(z_part, "tp")

    def cold_expand():
        z_cold = (done["z_part"] + done["z_got"]).astype(jnp.bfloat16)
        done["delta"] = narrow(z_cold, after(expand_store, chain.last))

    def cold_back():
        delta = chain.hold(done["delta"].reshape(dp_count, step_count * CAP, head_part))
        delta = lax.all_to_all(delta, DP, split_axis=0, concat_axis=0, tiled=True)
        done["delta_cold"] = delta.reshape(cold_rows, head_part)

    def all_but_hot():
        place_cold = pick(jnp.arange(cold_rows, dtype=jnp.int32)[:, None] == cold_target)
        partial = lax.dot_general(
            place_cold, done["delta_cold"], (((0,), (0,)), ((), ())), preferred_element_type=jnp.float32
        )
        done["partial"] = partial + done["base_own"] + done["base_got"]

    cold_tokens_out()
    chain.last, got[0, 0], done["hot_in"] = lax.optimization_barrier((chain.last, got[0, 0], done["hot_in"]))
    view(1)
    send(1, 0)
    send(0, 1)
    view(2)
    send(2, 0)
    if far_count == 2:
        send(0, 2)
        chain.last, got[1, 0], done["packet"] = lax.optimization_barrier((chain.last, got[1, 0], done["packet"]))
        send(1, 1)
        chain.wait(got[0, 2])
        send(1, 2)
        got[2, 0] = after(got[2, 0], chain.last)
        send(2, 1)
        cold_shrink()
        cold_over_tp()
        base_product()
        names_here = ["z_got", "base_own", "base_other"]
        arrived = lax.optimization_barrier((chain.last, got[1, 2], *[done[name] for name in names_here]))
        chain.last = arrived[0]
        done.update(zip(names_here, arrived[2:]))
        cold_expand()
        send(2, 2)
        base_over_tp()
        cold_back()
    else:
        base_product()
        for c in range(chunk_count):
            for stage in range(1, len(hops)):
                if (c, stage) != (0, 1):
                    send(c, stage)
        base_over_tp()
        cold_shrink()
        cold_over_tp()
        cold_expand()
        cold_back()
    all_but_hot()
    partial = done["partial"]

    hot_in = done["hot_in"].reshape(hot_rows, depth)
    dense = None
    for c in range(chunk_count):
        last = min((c + 1) * part, depth)
        for piece in (held[c], got[c, len(hops) - 1]):
            product = matmul(hot_in[:, c * part:last], piece[:last - c * part])
            dense = product if dense is None else dense + product
    dense = dense.reshape(group_count, near, HCAP, kept)
    at_step = jnp.arange(kept) // R
    z_part = sum(jnp.where(at_step == i, dense[:, i], 0.0) for i in range(near)).reshape(group_count * HCAP, kept)
    if lax.axis_size("tp") == 2:
        z_got = lax.ppermute(z_part, "tp", SWAP)
    else:
        z_part = lax.psum(z_part, "tp")
        z_got = jnp.zeros_like(z_part)
    delta_hot = hot_expand(z_part, z_got, (held[c], got[c, len(hops) - 1]), head_part).reshape(group_count, near * HCAP, head_part)
    delta_hot = lax.all_to_all(delta_hot, GROUP, split_axis=0, concat_axis=0, tiled=True)
    added = add_hot(partial, hot_target, delta_hot.reshape(hot_rows, head_part))
    return added.reshape(step_count, token_count, head_part)


def solution(mesh):
    tp_count, dp_count = mesh.shape["tp"], mesh.shape["dp"]
    fine = Mesh(mesh.devices.reshape(tp_count, dp_count // 8, 2, 2, 2), ("tp", *DP))
    placed = (
        P(None, DP, "tp"),
        P("tp", None),
        P("tp", DP),
        P(DP, "tp"),
        P(),
        P(None, DP),
        P(),
    )
    return jax.shard_map(
        on_device, mesh=fine, in_specs=placed, out_specs=P(None, DP, "tp"), check_vma=False
    )
```
